32 devices in a mesh: slab: 8 (over y, x, core), orb: 4 (over z).
Axes of the slice: x: 2, y: 2, z: 4, core: 2. Of those that a mesh axis runs over, the one named last changes fastest.
Arguments:
- orbitals: float32 [256, 16384], P('orb', 'slab'), may hold values from -6 to 6
- cell_matrices: bfloat16 [64, 512, 512], P('slab'), as said below
- connectivity: int32 [64, 512], P('slab'), may hold values from 0 to 2559, as said below
- face_lower: int32 [2048], P('slab'), may hold values from 0 to 2047, as said below
- face_upper: int32 [2048], P('slab'), may hold values from 0 to 2047, as said below
Outputs:
- orthonormal_orbitals: float32 [256, 16384], P('orb', 'slab')
The draws below stay inside these ranges and needn't reach their ends.
Inputs may be any that keep to these rules, and one draw needn't show every extreme that they name: `connectivity`: each row names 512 distinct positions of its slab's extended numbering. `face_lower`: each slab's block of 256 entries names distinct own nodes; it shares no entry with the same slab's block of face_upper. `face_upper`: each slab's block of 256 entries names distinct own nodes; it shares no entry with the same slab's block of face_lower. `cell_matrices`: each cell matrix is symmetric.
All inputs are finite; a program needn't handle non-finite values.
Results may differ from the reference program's by a relative error of at most 0.023.
Values may be sent and summed in bfloat16 or wider, within the bound.
No kernel may reach another device: no remote copies, remote signals or barrier semaphores. Data moves between devices by JAX's collectives and lax.ppermute only.
A program may use at most 64 MiB of HBM per device.

```python
import math
import jax
import jax.numpy as jnp
from jax import lax

ORBITALS = 256
CELL_NODES = 512
DEGREE = 4
CELL_DEV = 8
NODE_DEV = 2048
FACE = 256
EXT = 2560
SLABS = 8
CELLS = 64
NODES = 16384


def place_value(order_row, wanted, place_at):
    found = jnp.argmax(order_row == wanted)
    held = order_row[place_at]
    order_row = order_row.at[found].set(held)
    return order_row.at[place_at].set(wanted)


def face_maps(key):
    slab_keys = jax.random.split(jax.random.fold_in(key, 5), SLABS)
    orders = jax.vmap(lambda one_key: jax.random.permutation(one_key, NODE_DEV))(slab_keys).astype(jnp.int32)
    first_row = place_value(place_value(orders[0], NODE_DEV - 1, 0), 0, 1)
    second_row = place_value(place_value(orders[1], NODE_DEV - 1, FACE), 0, FACE + 1)
    orders = orders.at[0].set(first_row).at[1].set(second_row)
    return (orders[:, :FACE].reshape(-1), orders[:, FACE:2 * FACE].reshape(-1))


def draw_face_lower(key, part):
    return face_maps(key)[0].astype(jnp.int32)


def draw_face_upper(key, part):
    return face_maps(key)[1].astype(jnp.int32)


def draw_connectivity(key, part):
    cell_keys = jax.random.split(jax.random.fold_in(key, 11), CELLS)
    orders = jax.vmap(lambda one_key: jax.random.permutation(one_key, EXT))(cell_keys).astype(jnp.int32)
    first_row = place_value(place_value(orders[0], EXT - 1, 0), 0, 1)
    orders = orders.at[0].set(first_row)
    return orders[:, :CELL_NODES].astype(jnp.int32)


def draw_cell_matrices(key, part):
    spread_scale = 0.45 / math.sqrt(CELL_DEV * CELL_NODES * CELL_NODES / EXT)
    inner_key = jax.random.fold_in(key, 17)
    entries = jax.random.normal(inner_key, (CELLS, CELL_NODES, CELL_NODES), jnp.float32)
    symmetric = (entries + jnp.swapaxes(entries, 1, 2)) * (spread_scale / math.sqrt(2.0))
    return symmetric.astype(jnp.bfloat16)


def block_scale(own_key, dims, cuts, least, high):
    def one(position, parts):
        heights = jax.random.uniform(jax.random.fold_in(jax.random.fold_in(own_key, 6), position), (parts,), jnp.float32, least / len(cuts), high / len(cuts))
        return jnp.repeat(jnp.exp(heights), dims[position] // parts).reshape((-1,) + (1,) * (len(dims) - position - 1))

    level = one(*cuts[0])
    for cut in cuts[1:]:
        level = level * one(*cut)
    return level


def noise(stream_key, dims, scale, most, shards=(), kind=jnp.bfloat16):
    values = jax.random.normal(stream_key, dims, jnp.float32) * scale
    if len(shards) > 0:
        values = block_scale(stream_key, dims, shards, -0.22, 0.18) * values
    return jnp.clip(values, min=-most, max=most).astype(kind)


def setup_inputs(seed: int = 0) -> dict:
    keys = jax.random.split(jax.random.key(seed), 6)
    orbitals = noise(keys[0], (ORBITALS, NODES), 1.0, 6.0, ((0, 4), (1, 8)), jnp.float32)
    cell_matrices = draw_cell_matrices(jax.random.fold_in(keys[5], 71), 0)
    connectivity = draw_connectivity(jax.random.fold_in(keys[5], 71), 0)
    face_lower = draw_face_lower(jax.random.fold_in(keys[5], 71), 0)
    face_upper = draw_face_upper(jax.random.fold_in(keys[5], 71), 0)
    return {"orbitals": orbitals, "cell_matrices": cell_matrices, "connectivity": connectivity, "face_lower": face_lower, "face_upper": face_upper}


def global_cells(connectivity, face_lower, face_upper):
    lower_maps = face_lower.reshape(SLABS, FACE)
    upper_maps = face_upper.reshape(SLABS, FACE)
    slab_ids = jnp.arange(SLABS, dtype=jnp.int32)[:, None]
    missing = jnp.int32(NODES)
    below = jnp.where(slab_ids > 0, (slab_ids - 1) * NODE_DEV + jnp.roll(upper_maps, 1, axis=0), missing)
    owned = slab_ids * NODE_DEV + jnp.arange(NODE_DEV, dtype=jnp.int32)[None, :]
    above = jnp.where(slab_ids < SLABS - 1, (slab_ids + 1) * NODE_DEV + jnp.roll(lower_maps, -1, axis=0), missing)
    table = jnp.concatenate([below, owned, above], axis=1).astype(jnp.int32)
    local_cells = connectivity.reshape(SLABS, CELL_DEV * CELL_NODES).astype(jnp.int32)
    return jnp.take_along_axis(table, local_cells, axis=1).astype(jnp.int32)

def apply_hamiltonian(wave_field, cell_index, cell_matrices):
    padded = jnp.concatenate([wave_field.astype(jnp.bfloat16), jnp.zeros((ORBITALS, 1), jnp.bfloat16)], axis=1)
    matrices = cell_matrices.reshape(SLABS, CELL_DEV, CELL_NODES, CELL_NODES)

    def add_slab(summed, inputs):
        slab_index, slab_blocks = inputs
        pieces = jnp.take(padded, slab_index, axis=1).reshape(ORBITALS, CELL_DEV, CELL_NODES).astype(jnp.float32)
        cell_terms = jnp.einsum('ocn,cnm->ocm', pieces, slab_blocks.astype(jnp.float32))
        return (summed.at[:, slab_index].add(cell_terms.reshape(ORBITALS, CELL_DEV * CELL_NODES)), None)
    summed, _ = lax.scan(add_slab, jnp.zeros((ORBITALS, NODES + 1), jnp.float32), (cell_index, matrices))
    return summed[:, :NODES]

def reference(orbitals, cell_matrices, connectivity, face_lower, face_upper):
    cell_index = global_cells(connectivity, face_lower, face_upper)
    previous = orbitals
    current = apply_hamiltonian(orbitals, cell_index, cell_matrices)
    for degree_step in range(1, DEGREE):
        following = 2.0 * apply_hamiltonian(current, cell_index, cell_matrices) - previous
        previous, current = (current, following)
    gram = jnp.dot(current, current.T, precision=lax.Precision.HIGHEST)
    factor = jnp.linalg.cholesky(gram)
    solved = lax.linalg.triangular_solve(factor, current, left_side=True, lower=True)
    return solved * math.sqrt(NODES)
```

```python
import functools
import math

import jax
import jax.numpy as jnp
from jax import lax
from jax.experimental import pallas as pl
from jax.experimental.pallas import tpu as pltpu
from jax.sharding import PartitionSpec as P

DEGREE = 4
LANES = 128
SUBLANES = 8
CHUNK = LANES * SUBLANES


def assemble_kernel(rows_ref, column_ref, nodes_ref, cell_ref, out_ref, total, terms):
    cell = pl.program_id(1)
    cell_nodes = cell_ref.shape[1]
    ext_count = out_ref.shape[0]

    @pl.when(cell == 0)
    def _():
        total[...] = jnp.zeros_like(total)

    picker = (nodes_ref[0] == column_ref[...]).astype(jnp.float32).astype(jnp.bfloat16)
    spread = jnp.dot(cell_ref[0], picker, preferred_element_type=jnp.float32)
    for block in range(SUBLANES):
        terms[pl.ds(block * cell_nodes, cell_nodes), :] = spread[:, block * LANES : (block + 1) * LANES]

    group = 16

    def add_rows(step, carry):
        first = pl.multiple_of(step * group, group)
        places = []
        sums = []
        for k in range(group):
            place = pl.multiple_of(rows_ref[cell * cell_nodes + first + k] * SUBLANES, SUBLANES)
            places.append(place)
            sums.append(
                total[pl.ds(place, SUBLANES), :] + terms[pl.ds(first + k, SUBLANES, stride=cell_nodes), :]
            )
        for k in range(group):
            total[pl.ds(places[k], SUBLANES), :] = sums[k]
        return carry

    lax.fori_loop(0, cell_nodes // group, add_rows, 0)

    @pl.when(cell == pl.num_programs(1) - 1)
    def _():
        def write_rows(step, carry):
            first = pl.multiple_of(step * 16, 16)
            for block in range(SUBLANES):
                upper = total[pl.ds(first * SUBLANES + block, SUBLANES, stride=SUBLANES), :]
                lower = total[pl.ds((first + 8) * SUBLANES + block, SUBLANES, stride=SUBLANES), :]
                out_ref[pl.ds(first, 16), block * LANES : (block + 1) * LANES] = jnp.concatenate(
                    [upper, lower], axis=0
                ).astype(jnp.bfloat16)
            return carry

        lax.fori_loop(0, ext_count // 16, write_rows, 0)


def assemble(rows, columns, connectivity, cell_matrices, ext_count):
    cells, cell_nodes, _ = cell_matrices.shape
    chunks = columns.shape[0] // CHUNK
    return pl.pallas_call(
        assemble_kernel,
        out_shape=jax.ShapeDtypeStruct((ext_count, columns.shape[0]), jnp.bfloat16),
        grid_spec=pltpu.PrefetchScalarGridSpec(
            num_scalar_prefetch=1,
            grid=(chunks, cells),
            in_specs=[
                pl.BlockSpec((1, CHUNK), lambda q, c, rows: (0, q)),
                pl.BlockSpec((1, cell_nodes, 1), lambda q, c, rows: (c, 0, 0)),
                pl.BlockSpec((1, cell_nodes, cell_nodes), lambda q, c, rows: (c, 0, 0)),
            ],
            out_specs=pl.BlockSpec((ext_count, CHUNK), lambda q, c, rows: (0, q)),
            scratch_shapes=[
                pltpu.VMEM((ext_count * SUBLANES, LANES), jnp.float32),
                pltpu.VMEM((cell_nodes * SUBLANES, LANES), jnp.float32),
            ],
        ),
        compiler_params=pltpu.CompilerParams(vmem_limit_bytes=48 * 1024 * 1024),
        cost_estimate=pl.CostEstimate(
            flops=2 * cells * cell_nodes * cell_nodes * columns.shape[0],
            bytes_accessed=chunks * cells * cell_nodes * cell_nodes * 2 + ext_count * columns.shape[0] * 2,
            transcendentals=0,
        ),
    )(rows, columns[None, :], connectivity[:, :, None], cell_matrices)


def swap_pairs(count, first):
    pairs = []
    for low in range(first, count - 1, 2):
        pairs += [(low, low + 1), (low + 1, low)]
    return pairs


def sum_over(values, axis):
    count = lax.axis_size(axis)
    if count & (count - 1):
        return lax.psum(values.astype(jnp.bfloat16), axis).astype(jnp.float32)
    step = 1
    while step < count:
        sent = values.astype(jnp.bfloat16)
        got = lax.ppermute(sent, axis, [(i, i ^ step) for i in range(count)])
        values = sent.astype(jnp.float32) + got.astype(jnp.float32)
        step *= 2
    return values


def per_device(orbitals, cell_matrices, connectivity, face_lower, face_upper):
    own_count = orbitals.shape[1]
    face = face_lower.shape[0]
    ext_count = own_count + 2 * face
    slabs = lax.axis_size("slab")
    slab = lax.axis_index("slab")
    even = slab % 2 == 0

    gathered = lax.all_gather(orbitals.astype(jnp.bfloat16), "orb", axis=0, tiled=True)

    has_lower = slab > 0
    has_upper = slab < slabs - 1
    has_a = jnp.where(even, has_upper, has_lower)
    has_b = jnp.where(even, has_lower, has_upper)
    ghost_lower = jnp.arange(face, dtype=jnp.int32)
    ghost_upper = ghost_lower + (face + own_count)
    face_a = jnp.where(even, face_upper, face_lower)
    face_b = jnp.where(even, face_lower, face_upper)
    ghost_a = jnp.where(even, ghost_upper, ghost_lower)
    ghost_b = jnp.where(even, ghost_lower, ghost_upper)

    lower_at = jnp.where(even, own_count + face, own_count)
    upper_at = jnp.where(even, own_count, own_count + face)
    rows = jnp.where(
        connectivity < face,
        connectivity + lower_at,
        jnp.where(
            connectivity < face + own_count,
            connectivity - face,
            connectivity - (face + own_count) + upper_at,
        ),
    ).reshape(-1)
    shared_columns = jnp.concatenate([ghost_a, face_a + face, ghost_b, face_b + face])
    own_columns = jnp.arange(own_count, dtype=jnp.int32) + face

    shared_matrix = assemble(rows, shared_columns, connectivity, cell_matrices, ext_count)
    own_matrix = assemble(rows, own_columns, connectivity, cell_matrices, ext_count)

    face_nodes = jnp.concatenate([face_a, face_b])
    face_table = (
        face_nodes[:, None] == lax.broadcasted_iota(jnp.int32, (2 * face, own_count), 1)
    ).astype(jnp.bfloat16)

    pairs_a = swap_pairs(slabs, 0)
    pairs_b = swap_pairs(slabs, 1)

    def times(left, right):
        return jnp.dot(left, right, preferred_element_type=jnp.float32)

    def apply_hamiltonian(extended):
        shared = times(extended, shared_matrix)
        sent = shared.astype(jnp.bfloat16)
        got_a = lax.ppermute(sent[:, : 2 * face], "slab", pairs_a)
        got_b = lax.ppermute(sent[:, 2 * face :], "slab", pairs_b)
        own = times(extended, own_matrix)
        incoming = jnp.concatenate([got_a[:, :face], got_b[:, :face]], axis=1)
        own = own + times(incoming, face_table)
        at_a = jnp.where(has_a, shared[:, :face] + got_a[:, face:].astype(jnp.float32), 0.0)
        at_b = jnp.where(
            has_b, shared[:, 2 * face : 3 * face] + got_b[:, face:].astype(jnp.float32), 0.0
        )
        return own, at_a, at_b

    def extend(own, at_a, at_b):
        return jnp.concatenate([own, at_a, at_b], axis=1).astype(jnp.bfloat16)

    faces = lax.dot_general(
        gathered, face_table, (((1,), (1,)), ((), ())), preferred_element_type=jnp.float32
    ).astype(jnp.bfloat16)
    ghosts_a = lax.ppermute(faces[:, :face], "slab", pairs_a)
    ghosts_b = lax.ppermute(faces[:, face:], "slab", pairs_b)
    start = jnp.concatenate([gathered, ghosts_a, ghosts_b], axis=1)
    previous = tuple(x.astype(jnp.float32) for x in (gathered, ghosts_a, ghosts_b))
    current = apply_hamiltonian(start)
    for degree_step in range(1, DEGREE):
        product = apply_hamiltonian(extend(*current))
        following = tuple(2.0 * p - q for p, q in zip(product, previous))
        previous, current = current, following

    filtered = current[0].astype(jnp.bfloat16)
    gram = lax.dot_general(
        filtered, filtered, (((1,), (1,)), ((), ())), preferred_element_type=jnp.float32
    )
    factor = jnp.linalg.cholesky(sum_over(gram, "slab"))
    block_rows = orbitals.shape[0]
    norm_scale = math.sqrt(own_count * slabs)
    inverse = lax.linalg.triangular_solve(
        factor, norm_scale * jnp.eye(factor.shape[0], dtype=jnp.float32), left_side=True, lower=True
    )
    mine = lax.dynamic_slice_in_dim(inverse, lax.axis_index("orb") * block_rows, block_rows, 0)
    high = mine.astype(jnp.bfloat16)
    low = (mine - high.astype(jnp.float32)).astype(jnp.bfloat16)
    return times(high, filtered) + times(low, filtered)


def solution(mesh):
    in_specs = (P("orb", "slab"), P("slab", None, None), P("slab", None), P("slab"), P("slab"))
    out_specs = P("orb", "slab")
    return jax.shard_map(
        per_device, mesh=mesh, in_specs=in_specs, out_specs=out_specs, check_vma=False
    )
```

```python
import functools
import math

import jax
import jax.numpy as jnp
from jax import lax
from jax.experimental import pallas as pl
from jax.experimental.pallas import tpu as pltpu
from jax.sharding import PartitionSpec as P

DEGREE = 4
LANES = 128
SUBLANES = 8
CHUNK = LANES * SUBLANES
PITCH = SUBLANES + 1


def assemble_kernel(rows_ref, column_ref, nodes_ref, cell_ref, out_ref, total, terms):
    cell = pl.program_id(1)
    cell_nodes = cell_ref.shape[1]
    ext_count = out_ref.shape[0]

    @pl.when(cell == 0)
    def _():
        total[...] = jnp.zeros_like(total)

    picker = (nodes_ref[0] == column_ref[...]).astype(jnp.float32).astype(jnp.bfloat16)
    for pair in range(CHUNK // 256):
        spread = jnp.dot(
            cell_ref[0], picker[:, pair * 256 : (pair + 1) * 256], preferred_element_type=jnp.float32
        )
        for first in range(0, cell_nodes, SUBLANES):
            for half in range(2):
                terms[pl.ds(first * PITCH + 2 * pair + half, SUBLANES, stride=PITCH), :] = spread[
                    first : first + SUBLANES, half * LANES : (half + 1) * LANES
                ]

    group = 16

    def add_rows(step, carry):
        first = step * group
        places = [rows_ref[cell * cell_nodes + first + k] * PITCH for k in range(group)]
        sums = [
            total[pl.ds(places[k], SUBLANES), :] + terms[pl.ds((first + k) * PITCH, SUBLANES), :]
            for k in range(group)
        ]
        for k in range(group):
            total[pl.ds(places[k], SUBLANES), :] = sums[k]
        return carry

    lax.fori_loop(0, cell_nodes // group, add_rows, 0)

    @pl.when(cell == pl.num_programs(1) - 1)
    def _():
        def write_rows(step, carry):
            first = pl.multiple_of(step * 16, 16)
            for block in range(SUBLANES):
                upper = total[pl.ds(first * PITCH + block, SUBLANES, stride=PITCH), :]
                lower = total[pl.ds((first + 8) * PITCH + block, SUBLANES, stride=PITCH), :]
                out_ref[pl.ds(first, 16), block * LANES : (block + 1) * LANES] = jnp.concatenate(
                    [upper, lower], axis=0
                ).astype(jnp.bfloat16)
            return carry

        lax.fori_loop(0, ext_count // 16, write_rows, 0)


def assemble(rows, columns, connectivity, cell_matrices, ext_count):
    cells, cell_nodes, _ = cell_matrices.shape
    chunks = columns.shape[0] // CHUNK
    return pl.pallas_call(
        assemble_kernel,
        out_shape=jax.ShapeDtypeStruct((ext_count, columns.shape[0]), jnp.bfloat16),
        grid_spec=pltpu.PrefetchScalarGridSpec(
            num_scalar_prefetch=1,
            grid=(chunks, cells),
            in_specs=[
                pl.BlockSpec((1, CHUNK), lambda q, c, rows: (0, q)),
                pl.BlockSpec((1, cell_nodes, 1), lambda q, c, rows: (c, 0, 0)),
                pl.BlockSpec((1, cell_nodes, cell_nodes), lambda q, c, rows: (c, 0, 0)),
            ],
            out_specs=pl.BlockSpec((ext_count, CHUNK), lambda q, c, rows: (0, q)),
            scratch_shapes=[
                pltpu.VMEM((ext_count * PITCH, LANES), jnp.float32),
                pltpu.VMEM((cell_nodes * PITCH, LANES), jnp.float32),
            ],
        ),
        compiler_params=pltpu.CompilerParams(vmem_limit_bytes=48 * 1024 * 1024),
        cost_estimate=pl.CostEstimate(
            flops=2 * cells * cell_nodes * cell_nodes * columns.shape[0],
            bytes_accessed=chunks * cells * cell_nodes * cell_nodes * 2 + ext_count * columns.shape[0] * 2,
            transcendentals=0,
        ),
    )(rows, columns[None, :], connectivity[:, :, None], cell_matrices)


def swap_pairs(count, first):
    pairs = []
    for low in range(first, count - 1, 2):
        pairs += [(low, low + 1), (low + 1, low)]
    return pairs


def sum_over(values, axis):
    count = lax.axis_size(axis)
    if count & (count - 1):
        return lax.psum(values.astype(jnp.bfloat16), axis).astype(jnp.float32)
    step = 1
    while step < count:
        sent = values.astype(jnp.bfloat16)
        got = lax.ppermute(sent, axis, [(i, i ^ step) for i in range(count)])
        values = sent.astype(jnp.float32) + got.astype(jnp.float32)
        step *= 2
    return values


def per_device(orbitals, cell_matrices, connectivity, face_lower, face_upper):
    own_count = orbitals.shape[1]
    face = face_lower.shape[0]
    ext_count = own_count + 2 * face
    slabs = lax.axis_size("slab")
    slab = lax.axis_index("slab")
    even = slab % 2 == 0

    gathered = lax.all_gather(orbitals.astype(jnp.bfloat16), "orb", axis=0, tiled=True)

    has_lower = slab > 0
    has_upper = slab < slabs - 1
    has_a = jnp.where(even, has_upper, has_lower)
    has_b = jnp.where(even, has_lower, has_upper)
    ghost_lower = jnp.arange(face, dtype=jnp.int32)
    ghost_upper = ghost_lower + (face + own_count)
    face_a = jnp.where(even, face_upper, face_lower)
    face_b = jnp.where(even, face_lower, face_upper)
    ghost_a = jnp.where(even, ghost_upper, ghost_lower)
    ghost_b = jnp.where(even, ghost_lower, ghost_upper)

    lower_at = jnp.where(even, own_count + face, own_count)
    upper_at = jnp.where(even, own_count, own_count + face)
    rows = jnp.where(
        connectivity < face,
        connectivity + lower_at,
        jnp.where(
            connectivity < face + own_count,
            connectivity - face,
            connectivity - (face + own_count) + upper_at,
        ),
    ).reshape(-1)
    shared_columns = jnp.concatenate([ghost_a, face_a + face, ghost_b, face_b + face])
    own_columns = jnp.arange(own_count, dtype=jnp.int32) + face

    shared_matrix = assemble(rows, shared_columns, connectivity, cell_matrices, ext_count)
    own_matrix = assemble(rows, own_columns, connectivity, cell_matrices, ext_count)

    face_nodes = jnp.concatenate([face_a, face_b])
    face_table = (
        face_nodes[:, None] == lax.broadcasted_iota(jnp.int32, (2 * face, own_count), 1)
    ).astype(jnp.bfloat16)

    pairs_a = swap_pairs(slabs, 0)
    pairs_b = swap_pairs(slabs, 1)

    def times(left, right):
        return jnp.dot(left, right, preferred_element_type=jnp.float32)

    def apply_hamiltonian(extended):
        shared = times(extended, shared_matrix)
        sent = shared.astype(jnp.bfloat16)
        got_a = lax.ppermute(sent[:, : 2 * face], "slab", pairs_a)
        got_b = lax.ppermute(sent[:, 2 * face :], "slab", pairs_b)
        own = times(extended, own_matrix)
        incoming = jnp.concatenate([got_a[:, :face], got_b[:, :face]], axis=1)
        own = own + times(incoming, face_table)
        at_a = jnp.where(has_a, shared[:, :face] + got_a[:, face:].astype(jnp.float32), 0.0)
        at_b = jnp.where(
            has_b, shared[:, 2 * face : 3 * face] + got_b[:, face:].astype(jnp.float32), 0.0
        )
        return own, at_a, at_b

    def extend(own, at_a, at_b):
        return jnp.concatenate([own, at_a, at_b], axis=1).astype(jnp.bfloat16)

    faces = lax.dot_general(
        gathered, face_table, (((1,), (1,)), ((), ())), preferred_element_type=jnp.float32
    ).astype(jnp.bfloat16)
    ghosts_a = lax.ppermute(faces[:, :face], "slab", pairs_a)
    ghosts_b = lax.ppermute(faces[:, face:], "slab", pairs_b)
    start = jnp.concatenate([gathered, ghosts_a, ghosts_b], axis=1)
    previous = tuple(x.astype(jnp.float32) for x in (gathered, ghosts_a, ghosts_b))
    current = apply_hamiltonian(start)
    for degree_step in range(1, DEGREE):
        product = apply_hamiltonian(extend(*current))
        following = tuple(2.0 * p - q for p, q in zip(product, previous))
        previous, current = current, following

    filtered = current[0].astype(jnp.bfloat16)
    gram = lax.dot_general(
        filtered, filtered, (((1,), (1,)), ((), ())), preferred_element_type=jnp.float32
    )
    factor = jnp.linalg.cholesky(sum_over(gram, "slab"))
    block_rows = orbitals.shape[0]
    norm_scale = math.sqrt(own_count * slabs)
    inverse = lax.linalg.triangular_solve(
        factor, norm_scale * jnp.eye(factor.shape[0], dtype=jnp.float32), left_side=True, lower=True
    )
    mine = lax.dynamic_slice_in_dim(inverse, lax.axis_index("orb") * block_rows, block_rows, 0)
    high = mine.astype(jnp.bfloat16)
    low = (mine - high.astype(jnp.float32)).astype(jnp.bfloat16)
    return times(high, filtered) + times(low, filtered)


def solution(mesh):
    in_specs = (P("orb", "slab"), P("slab", None, None), P("slab", None), P("slab"), P("slab"))
    out_specs = P("orb", "slab")
    return jax.shard_map(
        per_device, mesh=mesh, in_specs=in_specs, out_specs=out_specs, check_vma=False
    )
```

```python
import functools
import math

import jax
import jax.numpy as jnp
from jax import lax
from jax.experimental import pallas as pl
from jax.experimental.pallas import tpu as pltpu
from jax.sharding import PartitionSpec as P

DEGREE = 4
LANES = 128
SUBLANES = 8
CHUNK = LANES * SUBLANES
PITCH = SUBLANES + 1


def assemble_kernel(places_ref, column_ref, nodes_ref, cell_ref, out_ref, total, even_terms, odd_terms):
    cell = pl.program_id(1)
    cells = pl.num_programs(1)
    cell_nodes = cell_ref.shape[1]
    ext_count = out_ref.shape[0]
    parts = CHUNK // 256
    part_rows = cell_nodes // parts
    group = 32

    def spread_part(part, terms):
        columns = column_ref[:, pl.ds(pl.multiple_of(part * 256, 256), 256)]
        picker = (nodes_ref[0] == columns).astype(jnp.float32).astype(jnp.bfloat16)
        spread = jnp.dot(cell_ref[0], picker, preferred_element_type=jnp.float32)
        for first in range(0, cell_nodes, SUBLANES):
            for half in range(2):
                terms[pl.ds(first * PITCH + 2 * part + half, SUBLANES, stride=PITCH), :] = spread[
                    first : first + SUBLANES, half * LANES : (half + 1) * LANES
                ]

    def add_part(part, of_cell, terms):
        first = part * part_rows
        for start in range(0, part_rows, group):
            places = [places_ref[of_cell * cell_nodes + first + start + k] for k in range(group)]
            sums = [
                total[pl.ds(places[k], SUBLANES), :]
                + terms[pl.ds((first + start + k) * PITCH, SUBLANES), :]
                for k in range(group)
            ]
            for k in range(group):
                total[pl.ds(places[k], SUBLANES), :] = sums[k]

    @pl.when(cell == 0)
    def _():
        zero_rows = total.shape[0] // parts

        def body(part, carry):
            spread_part(part, even_terms)
            total[pl.ds(pl.multiple_of(part * zero_rows, SUBLANES), zero_rows), :] = jnp.zeros(
                (zero_rows, LANES), jnp.float32
            )
            return carry

        lax.fori_loop(0, parts, body, 0)

    for parity, (before, now) in enumerate(((odd_terms, even_terms), (even_terms, odd_terms))):

        @pl.when((cell > 0) & (cell % 2 == parity))
        def _():
            def body(part, carry):
                add_part(part, cell - 1, before)
                spread_part(part, now)
                return carry

            lax.fori_loop(0, parts, body, 0)

        @pl.when((cell == cells - 1) & (cell % 2 == parity))
        def _():
            def body(part, carry):
                add_part(part, cell, now)
                return carry

            lax.fori_loop(0, parts, body, 0)

    @pl.when(cell == cells - 1)
    def _():
        def write_rows(step, carry):
            first = pl.multiple_of(step * 16, 16)
            for block in range(SUBLANES):
                upper = total[pl.ds(first * PITCH + block, SUBLANES, stride=PITCH), :]
                lower = total[pl.ds((first + 8) * PITCH + block, SUBLANES, stride=PITCH), :]
                out_ref[pl.ds(first, 16), block * LANES : (block + 1) * LANES] = jnp.concatenate(
                    [upper, lower], axis=0
                ).astype(jnp.bfloat16)
            return carry

        lax.fori_loop(0, ext_count // 16, write_rows, 0, unroll=4)


def assemble(places, columns, connectivity, cell_matrices, ext_count):
    cells, cell_nodes, _ = cell_matrices.shape
    chunks = columns.shape[0] // CHUNK
    return pl.pallas_call(
        assemble_kernel,
        out_shape=jax.ShapeDtypeStruct((ext_count, columns.shape[0]), jnp.bfloat16),
        grid_spec=pltpu.PrefetchScalarGridSpec(
            num_scalar_prefetch=1,
            grid=(chunks, cells),
            in_specs=[
                pl.BlockSpec((1, CHUNK), lambda q, c, places: (0, q)),
                pl.BlockSpec((1, cell_nodes, 1), lambda q, c, places: (c, 0, 0)),
                pl.BlockSpec((1, cell_nodes, cell_nodes), lambda q, c, places: (c, 0, 0)),
            ],
            out_specs=pl.BlockSpec((ext_count, CHUNK), lambda q, c, places: (0, q)),
            scratch_shapes=[
                pltpu.VMEM((ext_count * PITCH, LANES), jnp.float32),
                pltpu.VMEM((cell_nodes * PITCH, LANES), jnp.float32),
                pltpu.VMEM((cell_nodes * PITCH, LANES), jnp.float32),
            ],
        ),
        compiler_params=pltpu.CompilerParams(vmem_limit_bytes=48 * 1024 * 1024),
        cost_estimate=pl.CostEstimate(
            flops=2 * cells * cell_nodes * cell_nodes * columns.shape[0],
            bytes_accessed=chunks * cells * cell_nodes * cell_nodes * 2 + ext_count * columns.shape[0] * 2,
            transcendentals=0,
        ),
    )(places, columns[None, :], connectivity[:, :, None], cell_matrices)


def swap_pairs(count, first):
    pairs = []
    for low in range(first, count - 1, 2):
        pairs += [(low, low + 1), (low + 1, low)]
    return pairs


def sum_over(values, axis):
    count = lax.axis_size(axis)
    if count & (count - 1):
        return lax.psum(values.astype(jnp.bfloat16), axis).astype(jnp.float32)
    step = 1
    while step < count:
        sent = values.astype(jnp.bfloat16)
        got = lax.ppermute(sent, axis, [(i, i ^ step) for i in range(count)])
        values = sent.astype(jnp.float32) + got.astype(jnp.float32)
        step *= 2
    return values


def per_device(orbitals, cell_matrices, connectivity, face_lower, face_upper):
    own_count = orbitals.shape[1]
    face = face_lower.shape[0]
    ext_count = own_count + 2 * face
    slabs = lax.axis_size("slab")
    slab = lax.axis_index("slab")
    even = slab % 2 == 0

    gathered = lax.all_gather(orbitals.astype(jnp.bfloat16), "orb", axis=0, tiled=True)

    has_lower = slab > 0
    has_upper = slab < slabs - 1
    has_a = jnp.where(even, has_upper, has_lower)
    has_b = jnp.where(even, has_lower, has_upper)
    ghost_lower = jnp.arange(face, dtype=jnp.int32)
    ghost_upper = ghost_lower + (face + own_count)
    face_a = jnp.where(even, face_upper, face_lower)
    face_b = jnp.where(even, face_lower, face_upper)
    ghost_a = jnp.where(even, ghost_upper, ghost_lower)
    ghost_b = jnp.where(even, ghost_lower, ghost_upper)

    lower_at = jnp.where(even, own_count + face, own_count)
    upper_at = jnp.where(even, own_count, own_count + face)
    places = jnp.where(
        connectivity < face,
        connectivity + lower_at,
        jnp.where(
            connectivity < face + own_count,
            connectivity - face,
            connectivity - (face + own_count) + upper_at,
        ),
    ).reshape(-1) * PITCH
    shared_columns = jnp.concatenate([ghost_a, face_a + face, ghost_b, face_b + face])
    own_columns = jnp.arange(own_count, dtype=jnp.int32) + face

    shared_matrix = assemble(places, shared_columns, connectivity, cell_matrices, ext_count)
    own_matrix = assemble(places, own_columns, connectivity, cell_matrices, ext_count)

    face_nodes = jnp.concatenate([face_a, face_b])
    face_table = (
        face_nodes[:, None] == lax.broadcasted_iota(jnp.int32, (2 * face, own_count), 1)
    ).astype(jnp.bfloat16)

    pairs_a = swap_pairs(slabs, 0)
    pairs_b = swap_pairs(slabs, 1)

    def times(left, right):
        return jnp.dot(left, right, preferred_element_type=jnp.float32)

    def apply_hamiltonian(extended):
        shared = times(extended, shared_matrix)
        sent = shared.astype(jnp.bfloat16)
        got_a = lax.ppermute(sent[:, : 2 * face], "slab", pairs_a)
        got_b = lax.ppermute(sent[:, 2 * face :], "slab", pairs_b)
        own = times(extended, own_matrix)
        incoming = jnp.concatenate([got_a[:, :face], got_b[:, :face]], axis=1)
        own = own + times(incoming, face_table)
        at_a = jnp.where(has_a, shared[:, :face] + got_a[:, face:].astype(jnp.float32), 0.0)
        at_b = jnp.where(
            has_b, shared[:, 2 * face : 3 * face] + got_b[:, face:].astype(jnp.float32), 0.0
        )
        return own, at_a, at_b

    def extend(own, at_a, at_b):
        return jnp.concatenate([own, at_a, at_b], axis=1).astype(jnp.bfloat16)

    faces = lax.dot_general(
        gathered, face_table, (((1,), (1,)), ((), ())), preferred_element_type=jnp.float32
    ).astype(jnp.bfloat16)
    ghosts_a = lax.ppermute(faces[:, :face], "slab", pairs_a)
    ghosts_b = lax.ppermute(faces[:, face:], "slab", pairs_b)
    start = jnp.concatenate([gathered, ghosts_a, ghosts_b], axis=1)
    previous = tuple(x.astype(jnp.float32) for x in (gathered, ghosts_a, ghosts_b))
    current = apply_hamiltonian(start)
    for degree_step in range(1, DEGREE):
        product = apply_hamiltonian(extend(*current))
        following = tuple(2.0 * p - q for p, q in zip(product, previous))
        previous, current = current, following

    filtered = current[0].astype(jnp.bfloat16)
    gram = lax.dot_general(
        filtered, filtered, (((1,), (1,)), ((), ())), preferred_element_type=jnp.float32
    )
    factor = jnp.linalg.cholesky(sum_over(gram, "slab"))
    block_rows = orbitals.shape[0]
    norm_scale = math.sqrt(own_count * slabs)
    inverse = lax.linalg.triangular_solve(
        factor, norm_scale * jnp.eye(factor.shape[0], dtype=jnp.float32), left_side=True, lower=True
    )
    mine = lax.dynamic_slice_in_dim(inverse, lax.axis_index("orb") * block_rows, block_rows, 0)
    high = mine.astype(jnp.bfloat16)
    low = (mine - high.astype(jnp.float32)).astype(jnp.bfloat16)
    return times(high, filtered) + times(low, filtered)


def solution(mesh):
    in_specs = (P("orb", "slab"), P("slab", None, None), P("slab", None), P("slab"), P("slab"))
    out_specs = P("orb", "slab")
    return jax.shard_map(
        per_device, mesh=mesh, in_specs=in_specs, out_specs=out_specs, check_vma=False
    )
```

```python
import functools
import math

import jax
import jax.numpy as jnp
from jax import lax
from jax.experimental import pallas as pl
from jax.experimental.pallas import tpu as pltpu
from jax.sharding import PartitionSpec as P

DEGREE = 4
LANES = 128
SUBLANES = 8
CHUNK = LANES * SUBLANES
PITCH = SUBLANES + 1


def assemble_kernel(rows_ref, column_ref, nodes_ref, cell_ref, out_ref, total, terms):
    cell = pl.program_id(1)
    cell_nodes = cell_ref.shape[1]
    ext_count = out_ref.shape[0]

    @pl.when(cell == 0)
    def _():
        total[...] = jnp.zeros_like(total)

    picker = (nodes_ref[0] == column_ref[...]).astype(jnp.float32).astype(jnp.bfloat16)
    for pair in range(CHUNK // 256):
        spread = jnp.dot(
            cell_ref[0], picker[:, pair * 256 : (pair + 1) * 256], preferred_element_type=jnp.float32
        )
        for first in range(0, cell_nodes, SUBLANES):
            for half in range(2):
                terms[pl.ds(first * PITCH + 2 * pair + half, SUBLANES, stride=PITCH), :] = spread[
                    first : first + SUBLANES, half * LANES : (half + 1) * LANES
                ]

    group = 16

    def add_rows(step, carry):
        first = step * group
        places = [rows_ref[cell * cell_nodes + first + k] * PITCH for k in range(group)]
        sums = [
            total[pl.ds(places[k], SUBLANES), :] + terms[pl.ds((first + k) * PITCH, SUBLANES), :]
            for k in range(group)
        ]
        for k in range(group):
            total[pl.ds(places[k], SUBLANES), :] = sums[k]
        return carry

    lax.fori_loop(0, cell_nodes // group, add_rows, 0)

    @pl.when(cell == pl.num_programs(1) - 1)
    def _():
        def write_rows(step, carry):
            first = pl.multiple_of(step * 16, 16)
            for block in range(SUBLANES):
                upper = total[pl.ds(first * PITCH + block, SUBLANES, stride=PITCH), :]
                lower = total[pl.ds((first + 8) * PITCH + block, SUBLANES, stride=PITCH), :]
                out_ref[pl.ds(first, 16), block * LANES : (block + 1) * LANES] = jnp.concatenate(
                    [upper, lower], axis=0
                ).astype(jnp.bfloat16)
            return carry

        lax.fori_loop(0, ext_count // 16, write_rows, 0)


def assemble(rows, columns, connectivity, cell_matrices, ext_count):
    cells, cell_nodes, _ = cell_matrices.shape
    chunks = columns.shape[0] // CHUNK
    return pl.pallas_call(
        assemble_kernel,
        out_shape=jax.ShapeDtypeStruct((ext_count, columns.shape[0]), jnp.bfloat16),
        grid_spec=pltpu.PrefetchScalarGridSpec(
            num_scalar_prefetch=1,
            grid=(chunks, cells),
            in_specs=[
                pl.BlockSpec((1, CHUNK), lambda q, c, rows: (0, q)),
                pl.BlockSpec((1, cell_nodes, 1), lambda q, c, rows: (c, 0, 0)),
                pl.BlockSpec((1, cell_nodes, cell_nodes), lambda q, c, rows: (c, 0, 0)),
            ],
            out_specs=pl.BlockSpec((ext_count, CHUNK), lambda q, c, rows: (0, q)),
            scratch_shapes=[
                pltpu.VMEM((ext_count * PITCH, LANES), jnp.float32),
                pltpu.VMEM((cell_nodes * PITCH, LANES), jnp.float32),
            ],
        ),
        compiler_params=pltpu.CompilerParams(vmem_limit_bytes=48 * 1024 * 1024),
        cost_estimate=pl.CostEstimate(
            flops=2 * cells * cell_nodes * cell_nodes * columns.shape[0],
            bytes_accessed=chunks * cells * cell_nodes * cell_nodes * 2 + ext_count * columns.shape[0] * 2,
            transcendentals=0,
        ),
    )(rows, columns[None, :], connectivity[:, :, None], cell_matrices)


def exact(left, right, contract):
    return lax.dot_general(
        left,
        right,
        (contract, ((), ())),
        precision=lax.Precision.HIGHEST,
        preferred_element_type=jnp.float32,
    )


def inverse_factor(block):
    size = block.shape[0]
    groups = size // SUBLANES
    row = lax.broadcasted_iota(jnp.int32, (SUBLANES, LANES), 0)
    lane = lax.broadcasted_iota(jnp.int32, (SUBLANES, LANES), 1)
    left = [block[g * SUBLANES : (g + 1) * SUBLANES, :] for g in range(groups)]
    right = [(lane == row + g * SUBLANES).astype(jnp.float32) for g in range(groups)]

    def over_rows(values, index):
        return jnp.broadcast_to(values[index : index + 1, :], (SUBLANES, LANES))

    for k in range(groups):
        later = range(k, groups)
        column = {
            g: [
                jnp.broadcast_to(
                    left[g][:, k * SUBLANES + q : k * SUBLANES + q + 1], (SUBLANES, LANES)
                )
                for q in range(SUBLANES)
            ]
            for g in later
        }
        for q in range(SUBLANES):
            scale = lax.rsqrt(over_rows(column[k][q], q))
            factor = {g: column[g][q] * scale for g in later}
            left_row = over_rows(left[k], q) * scale
            right_row = over_rows(right[k], q) * scale
            below = jnp.where(row > q, factor[k], 0.0)
            left[k] = jnp.where(row == q, left_row, left[k] - below * left_row)
            right[k] = jnp.where(row == q, right_row, right[k] - below * right_row)
            for other in range(q + 1, SUBLANES):
                weight = over_rows(factor[k], other)
                for g in later:
                    column[g][other] = column[g][other] - factor[g] * weight
            for g in range(k + 1, groups):
                left[g] = left[g] - factor[g] * left_row
                right[g] = right[g] - factor[g] * right_row
    return jnp.concatenate(right, axis=0)


def orthonormal_kernel(scale, block_ref, gram_ref, filtered_ref, out_ref, inverse):
    size = gram_ref.shape[0]
    count = size // LANES
    at = [slice(i * LANES, (i + 1) * LANES) for i in range(count)]
    lower = {}
    inverses = {}
    for i in range(count):
        diagonal = gram_ref[at[i], at[i]]
        for j in range(i):
            diagonal = diagonal - exact(lower[i, j], lower[i, j], ((1,), (1,)))
        inverses[i, i] = inverse_factor(diagonal)
        for k in range(i + 1, count):
            entry = gram_ref[at[k], at[i]]
            for j in range(i):
                entry = entry - exact(lower[k, j], lower[i, j], ((1,), (1,)))
            lower[k, i] = exact(entry, inverses[i, i], ((1,), (1,)))
    inverse[...] = jnp.zeros_like(inverse)
    for i in range(count):
        for j in range(i):
            entry = exact(lower[i, j], inverses[j, j], ((1,), (0,)))
            for m in range(j + 1, i):
                entry = entry + exact(lower[i, m], inverses[m, j], ((1,), (0,)))
            inverses[i, j] = -exact(inverses[i, i], entry, ((1,), (0,)))
            inverse[at[i], at[j]] = inverses[i, j] * scale
        inverse[at[i], at[i]] = inverses[i, i] * scale
    rows = out_ref.shape[0]
    mine = inverse[pl.ds(pl.multiple_of(block_ref[0] * rows, rows), rows), :]
    high = mine.astype(jnp.bfloat16)
    low = (mine - high.astype(jnp.float32)).astype(jnp.bfloat16)
    width = 512
    for first in range(0, out_ref.shape[1], width):
        part = filtered_ref[:, first : first + width]
        out_ref[:, first : first + width] = jnp.dot(
            high, part, preferred_element_type=jnp.float32
        ) + jnp.dot(low, part, preferred_element_type=jnp.float32)


def orthonormal(block, gram, filtered, rows, scale):
    size = gram.shape[0]
    return pl.pallas_call(
        functools.partial(orthonormal_kernel, scale),
        out_shape=jax.ShapeDtypeStruct((rows, filtered.shape[1]), jnp.float32),
        in_specs=[
            pl.BlockSpec(memory_space=pltpu.SMEM),
            pl.BlockSpec(memory_space=pltpu.VMEM),
            pl.BlockSpec(memory_space=pltpu.VMEM),
        ],
        out_specs=pl.BlockSpec(memory_space=pltpu.VMEM),
        scratch_shapes=[pltpu.VMEM((size, size), jnp.float32)],
        compiler_params=pltpu.CompilerParams(vmem_limit_bytes=16 * 1024 * 1024),
    )(block, gram, filtered)


def swap_pairs(count, first):
    pairs = []
    for low in range(first, count - 1, 2):
        pairs += [(low, low + 1), (low + 1, low)]
    return pairs


def sum_over(values, axis):
    count = lax.axis_size(axis)
    if count & (count - 1):
        return lax.psum(values.astype(jnp.bfloat16), axis).astype(jnp.float32)
    step = 1
    while step < count:
        sent = values.astype(jnp.bfloat16)
        got = lax.ppermute(sent, axis, [(i, i ^ step) for i in range(count)])
        values = sent.astype(jnp.float32) + got.astype(jnp.float32)
        step *= 2
    return values


def per_device(orbitals, cell_matrices, connectivity, face_lower, face_upper):
    own_count = orbitals.shape[1]
    face = face_lower.shape[0]
    ext_count = own_count + 2 * face
    slabs = lax.axis_size("slab")
    slab = lax.axis_index("slab")
    even = slab % 2 == 0

    gathered = lax.all_gather(orbitals.astype(jnp.bfloat16), "orb", axis=0, tiled=True)

    has_lower = slab > 0
    has_upper = slab < slabs - 1
    has_a = jnp.where(even, has_upper, has_lower)
    has_b = jnp.where(even, has_lower, has_upper)
    ghost_lower = jnp.arange(face, dtype=jnp.int32)
    ghost_upper = ghost_lower + (face + own_count)
    face_a = jnp.where(even, face_upper, face_lower)
    face_b = jnp.where(even, face_lower, face_upper)
    ghost_a = jnp.where(even, ghost_upper, ghost_lower)
    ghost_b = jnp.where(even, ghost_lower, ghost_upper)

    lower_at = jnp.where(even, own_count + face, own_count)
    upper_at = jnp.where(even, own_count, own_count + face)
    rows = jnp.where(
        connectivity < face,
        connectivity + lower_at,
        jnp.where(
            connectivity < face + own_count,
            connectivity - face,
            connectivity - (face + own_count) + upper_at,
        ),
    ).reshape(-1)
    shared_columns = jnp.concatenate([ghost_a, face_a + face, ghost_b, face_b + face])
    own_columns = jnp.arange(own_count, dtype=jnp.int32) + face

    shared_matrix = assemble(rows, shared_columns, connectivity, cell_matrices, ext_count)
    own_matrix = assemble(rows, own_columns, connectivity, cell_matrices, ext_count)

    face_nodes = jnp.concatenate([face_a, face_b])
    face_table = (
        face_nodes[:, None] == lax.broadcasted_iota(jnp.int32, (2 * face, own_count), 1)
    ).astype(jnp.bfloat16)

    pairs_a = swap_pairs(slabs, 0)
    pairs_b = swap_pairs(slabs, 1)

    def times(left, right):
        return jnp.dot(left, right, preferred_element_type=jnp.float32)

    def apply_hamiltonian(extended):
        shared = times(extended, shared_matrix)
        sent = shared.astype(jnp.bfloat16)
        got_a = lax.ppermute(sent[:, : 2 * face], "slab", pairs_a)
        got_b = lax.ppermute(sent[:, 2 * face :], "slab", pairs_b)
        own = times(extended, own_matrix)
        incoming = jnp.concatenate([got_a[:, :face], got_b[:, :face]], axis=1)
        own = own + times(incoming, face_table)
        at_a = jnp.where(has_a, shared[:, :face] + got_a[:, face:].astype(jnp.float32), 0.0)
        at_b = jnp.where(
            has_b, shared[:, 2 * face : 3 * face] + got_b[:, face:].astype(jnp.float32), 0.0
        )
        return own, at_a, at_b

    def extend(own, at_a, at_b):
        return jnp.concatenate([own, at_a, at_b], axis=1).astype(jnp.bfloat16)

    faces = lax.dot_general(
        gathered, face_table, (((1,), (1,)), ((), ())), preferred_element_type=jnp.float32
    ).astype(jnp.bfloat16)
    ghosts_a = lax.ppermute(faces[:, :face], "slab", pairs_a)
    ghosts_b = lax.ppermute(faces[:, face:], "slab", pairs_b)
    start = jnp.concatenate([gathered, ghosts_a, ghosts_b], axis=1)
    previous = tuple(x.astype(jnp.float32) for x in (gathered, ghosts_a, ghosts_b))
    current = apply_hamiltonian(start)
    for degree_step in range(1, DEGREE):
        product = apply_hamiltonian(extend(*current))
        following = tuple(2.0 * p - q for p, q in zip(product, previous))
        previous, current = current, following

    filtered = current[0].astype(jnp.bfloat16)
    gram = lax.dot_general(
        filtered, filtered, (((1,), (1,)), ((), ())), preferred_element_type=jnp.float32
    )
    total = sum_over(gram, "slab")
    block = lax.axis_index("orb").astype(jnp.int32).reshape(1)
    return orthonormal(block, total, filtered, orbitals.shape[0], math.sqrt(own_count * slabs))


def solution(mesh):
    in_specs = (P("orb", "slab"), P("slab", None, None), P("slab", None), P("slab"), P("slab"))
    out_specs = P("orb", "slab")
    return jax.shard_map(
        per_device, mesh=mesh, in_specs=in_specs, out_specs=out_specs, check_vma=False
    )
```

```python
import functools
import math

import jax
import jax.numpy as jnp
from jax import lax
from jax.experimental import pallas as pl
from jax.experimental.pallas import tpu as pltpu
from jax.sharding import PartitionSpec as P

DEGREE = 4
LANES = 128
SUBLANES = 8
CHUNK = LANES * SUBLANES
PITCH = SUBLANES + 1


def assemble_kernel(places_ref, column_ref, nodes_ref, cell_ref, out_ref, total, even_terms, odd_terms):
    cell = pl.program_id(1)
    cells = pl.num_programs(1)
    cell_nodes = cell_ref.shape[1]
    ext_count = out_ref.shape[0]
    parts = CHUNK // 256
    part_rows = cell_nodes // parts
    group = 32

    def spread_part(part):
        columns = column_ref[:, pl.ds(pl.multiple_of(part * 256, 256), 256)]
        picker = jnp.concatenate(
            [
                (nodes_ref[0] == columns[:, half * LANES : (half + 1) * LANES])
                .astype(jnp.float32)
                .astype(jnp.bfloat16)
                for half in range(2)
            ],
            axis=1,
        )
        return jnp.dot(cell_ref[0], picker, preferred_element_type=jnp.float32)

    def keep_part(part, spread, terms):
        for first in range(0, cell_nodes, SUBLANES):
            for half in range(2):
                terms[pl.ds(first * PITCH + 2 * part + half, SUBLANES, stride=PITCH), :] = spread[
                    first : first + SUBLANES, half * LANES : (half + 1) * LANES
                ]

    def add_part(part, of_cell, terms):
        first = part * part_rows
        for start in range(0, part_rows, group):
            places = [places_ref[of_cell * cell_nodes + first + start + k] for k in range(group)]
            sums = [
                total[pl.ds(places[k], SUBLANES), :]
                + terms[pl.ds((first + start + k) * PITCH, SUBLANES), :]
                for k in range(group)
            ]
            for k in range(group):
                total[pl.ds(places[k], SUBLANES), :] = sums[k]

    @pl.when(cell == 0)
    def _():
        zero_rows = total.shape[0] // parts

        def body(part, carry):
            spread = spread_part(part)
            total[pl.ds(pl.multiple_of(part * zero_rows, SUBLANES), zero_rows), :] = jnp.zeros(
                (zero_rows, LANES), jnp.float32
            )
            keep_part(part, spread, even_terms)
            return carry

        lax.fori_loop(0, parts, body, 0)

    for parity, (before, now) in enumerate(((odd_terms, even_terms), (even_terms, odd_terms))):

        @pl.when((cell > 0) & (cell % 2 == parity))
        def _():
            def body(part, carry):
                spread = spread_part(part)
                add_part(part, cell - 1, before)
                keep_part(part, spread, now)
                return carry

            lax.fori_loop(0, parts, body, 0)

        @pl.when((cell == cells - 1) & (cell % 2 == parity))
        def _():
            def body(part, carry):
                add_part(part, cell, now)
                return carry

            lax.fori_loop(0, parts, body, 0)

    @pl.when(cell == cells - 1)
    def _():
        def write_rows(step, carry):
            first = pl.multiple_of(step * 16, 16)
            for block in range(SUBLANES):
                upper = total[pl.ds(first * PITCH + block, SUBLANES, stride=PITCH), :]
                lower = total[pl.ds((first + 8) * PITCH + block, SUBLANES, stride=PITCH), :]
                out_ref[pl.ds(first, 16), block * LANES : (block + 1) * LANES] = jnp.concatenate(
                    [upper, lower], axis=0
                ).astype(jnp.bfloat16)
            return carry

        lax.fori_loop(0, ext_count // 16, write_rows, 0, unroll=4)


def assemble(places, columns, nodes, cell_matrices, ext_count):
    cells, cell_nodes, _ = cell_matrices.shape
    chunks = columns.shape[0] // CHUNK
    return pl.pallas_call(
        assemble_kernel,
        out_shape=jax.ShapeDtypeStruct((ext_count, columns.shape[0]), jnp.bfloat16),
        grid_spec=pltpu.PrefetchScalarGridSpec(
            num_scalar_prefetch=1,
            grid=(chunks, cells),
            in_specs=[
                pl.BlockSpec((1, CHUNK), lambda q, c, places: (0, q)),
                pl.BlockSpec((1, cell_nodes, LANES), lambda q, c, places: (c, 0, 0)),
                pl.BlockSpec((1, cell_nodes, cell_nodes), lambda q, c, places: (c, 0, 0)),
            ],
            out_specs=pl.BlockSpec((ext_count, CHUNK), lambda q, c, places: (0, q)),
            scratch_shapes=[
                pltpu.VMEM((ext_count * PITCH, LANES), jnp.float32),
                pltpu.VMEM((cell_nodes * PITCH, LANES), jnp.float32),
                pltpu.VMEM((cell_nodes * PITCH, LANES), jnp.float32),
            ],
        ),
        compiler_params=pltpu.CompilerParams(vmem_limit_bytes=48 * 1024 * 1024),
        cost_estimate=pl.CostEstimate(
            flops=2 * cells * cell_nodes * cell_nodes * columns.shape[0],
            bytes_accessed=chunks * cells * cell_nodes * cell_nodes * 2 + ext_count * columns.shape[0] * 2,
            transcendentals=0,
        ),
    )(places, columns[None, :], nodes, cell_matrices)


def exact(left, right, contract):
    return lax.dot_general(
        left,
        right,
        (contract, ((), ())),
        precision=lax.Precision.HIGHEST,
        preferred_element_type=jnp.float32,
    )


def inverse_factor(block):
    size = block.shape[0]
    groups = size // SUBLANES
    row = lax.broadcasted_iota(jnp.int32, (SUBLANES, LANES), 0)
    lane = lax.broadcasted_iota(jnp.int32, (SUBLANES, LANES), 1)
    left = [block[g * SUBLANES : (g + 1) * SUBLANES, :] for g in range(groups)]
    right = [(lane == row + g * SUBLANES).astype(jnp.float32) for g in range(groups)]

    def over_rows(values, index):
        return jnp.broadcast_to(values[index : index + 1, :], (SUBLANES, LANES))

    for k in range(groups):
        later = range(k, groups)
        column = {
            g: [
                jnp.broadcast_to(
                    left[g][:, k * SUBLANES + q : k * SUBLANES + q + 1], (SUBLANES, LANES)
                )
                for q in range(SUBLANES)
            ]
            for g in later
        }
        for q in range(SUBLANES):
            scale = lax.rsqrt(over_rows(column[k][q], q))
            factor = {g: column[g][q] * scale for g in later}
            left_row = over_rows(left[k], q) * scale
            right_row = over_rows(right[k], q) * scale
            below = jnp.where(row > q, factor[k], 0.0)
            left[k] = jnp.where(row == q, left_row, left[k] - below * left_row)
            right[k] = jnp.where(row == q, right_row, right[k] - below * right_row)
            for other in range(q + 1, SUBLANES):
                weight = over_rows(factor[k], other)
                for g in later:
                    column[g][other] = column[g][other] - factor[g] * weight
            for g in range(k + 1, groups):
                left[g] = left[g] - factor[g] * left_row
                right[g] = right[g] - factor[g] * right_row
    return jnp.concatenate(right, axis=0)


def orthonormal_kernel(scale, block_ref, gram_ref, filtered_ref, out_ref, inverse):
    size = gram_ref.shape[0]
    count = size // LANES
    at = [slice(i * LANES, (i + 1) * LANES) for i in range(count)]
    lower = {}
    inverses = {}
    for i in range(count):
        diagonal = gram_ref[at[i], at[i]]
        for j in range(i):
            diagonal = diagonal - exact(lower[i, j], lower[i, j], ((1,), (1,)))
        inverses[i, i] = inverse_factor(diagonal)
        for k in range(i + 1, count):
            entry = gram_ref[at[k], at[i]]
            for j in range(i):
                entry = entry - exact(lower[k, j], lower[i, j], ((1,), (1,)))
            lower[k, i] = exact(entry, inverses[i, i], ((1,), (1,)))
    inverse[...] = jnp.zeros_like(inverse)
    for i in range(count):
        for j in range(i):
            entry = exact(lower[i, j], inverses[j, j], ((1,), (0,)))
            for m in range(j + 1, i):
                entry = entry + exact(lower[i, m], inverses[m, j], ((1,), (0,)))
            inverses[i, j] = -exact(inverses[i, i], entry, ((1,), (0,)))
            inverse[at[i], at[j]] = inverses[i, j] * scale
        inverse[at[i], at[i]] = inverses[i, i] * scale
    rows = out_ref.shape[0]
    mine = inverse[pl.ds(pl.multiple_of(block_ref[0] * rows, rows), rows), :]
    high = mine.astype(jnp.bfloat16)
    low = (mine - high.astype(jnp.float32)).astype(jnp.bfloat16)
    width = 512
    for first in range(0, out_ref.shape[1], width):
        part = filtered_ref[:, first : first + width]
        out_ref[:, first : first + width] = jnp.dot(
            high, part, preferred_element_type=jnp.float32
        ) + jnp.dot(low, part, preferred_element_type=jnp.float32)


def orthonormal(block, gram, filtered, rows, scale):
    size = gram.shape[0]
    return pl.pallas_call(
        functools.partial(orthonormal_kernel, scale),
        out_shape=jax.ShapeDtypeStruct((rows, filtered.shape[1]), jnp.float32),
        in_specs=[
            pl.BlockSpec(memory_space=pltpu.SMEM),
            pl.BlockSpec(memory_space=pltpu.VMEM),
            pl.BlockSpec(memory_space=pltpu.VMEM),
        ],
        out_specs=pl.BlockSpec(memory_space=pltpu.VMEM),
        scratch_shapes=[pltpu.VMEM((size, size), jnp.float32)],
        compiler_params=pltpu.CompilerParams(vmem_limit_bytes=16 * 1024 * 1024),
    )(block, gram, filtered)


def swap_pairs(count, first):
    pairs = []
    for low in range(first, count - 1, 2):
        pairs += [(low, low + 1), (low + 1, low)]
    return pairs


def sum_over(values, axis):
    count = lax.axis_size(axis)
    if count & (count - 1):
        return lax.psum(values.astype(jnp.bfloat16), axis).astype(jnp.float32)
    step = 1
    while step < count:
        sent = values.astype(jnp.bfloat16)
        got = lax.ppermute(sent, axis, [(i, i ^ step) for i in range(count)])
        values = sent.astype(jnp.float32) + got.astype(jnp.float32)
        step *= 2
    return values


def per_device(orbitals, cell_matrices, connectivity, face_lower, face_upper):
    own_count = orbitals.shape[1]
    face = face_lower.shape[0]
    ext_count = own_count + 2 * face
    slabs = lax.axis_size("slab")
    slab = lax.axis_index("slab")
    even = slab % 2 == 0

    gathered = lax.all_gather(orbitals.astype(jnp.bfloat16), "orb", axis=0, tiled=True)

    has_lower = slab > 0
    has_upper = slab < slabs - 1
    has_a = jnp.where(even, has_upper, has_lower)
    has_b = jnp.where(even, has_lower, has_upper)
    ghost_lower = jnp.arange(face, dtype=jnp.int32)
    ghost_upper = ghost_lower + (face + own_count)
    face_a = jnp.where(even, face_upper, face_lower)
    face_b = jnp.where(even, face_lower, face_upper)
    ghost_a = jnp.where(even, ghost_upper, ghost_lower)
    ghost_b = jnp.where(even, ghost_lower, ghost_upper)

    lower_at = jnp.where(even, own_count + face, own_count)
    upper_at = jnp.where(even, own_count, own_count + face)
    places = jnp.where(
        connectivity < face,
        connectivity + lower_at,
        jnp.where(
            connectivity < face + own_count,
            connectivity - face,
            connectivity - (face + own_count) + upper_at,
        ),
    ).reshape(-1) * PITCH
    shared_columns = jnp.concatenate([ghost_a, face_a + face, ghost_b, face_b + face])
    own_columns = jnp.arange(own_count, dtype=jnp.int32) + face

    nodes = jnp.broadcast_to(connectivity[:, :, None], connectivity.shape + (LANES,))
    shared_matrix = assemble(places, shared_columns, nodes, cell_matrices, ext_count)
    own_matrix = assemble(places, own_columns, nodes, cell_matrices, ext_count)

    face_nodes = jnp.concatenate([face_a, face_b])
    face_table = (
        face_nodes[:, None] == lax.broadcasted_iota(jnp.int32, (2 * face, own_count), 1)
    ).astype(jnp.bfloat16)

    pairs_a = swap_pairs(slabs, 0)
    pairs_b = swap_pairs(slabs, 1)

    def times(left, right):
        return jnp.dot(left, right, preferred_element_type=jnp.float32)

    def apply_hamiltonian(extended):
        shared = times(extended, shared_matrix)
        sent = shared.astype(jnp.bfloat16)
        got_a = lax.ppermute(sent[:, : 2 * face], "slab", pairs_a)
        got_b = lax.ppermute(sent[:, 2 * face :], "slab", pairs_b)
        own = times(extended, own_matrix)
        incoming = jnp.concatenate([got_a[:, :face], got_b[:, :face]], axis=1)
        own = own + times(incoming, face_table)
        at_a = jnp.where(has_a, shared[:, :face] + got_a[:, face:].astype(jnp.float32), 0.0)
        at_b = jnp.where(
            has_b, shared[:, 2 * face : 3 * face] + got_b[:, face:].astype(jnp.float32), 0.0
        )
        return own, at_a, at_b

    def extend(own, at_a, at_b):
        return jnp.concatenate([own, at_a, at_b], axis=1).astype(jnp.bfloat16)

    faces = lax.dot_general(
        gathered, face_table, (((1,), (1,)), ((), ())), preferred_element_type=jnp.float32
    ).astype(jnp.bfloat16)
    ghosts_a = lax.ppermute(faces[:, :face], "slab", pairs_a)
    ghosts_b = lax.ppermute(faces[:, face:], "slab", pairs_b)
    start = jnp.concatenate([gathered, ghosts_a, ghosts_b], axis=1)
    previous = tuple(x.astype(jnp.float32) for x in (gathered, ghosts_a, ghosts_b))
    current = apply_hamiltonian(start)
    for degree_step in range(1, DEGREE):
        product = apply_hamiltonian(extend(*current))
        following = tuple(2.0 * p - q for p, q in zip(product, previous))
        previous, current = current, following

    filtered = current[0].astype(jnp.bfloat16)
    gram = lax.dot_general(
        filtered, filtered, (((1,), (1,)), ((), ())), preferred_element_type=jnp.float32
    )
    total = sum_over(gram, "slab")
    block = lax.axis_index("orb").astype(jnp.int32).reshape(1)
    return orthonormal(block, total, filtered, orbitals.shape[0], math.sqrt(own_count * slabs))


def solution(mesh):
    in_specs = (P("orb", "slab"), P("slab", None, None), P("slab", None), P("slab"), P("slab"))
    out_specs = P("orb", "slab")
    return jax.shard_map(
        per_device, mesh=mesh, in_specs=in_specs, out_specs=out_specs, check_vma=False
    )
```

```python
import functools
import math

import jax
import jax.numpy as jnp
from jax import lax
from jax.experimental import pallas as pl
from jax.experimental.pallas import tpu as pltpu
from jax.sharding import PartitionSpec as P

DEGREE = 4
LANES = 128
SUBLANES = 8
CHUNK = LANES * SUBLANES


def turn(tiles):
    row = lax.broadcasted_iota(jnp.int32, (SUBLANES, LANES), 0)
    tiles = [pltpu.roll(tile, i, 0) if i else tile for i, tile in enumerate(tiles)]
    step = 1
    while step < SUBLANES:
        far = (row & step) != 0
        tiles = [
            jnp.where(far, tiles[(i + step) % SUBLANES], tiles[i]) for i in range(SUBLANES)
        ]
        step *= 2
    tiles = [tiles[-i % SUBLANES] for i in range(SUBLANES)]
    return [
        pltpu.roll(tile, SUBLANES - i, 0) if i else tile for i, tile in enumerate(tiles)
    ]


def assemble_kernel(places_ref, column_ref, nodes_ref, cell_ref, out_ref, total, even_terms, odd_terms):
    cell = pl.program_id(1)
    cells = pl.num_programs(1)
    cell_nodes = cell_ref.shape[1]
    ext_count = out_ref.shape[0]
    parts = CHUNK // 256
    part_rows = cell_nodes // parts
    group = 32

    def spread_part(part):
        columns = column_ref[:, pl.ds(pl.multiple_of(part * 256, 256), 256)]
        picker = jnp.concatenate(
            [
                (nodes_ref[0] == columns[:, half * LANES : (half + 1) * LANES])
                .astype(jnp.float32)
                .astype(jnp.bfloat16)
                for half in range(2)
            ],
            axis=1,
        )
        return jnp.dot(cell_ref[0], picker, preferred_element_type=jnp.float32)

    def keep_part(part, spread, terms):
        for half in range(2):
            terms[2 * part + half] = spread[:, half * LANES : (half + 1) * LANES]

    def add_part(part, of_cell, terms):
        first = pl.multiple_of(part * part_rows, part_rows)
        for start in range(0, part_rows, group):
            places = [
                pl.multiple_of(places_ref[of_cell * cell_nodes + first + start + k], SUBLANES)
                for k in range(group)
            ]
            added = []
            for inner in range(0, group, SUBLANES):
                added += turn(
                    [terms[b, pl.ds(first + start + inner, SUBLANES), :] for b in range(SUBLANES)]
                )
            sums = [total[pl.ds(places[k], SUBLANES), :] + added[k] for k in range(group)]
            for k in range(group):
                total[pl.ds(places[k], SUBLANES), :] = sums[k]

    @pl.when(cell == 0)
    def _():
        zero_rows = total.shape[0] // parts

        def body(part, carry):
            spread = spread_part(part)
            total[pl.ds(pl.multiple_of(part * zero_rows, SUBLANES), zero_rows), :] = jnp.zeros(
                (zero_rows, LANES), jnp.float32
            )
            keep_part(part, spread, even_terms)
            return carry

        lax.fori_loop(0, parts, body, 0)

    for parity, (before, now) in enumerate(((odd_terms, even_terms), (even_terms, odd_terms))):

        @pl.when((cell > 0) & (cell % 2 == parity))
        def _():
            def body(part, carry):
                spread = spread_part(part)
                add_part(part, cell - 1, before)
                keep_part(part, spread, now)
                return carry

            lax.fori_loop(0, parts, body, 0)

        @pl.when((cell == cells - 1) & (cell % 2 == parity))
        def _():
            def body(part, carry):
                add_part(part, cell, now)
                return carry

            lax.fori_loop(0, parts, body, 0)

    @pl.when(cell == cells - 1)
    def _():
        def write_rows(step, carry):
            first = pl.multiple_of(step * 16, 16)
            upper, lower = (
                turn(
                    [
                        total[pl.ds(pl.multiple_of((first + start + i) * SUBLANES, SUBLANES), SUBLANES), :]
                        for i in range(SUBLANES)
                    ]
                )
                for start in (0, SUBLANES)
            )
            for block in range(SUBLANES):
                out_ref[pl.ds(first, 16), block * LANES : (block + 1) * LANES] = jnp.concatenate(
                    [upper[block], lower[block]], axis=0
                ).astype(jnp.bfloat16)
            return carry

        lax.fori_loop(0, ext_count // 16, write_rows, 0, unroll=4)


def assemble(places, columns, nodes, cell_matrices, ext_count):
    cells, cell_nodes, _ = cell_matrices.shape
    chunks = columns.shape[0] // CHUNK
    return pl.pallas_call(
        assemble_kernel,
        out_shape=jax.ShapeDtypeStruct((ext_count, columns.shape[0]), jnp.bfloat16),
        grid_spec=pltpu.PrefetchScalarGridSpec(
            num_scalar_prefetch=1,
            grid=(chunks, cells),
            in_specs=[
                pl.BlockSpec((1, CHUNK), lambda q, c, places: (0, q)),
                pl.BlockSpec((1, cell_nodes, LANES), lambda q, c, places: (c, 0, 0)),
                pl.BlockSpec((1, cell_nodes, cell_nodes), lambda q, c, places: (c, 0, 0)),
            ],
            out_specs=pl.BlockSpec((ext_count, CHUNK), lambda q, c, places: (0, q)),
            scratch_shapes=[
                pltpu.VMEM((ext_count * SUBLANES, LANES), jnp.float32),
                pltpu.VMEM((SUBLANES, cell_nodes, LANES), jnp.float32),
                pltpu.VMEM((SUBLANES, cell_nodes, LANES), jnp.float32),
            ],
        ),
        compiler_params=pltpu.CompilerParams(vmem_limit_bytes=48 * 1024 * 1024),
        cost_estimate=pl.CostEstimate(
            flops=2 * cells * cell_nodes * cell_nodes * columns.shape[0],
            bytes_accessed=chunks * cells * cell_nodes * cell_nodes * 2 + ext_count * columns.shape[0] * 2,
            transcendentals=0,
        ),
    )(places, columns[None, :], nodes, cell_matrices)


def exact(left, right, contract):
    return lax.dot_general(
        left,
        right,
        (contract, ((), ())),
        precision=lax.Precision.HIGHEST,
        preferred_element_type=jnp.float32,
    )


def inverse_factor(block):
    size = block.shape[0]
    groups = size // SUBLANES
    row = lax.broadcasted_iota(jnp.int32, (SUBLANES, LANES), 0)
    lane = lax.broadcasted_iota(jnp.int32, (SUBLANES, LANES), 1)
    left = [block[g * SUBLANES : (g + 1) * SUBLANES, :] for g in range(groups)]
    right = [(lane == row + g * SUBLANES).astype(jnp.float32) for g in range(groups)]

    def over_rows(values, index):
        return jnp.broadcast_to(values[index : index + 1, :], (SUBLANES, LANES))

    for k in range(groups):
        later = range(k, groups)
        column = {
            g: [
                jnp.broadcast_to(
                    left[g][:, k * SUBLANES + q : k * SUBLANES + q + 1], (SUBLANES, LANES)
                )
                for q in range(SUBLANES)
            ]
            for g in later
        }
        for q in range(SUBLANES):
            scale = lax.rsqrt(over_rows(column[k][q], q))
            factor = {g: column[g][q] * scale for g in later}
            left_row = over_rows(left[k], q) * scale
            right_row = over_rows(right[k], q) * scale
            below = jnp.where(row > q, factor[k], 0.0)
            left[k] = jnp.where(row == q, left_row, left[k] - below * left_row)
            right[k] = jnp.where(row == q, right_row, right[k] - below * right_row)
            for other in range(q + 1, SUBLANES):
                weight = over_rows(factor[k], other)
                for g in later:
                    column[g][other] = column[g][other] - factor[g] * weight
            for g in range(k + 1, groups):
                left[g] = left[g] - factor[g] * left_row
                right[g] = right[g] - factor[g] * right_row
    return jnp.concatenate(right, axis=0)


def orthonormal_kernel(scale, block_ref, gram_ref, filtered_ref, out_ref, inverse):
    size = gram_ref.shape[0]
    count = size // LANES
    at = [slice(i * LANES, (i + 1) * LANES) for i in range(count)]
    lower = {}
    inverses = {}
    for i in range(count):
        diagonal = gram_ref[at[i], at[i]]
        for j in range(i):
            diagonal = diagonal - exact(lower[i, j], lower[i, j], ((1,), (1,)))
        inverses[i, i] = inverse_factor(diagonal)
        for k in range(i + 1, count):
            entry = gram_ref[at[k], at[i]]
            for j in range(i):
                entry = entry - exact(lower[k, j], lower[i, j], ((1,), (1,)))
            lower[k, i] = exact(entry, inverses[i, i], ((1,), (1,)))
    inverse[...] = jnp.zeros_like(inverse)
    for i in range(count):
        for j in range(i):
            entry = exact(lower[i, j], inverses[j, j], ((1,), (0,)))
            for m in range(j + 1, i):
                entry = entry + exact(lower[i, m], inverses[m, j], ((1,), (0,)))
            inverses[i, j] = -exact(inverses[i, i], entry, ((1,), (0,)))
            inverse[at[i], at[j]] = inverses[i, j] * scale
        inverse[at[i], at[i]] = inverses[i, i] * scale
    rows = out_ref.shape[0]
    mine = inverse[pl.ds(pl.multiple_of(block_ref[0] * rows, rows), rows), :]
    high = mine.astype(jnp.bfloat16)
    low = (mine - high.astype(jnp.float32)).astype(jnp.bfloat16)
    width = 512
    for first in range(0, out_ref.shape[1], width):
        part = filtered_ref[:, first : first + width]
        out_ref[:, first : first + width] = jnp.dot(
            high, part, preferred_element_type=jnp.float32
        ) + jnp.dot(low, part, preferred_element_type=jnp.float32)


def orthonormal(block, gram, filtered, rows, scale):
    size = gram.shape[0]
    return pl.pallas_call(
        functools.partial(orthonormal_kernel, scale),
        out_shape=jax.ShapeDtypeStruct((rows, filtered.shape[1]), jnp.float32),
        in_specs=[
            pl.BlockSpec(memory_space=pltpu.SMEM),
            pl.BlockSpec(memory_space=pltpu.VMEM),
            pl.BlockSpec(memory_space=pltpu.VMEM),
        ],
        out_specs=pl.BlockSpec(memory_space=pltpu.VMEM),
        scratch_shapes=[pltpu.VMEM((size, size), jnp.float32)],
        compiler_params=pltpu.CompilerParams(vmem_limit_bytes=16 * 1024 * 1024),
    )(block, gram, filtered)


def swap_pairs(count, first):
    pairs = []
    for low in range(first, count - 1, 2):
        pairs += [(low, low + 1), (low + 1, low)]
    return pairs


def sum_over(values, axis):
    count = lax.axis_size(axis)
    if count & (count - 1):
        return lax.psum(values.astype(jnp.bfloat16), axis).astype(jnp.float32)
    step = 1
    while step < count:
        sent = values.astype(jnp.bfloat16)
        got = lax.ppermute(sent, axis, [(i, i ^ step) for i in range(count)])
        values = sent.astype(jnp.float32) + got.astype(jnp.float32)
        step *= 2
    return values


def per_device(orbitals, cell_matrices, connectivity, face_lower, face_upper):
    own_count = orbitals.shape[1]
    face = face_lower.shape[0]
    ext_count = own_count + 2 * face
    slabs = lax.axis_size("slab")
    slab = lax.axis_index("slab")
    even = slab % 2 == 0

    gathered = lax.all_gather(orbitals.astype(jnp.bfloat16), "orb", axis=0, tiled=True)

    has_lower = slab > 0
    has_upper = slab < slabs - 1
    has_a = jnp.where(even, has_upper, has_lower)
    has_b = jnp.where(even, has_lower, has_upper)
    ghost_lower = jnp.arange(face, dtype=jnp.int32)
    ghost_upper = ghost_lower + (face + own_count)
    face_a = jnp.where(even, face_upper, face_lower)
    face_b = jnp.where(even, face_lower, face_upper)
    ghost_a = jnp.where(even, ghost_upper, ghost_lower)
    ghost_b = jnp.where(even, ghost_lower, ghost_upper)

    lower_at = jnp.where(even, own_count + face, own_count)
    upper_at = jnp.where(even, own_count, own_count + face)
    places = jnp.where(
        connectivity < face,
        connectivity + lower_at,
        jnp.where(
            connectivity < face + own_count,
            connectivity - face,
            connectivity - (face + own_count) + upper_at,
        ),
    ).reshape(-1) * SUBLANES
    shared_columns = jnp.concatenate([ghost_a, face_a + face, ghost_b, face_b + face])
    own_columns = jnp.arange(own_count, dtype=jnp.int32) + face

    nodes = jnp.broadcast_to(connectivity[:, :, None], connectivity.shape + (LANES,))
    shared_matrix = assemble(places, shared_columns, nodes, cell_matrices, ext_count)
    own_matrix = assemble(places, own_columns, nodes, cell_matrices, ext_count)

    face_nodes = jnp.concatenate([face_a, face_b])
    face_table = (
        face_nodes[:, None] == lax.broadcasted_iota(jnp.int32, (2 * face, own_count), 1)
    ).astype(jnp.bfloat16)

    pairs_a = swap_pairs(slabs, 0)
    pairs_b = swap_pairs(slabs, 1)

    def times(left, right):
        return jnp.dot(left, right, preferred_element_type=jnp.float32)

    def apply_hamiltonian(extended):
        shared = times(extended, shared_matrix)
        sent = shared.astype(jnp.bfloat16)
        got_a = lax.ppermute(sent[:, : 2 * face], "slab", pairs_a)
        got_b = lax.ppermute(sent[:, 2 * face :], "slab", pairs_b)
        own = times(extended, own_matrix)
        incoming = jnp.concatenate([got_a[:, :face], got_b[:, :face]], axis=1)
        own = own + times(incoming, face_table)
        at_a = jnp.where(has_a, shared[:, :face] + got_a[:, face:].astype(jnp.float32), 0.0)
        at_b = jnp.where(
            has_b, shared[:, 2 * face : 3 * face] + got_b[:, face:].astype(jnp.float32), 0.0
        )
        return own, at_a, at_b

    def extend(own, at_a, at_b):
        return jnp.concatenate([own, at_a, at_b], axis=1).astype(jnp.bfloat16)

    faces = lax.dot_general(
        gathered, face_table, (((1,), (1,)), ((), ())), preferred_element_type=jnp.float32
    ).astype(jnp.bfloat16)
    ghosts_a = lax.ppermute(faces[:, :face], "slab", pairs_a)
    ghosts_b = lax.ppermute(faces[:, face:], "slab", pairs_b)
    start = jnp.concatenate([gathered, ghosts_a, ghosts_b], axis=1)
    previous = tuple(x.astype(jnp.float32) for x in (gathered, ghosts_a, ghosts_b))
    current = apply_hamiltonian(start)
    for degree_step in range(1, DEGREE):
        product = apply_hamiltonian(extend(*current))
        following = tuple(2.0 * p - q for p, q in zip(product, previous))
        previous, current = current, following

    filtered = current[0].astype(jnp.bfloat16)
    gram = lax.dot_general(
        filtered, filtered, (((1,), (1,)), ((), ())), preferred_element_type=jnp.float32
    )
    total = sum_over(gram, "slab")
    block = lax.axis_index("orb").astype(jnp.int32).reshape(1)
    return orthonormal(block, total, filtered, orbitals.shape[0], math.sqrt(own_count * slabs))


def solution(mesh):
    in_specs = (P("orb", "slab"), P("slab", None, None), P("slab", None), P("slab"), P("slab"))
    out_specs = P("orb", "slab")
    return jax.shard_map(
        per_device, mesh=mesh, in_specs=in_specs, out_specs=out_specs, check_vma=False
    )
```

```python
import functools
import math

import jax
import jax.numpy as jnp
from jax import lax
from jax.experimental import pallas as pl
from jax.experimental.pallas import tpu as pltpu
from jax.sharding import PartitionSpec as P

DEGREE = 4
LANES = 128
SUBLANES = 8
CHUNK = LANES * SUBLANES
PITCH = SUBLANES + 1


def assemble_kernel(
    places_ref, column_ref, nodes_ref, cell_ref, shared_ref, own_ref, total, even_terms, odd_terms
):
    chunk = pl.program_id(0)
    cell = pl.program_id(1)
    cells = pl.num_programs(1)
    cell_nodes = cell_ref.shape[1]
    ext_count = shared_ref.shape[0]
    parts = CHUNK // 256
    part_rows = cell_nodes // parts
    group = 32

    def spread_part(part):
        columns = column_ref[:, pl.ds(pl.multiple_of(part * 256, 256), 256)]
        picker = jnp.concatenate(
            [
                (nodes_ref[0] == columns[:, half * LANES : (half + 1) * LANES])
                .astype(jnp.float32)
                .astype(jnp.bfloat16)
                for half in range(2)
            ],
            axis=1,
        )
        return jnp.dot(cell_ref[0], picker, preferred_element_type=jnp.float32)

    def keep_part(part, spread, terms):
        for first in range(0, cell_nodes, SUBLANES):
            for half in range(2):
                terms[pl.ds(first * PITCH + 2 * part + half, SUBLANES, stride=PITCH), :] = spread[
                    first : first + SUBLANES, half * LANES : (half + 1) * LANES
                ]

    def add_part(part, of_cell, terms):
        first = part * part_rows
        for start in range(0, part_rows, group):
            places = [places_ref[of_cell * cell_nodes + first + start + k] for k in range(group)]
            sums = [
                total[pl.ds(places[k], SUBLANES), :]
                + terms[pl.ds((first + start + k) * PITCH, SUBLANES), :]
                for k in range(group)
            ]
            for k in range(group):
                total[pl.ds(places[k], SUBLANES), :] = sums[k]

    @pl.when(cell == 0)
    def _():
        zero_rows = total.shape[0] // parts

        def body(part, carry):
            spread = spread_part(part)
            total[pl.ds(pl.multiple_of(part * zero_rows, SUBLANES), zero_rows), :] = jnp.zeros(
                (zero_rows, LANES), jnp.float32
            )
            keep_part(part, spread, even_terms)
            return carry

        lax.fori_loop(0, parts, body, 0)

    for parity, (before, now) in enumerate(((odd_terms, even_terms), (even_terms, odd_terms))):

        @pl.when((cell > 0) & (cell % 2 == parity))
        def _():
            def body(part, carry):
                spread = spread_part(part)
                add_part(part, cell - 1, before)
                keep_part(part, spread, now)
                return carry

            lax.fori_loop(0, parts, body, 0)

        @pl.when((cell == cells - 1) & (cell % 2 == parity))
        def _():
            def body(part, carry):
                add_part(part, cell, now)
                return carry

            lax.fori_loop(0, parts, body, 0)

    def write_out(out_ref):
        def write_rows(step, carry):
            first = pl.multiple_of(step * 16, 16)
            for block in range(SUBLANES):
                upper = total[pl.ds(first * PITCH + block, SUBLANES, stride=PITCH), :]
                lower = total[pl.ds((first + 8) * PITCH + block, SUBLANES, stride=PITCH), :]
                out_ref[pl.ds(first, 16), block * LANES : (block + 1) * LANES] = jnp.concatenate(
                    [upper, lower], axis=0
                ).astype(jnp.bfloat16)
            return carry

        lax.fori_loop(0, ext_count // 16, write_rows, 0, unroll=4)

    @pl.when((cell == cells - 1) & (chunk == 0))
    def _():
        write_out(shared_ref)

    @pl.when((cell == cells - 1) & (chunk > 0))
    def _():
        write_out(own_ref)


def assemble(places, columns, nodes, cell_matrices, ext_count):
    cells, cell_nodes, _ = cell_matrices.shape
    chunks = columns.shape[0] // CHUNK
    return pl.pallas_call(
        assemble_kernel,
        out_shape=(
            jax.ShapeDtypeStruct((ext_count, CHUNK), jnp.bfloat16),
            jax.ShapeDtypeStruct((ext_count, columns.shape[0] - CHUNK), jnp.bfloat16),
        ),
        grid_spec=pltpu.PrefetchScalarGridSpec(
            num_scalar_prefetch=1,
            grid=(chunks, cells),
            in_specs=[
                pl.BlockSpec((1, CHUNK), lambda q, c, places: (0, q)),
                pl.BlockSpec((1, cell_nodes, LANES), lambda q, c, places: (c, 0, 0)),
                pl.BlockSpec((1, cell_nodes, cell_nodes), lambda q, c, places: (c, 0, 0)),
            ],
            out_specs=(
                pl.BlockSpec((ext_count, CHUNK), lambda q, c, places: (0, 0)),
                pl.BlockSpec((ext_count, CHUNK), lambda q, c, places: (0, jnp.maximum(q - 1, 0))),
            ),
            scratch_shapes=[
                pltpu.VMEM((ext_count * PITCH, LANES), jnp.float32),
                pltpu.VMEM((cell_nodes * PITCH, LANES), jnp.float32),
                pltpu.VMEM((cell_nodes * PITCH, LANES), jnp.float32),
            ],
        ),
        compiler_params=pltpu.CompilerParams(vmem_limit_bytes=48 * 1024 * 1024),
        cost_estimate=pl.CostEstimate(
            flops=2 * cells * cell_nodes * cell_nodes * columns.shape[0],
            bytes_accessed=chunks * cells * cell_nodes * cell_nodes * 2 + ext_count * columns.shape[0] * 2,
            transcendentals=0,
        ),
    )(places, columns[None, :], nodes, cell_matrices)


def exact(left, right, contract):
    return lax.dot_general(
        left,
        right,
        (contract, ((), ())),
        precision=lax.Precision.HIGHEST,
        preferred_element_type=jnp.float32,
    )


def inverse_factor(block):
    size = block.shape[0]
    groups = size // SUBLANES
    row = lax.broadcasted_iota(jnp.int32, (SUBLANES, LANES), 0)
    lane = lax.broadcasted_iota(jnp.int32, (SUBLANES, LANES), 1)
    left = [block[g * SUBLANES : (g + 1) * SUBLANES, :] for g in range(groups)]
    right = [(lane == row + g * SUBLANES).astype(jnp.float32) for g in range(groups)]

    def over_rows(values, index):
        return jnp.broadcast_to(values[index : index + 1, :], (SUBLANES, LANES))

    for k in range(groups):
        later = range(k, groups)
        column = {
            g: [
                jnp.broadcast_to(
                    left[g][:, k * SUBLANES + q : k * SUBLANES + q + 1], (SUBLANES, LANES)
                )
                for q in range(SUBLANES)
            ]
            for g in later
        }
        for q in range(SUBLANES):
            scale = lax.rsqrt(over_rows(column[k][q], q))
            factor = {g: column[g][q] * scale for g in later}
            left_row = over_rows(left[k], q) * scale
            right_row = over_rows(right[k], q) * scale
            below = jnp.where(row > q, factor[k], 0.0)
            left[k] = jnp.where(row == q, left_row, left[k] - below * left_row)
            right[k] = jnp.where(row == q, right_row, right[k] - below * right_row)
            for other in range(q + 1, SUBLANES):
                weight = over_rows(factor[k], other)
                for g in later:
                    column[g][other] = column[g][other] - factor[g] * weight
            for g in range(k + 1, groups):
                left[g] = left[g] - factor[g] * left_row
                right[g] = right[g] - factor[g] * right_row
    return jnp.concatenate(right, axis=0)


def orthonormal_kernel(scale, block_ref, gram_ref, filtered_ref, out_ref, inverse):
    size = gram_ref.shape[0]
    count = size // LANES
    at = [slice(i * LANES, (i + 1) * LANES) for i in range(count)]
    lower = {}
    inverses = {}
    for i in range(count):
        diagonal = gram_ref[at[i], at[i]]
        for j in range(i):
            diagonal = diagonal - exact(lower[i, j], lower[i, j], ((1,), (1,)))
        inverses[i, i] = inverse_factor(diagonal)
        for k in range(i + 1, count):
            entry = gram_ref[at[k], at[i]]
            for j in range(i):
                entry = entry - exact(lower[k, j], lower[i, j], ((1,), (1,)))
            lower[k, i] = exact(entry, inverses[i, i], ((1,), (1,)))
    inverse[...] = jnp.zeros_like(inverse)
    for i in range(count):
        for j in range(i):
            entry = exact(lower[i, j], inverses[j, j], ((1,), (0,)))
            for m in range(j + 1, i):
                entry = entry + exact(lower[i, m], inverses[m, j], ((1,), (0,)))
            inverses[i, j] = -exact(inverses[i, i], entry, ((1,), (0,)))
            inverse[at[i], at[j]] = inverses[i, j] * scale
        inverse[at[i], at[i]] = inverses[i, i] * scale
    rows = out_ref.shape[0]
    mine = inverse[pl.ds(pl.multiple_of(block_ref[0] * rows, rows), rows), :]
    high = mine.astype(jnp.bfloat16)
    low = (mine - high.astype(jnp.float32)).astype(jnp.bfloat16)
    width = 512
    for first in range(0, out_ref.shape[1], width):
        part = filtered_ref[:, first : first + width]
        out_ref[:, first : first + width] = jnp.dot(
            high, part, preferred_element_type=jnp.float32
        ) + jnp.dot(low, part, preferred_element_type=jnp.float32)


def orthonormal(block, gram, filtered, rows, scale):
    size = gram.shape[0]
    return pl.pallas_call(
        functools.partial(orthonormal_kernel, scale),
        out_shape=jax.ShapeDtypeStruct((rows, filtered.shape[1]), jnp.float32),
        in_specs=[
            pl.BlockSpec(memory_space=pltpu.SMEM),
            pl.BlockSpec(memory_space=pltpu.VMEM),
            pl.BlockSpec(memory_space=pltpu.VMEM),
        ],
        out_specs=pl.BlockSpec(memory_space=pltpu.VMEM),
        scratch_shapes=[pltpu.VMEM((size, size), jnp.float32)],
        compiler_params=pltpu.CompilerParams(vmem_limit_bytes=16 * 1024 * 1024),
    )(block, gram, filtered)


def swap_pairs(count, first):
    pairs = []
    for low in range(first, count - 1, 2):
        pairs += [(low, low + 1), (low + 1, low)]
    return pairs


def sum_over(values, axis):
    count = lax.axis_size(axis)
    if count & (count - 1):
        return lax.psum(values.astype(jnp.bfloat16), axis).astype(jnp.float32)
    step = 1
    while step < count:
        sent = values.astype(jnp.bfloat16)
        got = lax.ppermute(sent, axis, [(i, i ^ step) for i in range(count)])
        values = sent.astype(jnp.float32) + got.astype(jnp.float32)
        step *= 2
    return values


def per_device(orbitals, cell_matrices, connectivity, face_lower, face_upper):
    own_count = orbitals.shape[1]
    face = face_lower.shape[0]
    ext_count = own_count + 2 * face
    slabs = lax.axis_size("slab")
    slab = lax.axis_index("slab")
    even = slab % 2 == 0

    has_lower = slab > 0
    has_upper = slab < slabs - 1
    has_a = jnp.where(even, has_upper, has_lower)
    has_b = jnp.where(even, has_lower, has_upper)
    ghost_lower = jnp.arange(face, dtype=jnp.int32)
    ghost_upper = ghost_lower + (face + own_count)
    face_a = jnp.where(even, face_upper, face_lower)
    face_b = jnp.where(even, face_lower, face_upper)
    ghost_a = jnp.where(even, ghost_upper, ghost_lower)
    ghost_b = jnp.where(even, ghost_lower, ghost_upper)

    lower_at = jnp.where(even, own_count + face, own_count)
    upper_at = jnp.where(even, own_count, own_count + face)
    places = jnp.where(
        connectivity < face,
        connectivity + lower_at,
        jnp.where(
            connectivity < face + own_count,
            connectivity - face,
            connectivity - (face + own_count) + upper_at,
        ),
    ).reshape(-1) * PITCH
    shared_columns = jnp.concatenate([ghost_a, face_a + face, ghost_b, face_b + face])
    own_columns = jnp.arange(own_count, dtype=jnp.int32) + face

    nodes = jnp.broadcast_to(connectivity[:, :, None], connectivity.shape + (LANES,))
    shared_matrix, own_matrix = assemble(
        places, jnp.concatenate([shared_columns, own_columns]), nodes, cell_matrices, ext_count
    )

    face_nodes = jnp.concatenate([face_a, face_b])
    face_table = (
        face_nodes[:, None] == lax.broadcasted_iota(jnp.int32, (2 * face, own_count), 1)
    ).astype(jnp.bfloat16)

    pairs_a = swap_pairs(slabs, 0)
    pairs_b = swap_pairs(slabs, 1)

    def times(left, right):
        return jnp.dot(left, right, preferred_element_type=jnp.float32)

    def apply_hamiltonian(extended):
        shared = times(extended, shared_matrix)
        sent = shared.astype(jnp.bfloat16)
        got_a = lax.ppermute(sent[:, : 2 * face], "slab", pairs_a)
        got_b = lax.ppermute(sent[:, 2 * face :], "slab", pairs_b)
        own = times(extended, own_matrix)
        incoming = jnp.concatenate([got_a[:, :face], got_b[:, :face]], axis=1)
        own = own + times(incoming, face_table)
        at_a = jnp.where(has_a, shared[:, :face] + got_a[:, face:].astype(jnp.float32), 0.0)
        at_b = jnp.where(
            has_b, shared[:, 2 * face : 3 * face] + got_b[:, face:].astype(jnp.float32), 0.0
        )
        return own, at_a, at_b

    def extend(own, at_a, at_b):
        return jnp.concatenate([own, at_a, at_b], axis=1).astype(jnp.bfloat16)

    rounded = orbitals.astype(jnp.bfloat16)
    faces = lax.dot_general(
        rounded, face_table, (((1,), (1,)), ((), ())), preferred_element_type=jnp.float32
    ).astype(jnp.bfloat16)
    ghosts_a = lax.ppermute(faces[:, :face], "slab", pairs_a)
    ghosts_b = lax.ppermute(faces[:, face:], "slab", pairs_b)
    start = lax.all_gather(
        jnp.concatenate([rounded, ghosts_a, ghosts_b], axis=1), "orb", axis=0, tiled=True
    )
    previous = (
        start[:, :own_count],
        start[:, own_count : own_count + face],
        start[:, own_count + face :],
    )
    current = apply_hamiltonian(start)
    for degree_step in range(1, DEGREE):
        product = apply_hamiltonian(extend(*current))
        following = tuple(
            2.0 * p - q.astype(jnp.float32) for p, q in zip(product, previous)
        )
        previous, current = current, following

    filtered = current[0].astype(jnp.bfloat16)
    gram = lax.dot_general(
        filtered, filtered, (((1,), (1,)), ((), ())), preferred_element_type=jnp.float32
    )
    total = sum_over(gram, "slab")
    block = lax.axis_index("orb").astype(jnp.int32).reshape(1)
    return orthonormal(block, total, filtered, orbitals.shape[0], math.sqrt(own_count * slabs))


def solution(mesh):
    in_specs = (P("orb", "slab"), P("slab", None, None), P("slab", None), P("slab"), P("slab"))
    out_specs = P("orb", "slab")
    return jax.shard_map(
        per_device, mesh=mesh, in_specs=in_specs, out_specs=out_specs, check_vma=False
    )
```

```python
import functools
import math

import jax
import jax.numpy as jnp
from jax import lax
from jax.experimental import pallas as pl
from jax.experimental.pallas import tpu as pltpu
from jax.sharding import PartitionSpec as P

DEGREE = 4
LANES = 128
SUBLANES = 8
CHUNK = LANES * SUBLANES
PITCH = SUBLANES + 1


def assemble_kernel(
    places_ref, column_ref, nodes_ref, cell_ref, after_ref, out_ref, total, even_terms, odd_terms
):
    cell = pl.program_id(0)
    cells = pl.num_programs(0)
    cell_nodes = cell_ref.shape[1]
    ext_count = out_ref.shape[0]
    parts = CHUNK // 256
    part_rows = cell_nodes // parts
    group = 32

    def spread_part(part):
        columns = column_ref[:, pl.ds(part * 256, 256) if isinstance(part, int) else pl.ds(pl.multiple_of(part * 256, 256), 256)]
        picker = jnp.concatenate(
            [
                (nodes_ref[0] == columns[:, half * LANES : (half + 1) * LANES])
                .astype(jnp.float32)
                .astype(jnp.bfloat16)
                for half in range(2)
            ],
            axis=1,
        )
        return jnp.dot(cell_ref[0], picker, preferred_element_type=jnp.float32)

    def keep_part(part, spread, terms):
        for first in range(0, cell_nodes, SUBLANES):
            for half in range(2):
                terms[pl.ds(first * PITCH + 2 * part + half, SUBLANES, stride=PITCH), :] = spread[
                    first : first + SUBLANES, half * LANES : (half + 1) * LANES
                ]

    def add_part(part, of_cell, terms):
        first = part * part_rows
        for start in range(0, part_rows, group):
            places = [places_ref[of_cell * cell_nodes + first + start + k] for k in range(group)]
            sums = [
                total[pl.ds(places[k], SUBLANES), :]
                + terms[pl.ds((first + start + k) * PITCH, SUBLANES), :]
                for k in range(group)
            ]
            for k in range(group):
                total[pl.ds(places[k], SUBLANES), :] = sums[k]

    @pl.when(cell == 0)
    def _():
        zero_rows = total.shape[0] // parts

        def body(part, carry):
            spread = spread_part(part)
            total[pl.ds(pl.multiple_of(part * zero_rows, SUBLANES), zero_rows), :] = jnp.zeros(
                (zero_rows, LANES), jnp.float32
            )
            keep_part(part, spread, even_terms)
            return carry

        lax.fori_loop(0, parts, body, 0)

    for parity, (before, now) in enumerate(((odd_terms, even_terms), (even_terms, odd_terms))):

        @pl.when((cell > 0) & (cell % 2 == parity))
        def _():
            spread = spread_part(0)
            for part in range(parts):
                following = spread_part(part + 1) if part + 1 < parts else None
                add_part(part, cell - 1, before)
                keep_part(part, spread, now)
                spread = following

        @pl.when((cell == cells - 1) & (cell % 2 == parity))
        def _():
            def body(part, carry):
                add_part(part, cell, now)
                return carry

            lax.fori_loop(0, parts, body, 0)

    @pl.when(cell == cells - 1)
    def _():
        def write_rows(step, carry):
            first = pl.multiple_of(step * 16, 16)
            for block in range(SUBLANES):
                upper = total[pl.ds(first * PITCH + block, SUBLANES, stride=PITCH), :]
                lower = total[pl.ds((first + 8) * PITCH + block, SUBLANES, stride=PITCH), :]
                out_ref[pl.ds(first, 16), block * LANES : (block + 1) * LANES] = jnp.concatenate(
                    [upper, lower], axis=0
                ).astype(jnp.bfloat16)
            return carry

        lax.fori_loop(0, ext_count // 16, write_rows, 0, unroll=4)


def assemble(places, columns, nodes, cell_matrices, ext_count, after):
    cells, cell_nodes, _ = cell_matrices.shape
    return pl.pallas_call(
        assemble_kernel,
        out_shape=jax.ShapeDtypeStruct((ext_count, CHUNK), jnp.bfloat16),
        grid_spec=pltpu.PrefetchScalarGridSpec(
            num_scalar_prefetch=1,
            grid=(cells,),
            in_specs=[
                pl.BlockSpec((1, CHUNK), lambda c, places: (0, 0)),
                pl.BlockSpec((1, cell_nodes, LANES), lambda c, places: (c, 0, 0)),
                pl.BlockSpec((1, cell_nodes, cell_nodes), lambda c, places: (c, 0, 0)),
                pl.BlockSpec(memory_space=pl.ANY),
            ],
            out_specs=pl.BlockSpec((ext_count, CHUNK), lambda c, places: (0, 0)),
            scratch_shapes=[
                pltpu.VMEM((ext_count * PITCH, LANES), jnp.float32),
                pltpu.VMEM((cell_nodes * PITCH, LANES), jnp.float32),
                pltpu.VMEM((cell_nodes * PITCH, LANES), jnp.float32),
            ],
        ),
        compiler_params=pltpu.CompilerParams(vmem_limit_bytes=32 * 1024 * 1024),
        cost_estimate=pl.CostEstimate(
            flops=16 * cells * cell_nodes * cell_nodes * CHUNK,
            bytes_accessed=cells * cell_nodes * cell_nodes * 2 + ext_count * CHUNK * 2,
            transcendentals=0,
        ),
    )(places, columns[None, :], nodes, cell_matrices, after)


def exact(left, right, contract):
    return lax.dot_general(
        left,
        right,
        (contract, ((), ())),
        precision=lax.Precision.HIGHEST,
        preferred_element_type=jnp.float32,
    )


def inverse_factor(block):
    size = block.shape[0]
    groups = size // SUBLANES
    row = lax.broadcasted_iota(jnp.int32, (SUBLANES, LANES), 0)
    lane = lax.broadcasted_iota(jnp.int32, (SUBLANES, LANES), 1)
    left = [block[g * SUBLANES : (g + 1) * SUBLANES, :] for g in range(groups)]
    right = [(lane == row + g * SUBLANES).astype(jnp.float32) for g in range(groups)]

    def over_rows(values, index):
        return jnp.broadcast_to(values[index : index + 1, :], (SUBLANES, LANES))

    for k in range(groups):
        later = range(k, groups)
        column = {
            g: [
                jnp.broadcast_to(
                    left[g][:, k * SUBLANES + q : k * SUBLANES + q + 1], (SUBLANES, LANES)
                )
                for q in range(SUBLANES)
            ]
            for g in later
        }
        for q in range(SUBLANES):
            scale = lax.rsqrt(over_rows(column[k][q], q))
            factor = {g: column[g][q] * scale for g in later}
            left_row = over_rows(left[k], q) * scale
            right_row = over_rows(right[k], q) * scale
            below = jnp.where(row > q, factor[k], 0.0)
            left[k] = jnp.where(row == q, left_row, left[k] - below * left_row)
            right[k] = jnp.where(row == q, right_row, right[k] - below * right_row)
            for other in range(q + 1, SUBLANES):
                weight = over_rows(factor[k], other)
                for g in later:
                    column[g][other] = column[g][other] - factor[g] * weight
            for g in range(k + 1, groups):
                left[g] = left[g] - factor[g] * left_row
                right[g] = right[g] - factor[g] * right_row
    return jnp.concatenate(right, axis=0)


def orthonormal_kernel(scale, block_ref, gram_ref, filtered_ref, out_ref, inverse):
    size = gram_ref.shape[0]
    count = size // LANES
    at = [slice(i * LANES, (i + 1) * LANES) for i in range(count)]
    lower = {}
    inverses = {}
    for i in range(count):
        diagonal = gram_ref[at[i], at[i]]
        for j in range(i):
            diagonal = diagonal - exact(lower[i, j], lower[i, j], ((1,), (1,)))
        inverses[i, i] = inverse_factor(diagonal)
        for k in range(i + 1, count):
            entry = gram_ref[at[k], at[i]]
            for j in range(i):
                entry = entry - exact(lower[k, j], lower[i, j], ((1,), (1,)))
            lower[k, i] = exact(entry, inverses[i, i], ((1,), (1,)))
    inverse[...] = jnp.zeros_like(inverse)
    for i in range(count):
        for j in range(i):
            entry = exact(lower[i, j], inverses[j, j], ((1,), (0,)))
            for m in range(j + 1, i):
                entry = entry + exact(lower[i, m], inverses[m, j], ((1,), (0,)))
            inverses[i, j] = -exact(inverses[i, i], entry, ((1,), (0,)))
            inverse[at[i], at[j]] = inverses[i, j] * scale
        inverse[at[i], at[i]] = inverses[i, i] * scale
    rows = out_ref.shape[0]
    mine = inverse[pl.ds(pl.multiple_of(block_ref[0] * rows, rows), rows), :]
    high = mine.astype(jnp.bfloat16)
    low = (mine - high.astype(jnp.float32)).astype(jnp.bfloat16)
    width = 512
    for first in range(0, out_ref.shape[1], width):
        part = filtered_ref[:, first : first + width]
        out_ref[:, first : first + width] = jnp.dot(
            high, part, preferred_element_type=jnp.float32
        ) + jnp.dot(low, part, preferred_element_type=jnp.float32)


def orthonormal(block, gram, filtered, rows, scale):
    size = gram.shape[0]
    return pl.pallas_call(
        functools.partial(orthonormal_kernel, scale),
        out_shape=jax.ShapeDtypeStruct((rows, filtered.shape[1]), jnp.float32),
        in_specs=[
            pl.BlockSpec(memory_space=pltpu.SMEM),
            pl.BlockSpec(memory_space=pltpu.VMEM),
            pl.BlockSpec(memory_space=pltpu.VMEM),
        ],
        out_specs=pl.BlockSpec(memory_space=pltpu.VMEM),
        scratch_shapes=[pltpu.VMEM((size, size), jnp.float32)],
        compiler_params=pltpu.CompilerParams(vmem_limit_bytes=16 * 1024 * 1024),
    )(block, gram, filtered)


def swap_pairs(count, first):
    pairs = []
    for low in range(first, count - 1, 2):
        pairs += [(low, low + 1), (low + 1, low)]
    return pairs


def sum_over(values, axis):
    count = lax.axis_size(axis)
    if count & (count - 1):
        return lax.psum(values.astype(jnp.bfloat16), axis).astype(jnp.float32)
    step = 1
    while step < count:
        sent = values.astype(jnp.bfloat16)
        got = lax.ppermute(sent, axis, [(i, i ^ step) for i in range(count)])
        values = sent.astype(jnp.float32) + got.astype(jnp.float32)
        step *= 2
    return values


def per_device(orbitals, cell_matrices, connectivity, face_lower, face_upper):
    own_count = orbitals.shape[1]
    face = face_lower.shape[0]
    ext_count = own_count + 2 * face
    slabs = lax.axis_size("slab")
    slab = lax.axis_index("slab")
    even = slab % 2 == 0

    has_lower = slab > 0
    has_upper = slab < slabs - 1
    has_a = jnp.where(even, has_upper, has_lower)
    has_b = jnp.where(even, has_lower, has_upper)
    ghost_lower = jnp.arange(face, dtype=jnp.int32)
    ghost_upper = ghost_lower + (face + own_count)
    face_a = jnp.where(even, face_upper, face_lower)
    face_b = jnp.where(even, face_lower, face_upper)
    ghost_a = jnp.where(even, ghost_upper, ghost_lower)
    ghost_b = jnp.where(even, ghost_lower, ghost_upper)

    lower_at = jnp.where(even, own_count + face, own_count)
    upper_at = jnp.where(even, own_count, own_count + face)
    places = jnp.where(
        connectivity < face,
        connectivity + lower_at,
        jnp.where(
            connectivity < face + own_count,
            connectivity - face,
            connectivity - (face + own_count) + upper_at,
        ),
    ).reshape(-1) * PITCH
    shared_columns = jnp.concatenate([ghost_a, face_a + face, ghost_b, face_b + face])
    own_columns = jnp.arange(own_count, dtype=jnp.int32) + face

    nodes = jnp.broadcast_to(connectivity[:, :, None], connectivity.shape + (LANES,))
    face_nodes = jnp.concatenate([face_a, face_b])
    face_table = (
        face_nodes[:, None] == lax.broadcasted_iota(jnp.int32, (2 * face, own_count), 1)
    ).astype(jnp.bfloat16)

    pairs_a = swap_pairs(slabs, 0)
    pairs_b = swap_pairs(slabs, 1)

    def times(left, right):
        return jnp.dot(left, right, preferred_element_type=jnp.float32)

    def apply_hamiltonian(extended):
        shared = times(extended, shared_matrix)
        sent = shared.astype(jnp.bfloat16)
        if len(own_matrices) * CHUNK < own_count:
            own_matrices.append(assembled(own_columns[own_count - CHUNK :], sent))
        got_a = lax.ppermute(sent[:, : 2 * face], "slab", pairs_a)
        got_b = lax.ppermute(sent[:, 2 * face :], "slab", pairs_b)
        own = jnp.concatenate([times(extended, matrix) for matrix in own_matrices], axis=1)
        incoming = jnp.concatenate([got_a[:, :face], got_b[:, :face]], axis=1)
        own = own + times(incoming, face_table)
        at_a = jnp.where(has_a, shared[:, :face] + got_a[:, face:].astype(jnp.float32), 0.0)
        at_b = jnp.where(
            has_b, shared[:, 2 * face : 3 * face] + got_b[:, face:].astype(jnp.float32), 0.0
        )
        return own, at_a, at_b

    def extend(own, at_a, at_b):
        return jnp.concatenate([own, at_a, at_b], axis=1).astype(jnp.bfloat16)

    rounded = orbitals.astype(jnp.bfloat16)
    faces = lax.dot_general(
        rounded, face_table, (((1,), (1,)), ((), ())), preferred_element_type=jnp.float32
    ).astype(jnp.bfloat16)
    ghosts_a = lax.ppermute(faces[:, :face], "slab", pairs_a)
    ghosts_b = lax.ppermute(faces[:, face:], "slab", pairs_b)
    mine = jnp.concatenate([rounded, ghosts_a, ghosts_b], axis=1)
    start = lax.all_gather(mine, "orb", axis=0, tiled=True)

    def assembled(columns, after):
        return assemble(places, columns, nodes, cell_matrices, ext_count, after)

    shared_matrix = assembled(shared_columns, mine)
    own_matrices = [
        assembled(own_columns[first : first + CHUNK], mine)
        for first in range(0, own_count - CHUNK, CHUNK)
    ]
    previous = (
        start[:, :own_count],
        start[:, own_count : own_count + face],
        start[:, own_count + face :],
    )
    current = apply_hamiltonian(start)
    for degree_step in range(1, DEGREE):
        product = apply_hamiltonian(extend(*current))
        following = tuple(
            2.0 * p - q.astype(jnp.float32) for p, q in zip(product, previous)
        )
        previous, current = current, following

    filtered = current[0].astype(jnp.bfloat16)
    gram = lax.dot_general(
        filtered, filtered, (((1,), (1,)), ((), ())), preferred_element_type=jnp.float32
    )
    total = sum_over(gram, "slab")
    block = lax.axis_index("orb").astype(jnp.int32).reshape(1)
    return orthonormal(block, total, filtered, orbitals.shape[0], math.sqrt(own_count * slabs))


def solution(mesh):
    in_specs = (P("orb", "slab"), P("slab", None, None), P("slab", None), P("slab"), P("slab"))
    out_specs = P("orb", "slab")
    return jax.shard_map(
        per_device, mesh=mesh, in_specs=in_specs, out_specs=out_specs, check_vma=False
    )
```

```python
import functools
import math

import jax
import jax.numpy as jnp
from jax import lax
from jax.experimental import pallas as pl
from jax.experimental.pallas import tpu as pltpu
from jax.sharding import PartitionSpec as P

DEGREE = 4
LANES = 128
SUBLANES = 8
CHUNK = LANES * SUBLANES
PITCH = SUBLANES + 1


def assemble_kernel(outputs, places_ref, column_ref, nodes_ref, cells_ref, *refs):
    total, even_terms, odd_terms, fetched, arrived = refs[-5:]
    out_refs = refs[-5 - outputs : -5]
    cell = pl.program_id(0)
    cells = pl.num_programs(0)
    cell_nodes = fetched.shape[1]
    ext_count = out_refs[0].shape[0]
    parts = CHUNK // 256
    part_rows = cell_nodes // parts
    group = 32

    def fetch(index, slot):
        return pltpu.make_async_copy(cells_ref.at[index], fetched.at[slot], arrived.at[slot])

    def spread_part(part, slot):
        columns = column_ref[:, part * 256 : (part + 1) * 256]
        picker = jnp.concatenate(
            [
                (nodes_ref[0] == columns[:, half * LANES : (half + 1) * LANES])
                .astype(jnp.float32)
                .astype(jnp.bfloat16)
                for half in range(2)
            ],
            axis=1,
        )
        return jnp.dot(fetched[slot], picker, preferred_element_type=jnp.float32)

    def keep_part(part, spread, terms):
        for first in range(0, cell_nodes, SUBLANES):
            for half in range(2):
                terms[pl.ds(first * PITCH + 2 * part + half, SUBLANES, stride=PITCH), :] = spread[
                    first : first + SUBLANES, half * LANES : (half + 1) * LANES
                ]

    def add_part(part, of_cell, terms):
        first = part * part_rows
        for start in range(0, part_rows, group):
            places = [places_ref[of_cell * cell_nodes + first + start + k] for k in range(group)]
            sums = [
                total[pl.ds(places[k], SUBLANES), :]
                + terms[pl.ds((first + start + k) * PITCH, SUBLANES), :]
                for k in range(group)
            ]
            for k in range(group):
                total[pl.ds(places[k], SUBLANES), :] = sums[k]

    @pl.when(cell == 0)
    def _():
        fetch(0, 0).start()
        fetch(1, 1).start()
        total[...] = jnp.zeros_like(total)
        fetch(0, 0).wait()
        for part in range(parts):
            keep_part(part, spread_part(part, 0), even_terms)

    for parity, (before, now) in enumerate(((odd_terms, even_terms), (even_terms, odd_terms))):

        @pl.when((cell > 0) & (cell % 2 == parity))
        def _():
            @pl.when(cell + 1 < cells)
            def _():
                fetch(cell + 1, 1 - parity).start()

            fetch(cell, parity).wait()
            spread = spread_part(0, parity)
            for part in range(parts):
                following = spread_part(part + 1, parity) if part + 1 < parts else None
                add_part(part, cell - 1, before)
                keep_part(part, spread, now)
                spread = following

        @pl.when((cell == cells - 1) & (cell % 2 == parity))
        def _():
            def body(part, carry):
                add_part(part, cell, now)
                return carry

            lax.fori_loop(0, parts, body, 0)

    @pl.when(cell == cells - 1)
    def _():
        per_out = SUBLANES // outputs

        def write_rows(step, carry):
            first = pl.multiple_of(step * 16, 16)
            for block in range(SUBLANES):
                upper = total[pl.ds(first * PITCH + block, SUBLANES, stride=PITCH), :]
                lower = total[pl.ds((first + 8) * PITCH + block, SUBLANES, stride=PITCH), :]
                at = block % per_out * LANES
                out_refs[block // per_out][pl.ds(first, 16), at : at + LANES] = jnp.concatenate(
                    [upper, lower], axis=0
                ).astype(jnp.bfloat16)
            return carry

        lax.fori_loop(0, ext_count // 16, write_rows, 0, unroll=4)


def assemble(places, columns, nodes, cell_matrices, shapes, after, at=0, partial=None):
    cells, cell_nodes, _ = cell_matrices.shape
    ext_count = shapes[0][0]
    width = CHUNK // len(shapes)
    extra = (after,) if partial is None else (after, partial)
    return pl.pallas_call(
        functools.partial(assemble_kernel, len(shapes)),
        out_shape=tuple(jax.ShapeDtypeStruct(shape, jnp.bfloat16) for shape in shapes),
        grid_spec=pltpu.PrefetchScalarGridSpec(
            num_scalar_prefetch=1,
            grid=(cells,),
            in_specs=[
                pl.BlockSpec((1, CHUNK), lambda c, places: (0, 0)),
                pl.BlockSpec((1, cell_nodes, LANES), lambda c, places: (c, 0, 0)),
                pl.BlockSpec(memory_space=pltpu.HBM),
            ]
            + [pl.BlockSpec(memory_space=pl.ANY)] * len(extra),
            out_specs=tuple(pl.BlockSpec((ext_count, width), lambda c, places: (0, at)) for _ in shapes),
            scratch_shapes=[
                pltpu.VMEM((ext_count * PITCH, LANES), jnp.float32),
                pltpu.VMEM((cell_nodes * PITCH, LANES), jnp.float32),
                pltpu.VMEM((cell_nodes * PITCH, LANES), jnp.float32),
                pltpu.VMEM((2, cell_nodes, cell_nodes), jnp.bfloat16),
                pltpu.SemaphoreType.DMA((2,)),
            ],
        ),
        input_output_aliases={} if partial is None else {5: 0},
        compiler_params=pltpu.CompilerParams(vmem_limit_bytes=32 * 1024 * 1024),
        cost_estimate=pl.CostEstimate(
            flops=16 * cells * cell_nodes * cell_nodes * CHUNK,
            bytes_accessed=cells * cell_nodes * cell_nodes * 2 + ext_count * CHUNK * 2,
            transcendentals=0,
        ),
    )(places, columns[None, :], nodes, cell_matrices, *extra)


def join_kernel(left_ref, right_ref, out_ref):
    width = left_ref.shape[1]
    out_ref[:, :width] = left_ref[...]
    out_ref[:, width:] = right_ref[...]


def join(left, right):
    return pl.pallas_call(
        join_kernel,
        out_shape=jax.ShapeDtypeStruct((left.shape[0], left.shape[1] + right.shape[1]), left.dtype),
        compiler_params=pltpu.CompilerParams(vmem_limit_bytes=16 * 1024 * 1024),
    )(left, right)


def own_kernel(first_step, extended_ref, matrix_ref, previous_ref, *refs):
    out_ref = refs[-1]
    width = 256

    def body(step, carry):
        at = pl.ds(pl.multiple_of(step * width, width), width)
        product = jnp.dot(extended_ref[...], matrix_ref[:, at], preferred_element_type=jnp.float32)
        if not first_step:
            product = 2.0 * product - previous_ref[:, at].astype(jnp.float32)
        out_ref[:, at] = product
        return carry

    lax.fori_loop(0, out_ref.shape[1] // width, body, 0)


def own_part(first_step, extended, matrix, previous, after):
    rows, depth = extended.shape
    columns = matrix.shape[1]
    whole = pl.BlockSpec(memory_space=pltpu.VMEM)
    return pl.pallas_call(
        functools.partial(own_kernel, first_step),
        out_shape=jax.ShapeDtypeStruct((rows, columns), jnp.float32),
        in_specs=[whole] * 3 + [pl.BlockSpec(memory_space=pl.ANY)] * len(after),
        out_specs=whole,
        compiler_params=pltpu.CompilerParams(vmem_limit_bytes=16 * 1024 * 1024),
        cost_estimate=pl.CostEstimate(
            flops=8 * rows * depth * columns,
            bytes_accessed=2 * depth * columns + 4 * rows * columns,
            transcendentals=0,
        ),
    )(extended, matrix, previous, *after)


def exact(left, right, contract):
    return lax.dot_general(
        left,
        right,
        (contract, ((), ())),
        precision=lax.Precision.HIGHEST,
        preferred_element_type=jnp.float32,
    )


def inverse_factor(block):
    size = block.shape[0]
    groups = size // SUBLANES
    row = lax.broadcasted_iota(jnp.int32, (SUBLANES, LANES), 0)
    lane = lax.broadcasted_iota(jnp.int32, (SUBLANES, LANES), 1)
    left = [block[g * SUBLANES : (g + 1) * SUBLANES, :] for g in range(groups)]
    right = [(lane == row + g * SUBLANES).astype(jnp.float32) for g in range(groups)]

    def over_rows(values, index):
        return jnp.broadcast_to(values[index : index + 1, :], (SUBLANES, LANES))

    for k in range(groups):
        later = range(k, groups)
        column = {
            g: [
                jnp.broadcast_to(
                    left[g][:, k * SUBLANES + q : k * SUBLANES + q + 1], (SUBLANES, LANES)
                )
                for q in range(SUBLANES)
            ]
            for g in later
        }
        for q in range(SUBLANES):
            scale = lax.rsqrt(over_rows(column[k][q], q))
            factor = {g: column[g][q] * scale for g in later}
            left_row = over_rows(left[k], q) * scale
            right_row = over_rows(right[k], q) * scale
            below = jnp.where(row > q, factor[k], 0.0)
            left[k] = jnp.where(row == q, left_row, left[k] - below * left_row)
            right[k] = jnp.where(row == q, right_row, right[k] - below * right_row)
            for other in range(q + 1, SUBLANES):
                weight = over_rows(factor[k], other)
                for g in later:
                    column[g][other] = column[g][other] - factor[g] * weight
            for g in range(k + 1, groups):
                left[g] = left[g] - factor[g] * left_row
                right[g] = right[g] - factor[g] * right_row
    return jnp.concatenate(right, axis=0)


def orthonormal_kernel(scale, block_ref, gram_ref, filtered_ref, out_ref, inverse):
    size = gram_ref.shape[0]
    count = size // LANES
    at = [slice(i * LANES, (i + 1) * LANES) for i in range(count)]
    lower = {}
    inverses = {}
    for i in range(count):
        diagonal = gram_ref[at[i], at[i]]
        for j in range(i):
            diagonal = diagonal - exact(lower[i, j], lower[i, j], ((1,), (1,)))
        inverses[i, i] = inverse_factor(diagonal)
        for k in range(i + 1, count):
            entry = gram_ref[at[k], at[i]]
            for j in range(i):
                entry = entry - exact(lower[k, j], lower[i, j], ((1,), (1,)))
            lower[k, i] = exact(entry, inverses[i, i], ((1,), (1,)))
    inverse[...] = jnp.zeros_like(inverse)
    for i in range(count):
        for j in range(i):
            entry = exact(lower[i, j], inverses[j, j], ((1,), (0,)))
            for m in range(j + 1, i):
                entry = entry + exact(lower[i, m], inverses[m, j], ((1,), (0,)))
            inverses[i, j] = -exact(inverses[i, i], entry, ((1,), (0,)))
            inverse[at[i], at[j]] = inverses[i, j] * scale
        inverse[at[i], at[i]] = inverses[i, i] * scale
    rows = out_ref.shape[0]
    mine = inverse[pl.ds(pl.multiple_of(block_ref[0] * rows, rows), rows), :]
    high = mine.astype(jnp.bfloat16)
    low = (mine - high.astype(jnp.float32)).astype(jnp.bfloat16)
    width = 512
    for first in range(0, out_ref.shape[1], width):
        part = filtered_ref[:, first : first + width]
        out_ref[:, first : first + width] = jnp.dot(
            high, part, preferred_element_type=jnp.float32
        ) + jnp.dot(low, part, preferred_element_type=jnp.float32)


def orthonormal(block, gram, filtered, rows, scale):
    size = gram.shape[0]
    return pl.pallas_call(
        functools.partial(orthonormal_kernel, scale),
        out_shape=jax.ShapeDtypeStruct((rows, filtered.shape[1]), jnp.float32),
        in_specs=[
            pl.BlockSpec(memory_space=pltpu.SMEM),
            pl.BlockSpec(memory_space=pltpu.VMEM),
            pl.BlockSpec(memory_space=pltpu.VMEM),
        ],
        out_specs=pl.BlockSpec(memory_space=pltpu.VMEM),
        scratch_shapes=[pltpu.VMEM((size, size), jnp.float32)],
        compiler_params=pltpu.CompilerParams(vmem_limit_bytes=16 * 1024 * 1024),
    )(block, gram, filtered)


def swap_pairs(count, first):
    pairs = []
    for low in range(first, count - 1, 2):
        pairs += [(low, low + 1), (low + 1, low)]
    return pairs


def sum_over(values, axis):
    count = lax.axis_size(axis)
    if count & (count - 1):
        return lax.psum(values.astype(jnp.bfloat16), axis).astype(jnp.float32)
    step = 1
    while step < count:
        sent = values.astype(jnp.bfloat16)
        got = lax.ppermute(sent, axis, [(i, i ^ step) for i in range(count)])
        values = sent.astype(jnp.float32) + got.astype(jnp.float32)
        step *= 2
    return values


def per_device(orbitals, cell_matrices, connectivity, face_lower, face_upper):
    own_count = orbitals.shape[1]
    face = face_lower.shape[0]
    ext_count = own_count + 2 * face
    slabs = lax.axis_size("slab")
    slab = lax.axis_index("slab")
    even = slab % 2 == 0

    has_lower = slab > 0
    has_upper = slab < slabs - 1
    has_a = jnp.where(even, has_upper, has_lower)
    has_b = jnp.where(even, has_lower, has_upper)
    ghost_lower = jnp.arange(face, dtype=jnp.int32)
    ghost_upper = ghost_lower + (face + own_count)
    face_a = jnp.where(even, face_upper, face_lower)
    face_b = jnp.where(even, face_lower, face_upper)
    ghost_a = jnp.where(even, ghost_upper, ghost_lower)
    ghost_b = jnp.where(even, ghost_lower, ghost_upper)

    lower_at = jnp.where(even, own_count + face, own_count)
    upper_at = jnp.where(even, own_count, own_count + face)
    places = jnp.where(
        connectivity < face,
        connectivity + lower_at,
        jnp.where(
            connectivity < face + own_count,
            connectivity - face,
            connectivity - (face + own_count) + upper_at,
        ),
    ).reshape(-1) * PITCH
    columns_b = jnp.concatenate([ghost_b, face_b + face])
    columns_a = jnp.concatenate([ghost_a, face_a + face])
    own_columns = jnp.arange(own_count, dtype=jnp.int32) + face
    nodes = jnp.broadcast_to(connectivity[:, :, None], connectivity.shape + (LANES,))

    face_nodes = jnp.concatenate([face_a, face_b])
    face_table = (
        face_nodes[:, None] == lax.broadcasted_iota(jnp.int32, (2 * face, own_count), 1)
    ).astype(jnp.bfloat16)

    pairs_a = swap_pairs(slabs, 0)
    pairs_b = swap_pairs(slabs, 1)

    def times(left, right):
        return jnp.dot(left, right, preferred_element_type=jnp.float32)

    rounded = orbitals.astype(jnp.bfloat16)
    own_start = lax.all_gather(rounded, "orb", axis=0, tiled=True)
    faces = lax.dot_general(
        rounded, face_table, (((1,), (1,)), ((), ())), preferred_element_type=jnp.float32
    ).astype(jnp.bfloat16)
    ghosts_b = lax.ppermute(faces[:, face:], "slab", pairs_b)
    ghosts_a = lax.ppermute(faces[:, :face], "slab", pairs_a)
    ghosts = jnp.concatenate([ghosts_a, ghosts_b], axis=1)
    ghost_start = lax.all_gather(ghosts, "orb", axis=0, tiled=True)

    matrix_b, matrix_a = assemble(
        places,
        jnp.concatenate([columns_b, columns_a]),
        nodes,
        cell_matrices,
        ((ext_count, 2 * face), (ext_count, 2 * face)),
        faces,
    )

    def assemble_own(first, after, partial):
        return assemble(
            places,
            own_columns[first : first + CHUNK],
            nodes,
            cell_matrices,
            ((ext_count, own_count),),
            after,
            first // CHUNK,
            partial,
        )[0]

    own_matrix = None
    for first in range(0, own_count - CHUNK, CHUNK):
        own_matrix = assemble_own(first, ghosts, own_matrix)

    def following(first_step, extended, previous, own_matrix):
        factor = 1.0 if first_step else 2.0
        part_b = times(extended, matrix_b)
        sent_b = part_b.astype(jnp.bfloat16)
        got_b = lax.ppermute(sent_b, "slab", pairs_b)
        part_a = times(extended, matrix_a)
        sent_a = part_a.astype(jnp.bfloat16)
        got_a = lax.ppermute(sent_a, "slab", pairs_a)
        if first_step:
            own_matrix = assemble_own(own_count - CHUNK, sent_a, own_matrix)
        own = own_part(first_step, extended, own_matrix, previous[0], (sent_a, sent_b))
        incoming = jnp.concatenate([got_a[:, :face], got_b[:, :face]], axis=1)
        own = own + factor * times(incoming, face_table)

        def ghosts_of(there, part, got, before):
            value = factor * (part[:, :face] + got[:, face:].astype(jnp.float32))
            if not first_step:
                value = value - before.astype(jnp.float32)
            return jnp.where(there, value, 0.0)

        at_a = ghosts_of(has_a, part_a, got_a, previous[1])
        at_b = ghosts_of(has_b, part_b, got_b, previous[2])
        return (own, at_a, at_b), own_matrix

    def extend(own, at_a, at_b):
        return jnp.concatenate([own, at_a, at_b], axis=1).astype(jnp.bfloat16)

    start = join(own_start, ghost_start)
    previous = (start, start[:, own_count : own_count + face], start[:, own_count + face :])
    current, own_matrix = following(True, start, previous, own_matrix)
    for degree_step in range(1, DEGREE):
        later, _ = following(False, extend(*current), previous, own_matrix)
        previous, current = current, later

    filtered = current[0].astype(jnp.bfloat16)
    gram = lax.dot_general(
        filtered, filtered, (((1,), (1,)), ((), ())), preferred_element_type=jnp.float32
    )
    total = sum_over(gram, "slab")
    block = lax.axis_index("orb").astype(jnp.int32).reshape(1)
    return orthonormal(block, total, filtered, orbitals.shape[0], math.sqrt(own_count * slabs))


def solution(mesh):
    in_specs = (P("orb", "slab"), P("slab", None, None), P("slab", None), P("slab"), P("slab"))
    out_specs = P("orb", "slab")
    return jax.shard_map(
        per_device, mesh=mesh, in_specs=in_specs, out_specs=out_specs, check_vma=False
    )
```

```python
import functools
import math

import jax
import jax.numpy as jnp
from jax import lax
from jax.experimental import pallas as pl
from jax.experimental.pallas import tpu as pltpu
from jax.sharding import PartitionSpec as P

DEGREE = 4
LANES = 128
SUBLANES = 8
CHUNK = LANES * SUBLANES
PITCH = SUBLANES + 1


def assemble_kernel(
    places_ref, column_ref, nodes_ref, cells_ref, after_ref, shared_b_ref, shared_a_ref, own_ref,
    total, even_terms, odd_terms, fetched, arrived,
):
    chunk = pl.program_id(0)
    cell = pl.program_id(1)
    cells = pl.num_programs(1)
    cell_nodes = fetched.shape[1]
    ext_count = own_ref.shape[0]
    parts = CHUNK // 256
    part_rows = cell_nodes // parts
    group = 32

    def fetch(index, slot):
        return pltpu.make_async_copy(cells_ref.at[index], fetched.at[slot], arrived.at[slot])

    def spread_part(part, slot):
        columns = column_ref[:, part * 256 : (part + 1) * 256]
        picker = jnp.concatenate(
            [
                (nodes_ref[0] == columns[:, half * LANES : (half + 1) * LANES])
                .astype(jnp.float32)
                .astype(jnp.bfloat16)
                for half in range(2)
            ],
            axis=1,
        )
        return jnp.dot(fetched[slot], picker, preferred_element_type=jnp.float32)

    def keep_part(part, spread, terms):
        for first in range(0, cell_nodes, SUBLANES):
            for half in range(2):
                terms[pl.ds(first * PITCH + 2 * part + half, SUBLANES, stride=PITCH), :] = spread[
                    first : first + SUBLANES, half * LANES : (half + 1) * LANES
                ]

    def add_part(part, of_cell, terms):
        first = part * part_rows
        for start in range(0, part_rows, group):
            places = [places_ref[of_cell * cell_nodes + first + start + k] for k in range(group)]
            sums = [
                total[pl.ds(places[k], SUBLANES), :]
                + terms[pl.ds((first + start + k) * PITCH, SUBLANES), :]
                for k in range(group)
            ]
            for k in range(group):
                total[pl.ds(places[k], SUBLANES), :] = sums[k]

    @pl.when(cell == 0)
    def _():
        @pl.when(chunk == 0)
        def _():
            fetch(0, 0).start()

        fetch(1, 1).start()
        total[...] = jnp.zeros_like(total)
        fetch(0, 0).wait()
        for part in range(parts):
            keep_part(part, spread_part(part, 0), even_terms)

    for parity, (before, now) in enumerate(((odd_terms, even_terms), (even_terms, odd_terms))):

        @pl.when((cell > 0) & (cell % 2 == parity))
        def _():
            @pl.when((cell + 1 < cells) | (chunk + 1 < pl.num_programs(0)))
            def _():
                fetch(lax.rem(cell + 1, cells), 1 - parity).start()

            fetch(cell, parity).wait()
            spread = spread_part(0, parity)
            for part in range(parts):
                following = spread_part(part + 1, parity) if part + 1 < parts else None
                add_part(part, cell - 1, before)
                keep_part(part, spread, now)
                spread = following

        @pl.when((cell == cells - 1) & (cell % 2 == parity))
        def _():
            def body(part, carry):
                add_part(part, cell, now)
                return carry

            lax.fori_loop(0, parts, body, 0)

    def write_out(*out_refs):
        per_out = SUBLANES // len(out_refs)

        def write_rows(step, carry):
            first = pl.multiple_of(step * 16, 16)
            for block in range(SUBLANES):
                upper = total[pl.ds(first * PITCH + block, SUBLANES, stride=PITCH), :]
                lower = total[pl.ds((first + 8) * PITCH + block, SUBLANES, stride=PITCH), :]
                at = block % per_out * LANES
                out_refs[block // per_out][pl.ds(first, 16), at : at + LANES] = jnp.concatenate(
                    [upper, lower], axis=0
                ).astype(jnp.bfloat16)
            return carry

        lax.fori_loop(0, ext_count // 16, write_rows, 0, unroll=8)

    @pl.when((cell == cells - 1) & (chunk == 0))
    def _():
        write_out(shared_b_ref, shared_a_ref)

    @pl.when((cell == cells - 1) & (chunk > 0))
    def _():
        write_out(own_ref)


def assemble(places, columns, nodes, cell_matrices, ext_count, after):
    cells, cell_nodes, _ = cell_matrices.shape
    assert cells % 2 == 0
    count = columns.shape[0]
    chunks = count // CHUNK
    half = pl.BlockSpec((ext_count, CHUNK // 2), lambda q, c, places: (0, 0))
    return pl.pallas_call(
        assemble_kernel,
        out_shape=tuple(
            jax.ShapeDtypeStruct((ext_count, width), jnp.bfloat16)
            for width in (CHUNK // 2, CHUNK // 2, count - CHUNK)
        ),
        grid_spec=pltpu.PrefetchScalarGridSpec(
            num_scalar_prefetch=1,
            grid=(chunks, cells),
            in_specs=[
                pl.BlockSpec((1, CHUNK), lambda q, c, places: (0, q)),
                pl.BlockSpec((1, cell_nodes, LANES), lambda q, c, places: (c, 0, 0)),
                pl.BlockSpec(memory_space=pltpu.HBM),
                pl.BlockSpec(memory_space=pl.ANY),
            ],
            out_specs=(
                half,
                half,
                pl.BlockSpec((ext_count, CHUNK), lambda q, c, places: (0, jnp.maximum(q - 1, 0))),
            ),
            scratch_shapes=[
                pltpu.VMEM((ext_count * PITCH, LANES), jnp.float32),
                pltpu.VMEM((cell_nodes * PITCH, LANES), jnp.float32),
                pltpu.VMEM((cell_nodes * PITCH, LANES), jnp.float32),
                pltpu.VMEM((2, cell_nodes, cell_nodes), jnp.bfloat16),
                pltpu.SemaphoreType.DMA((2,)),
            ],
        ),
        compiler_params=pltpu.CompilerParams(vmem_limit_bytes=42 * 1024 * 1024),
        cost_estimate=pl.CostEstimate(
            flops=16 * cells * cell_nodes * cell_nodes * count,
            bytes_accessed=chunks * cells * cell_nodes * cell_nodes * 2 + ext_count * count * 2,
            transcendentals=0,
        ),
    )(places, columns[None, :], nodes, cell_matrices, after)


def hold_kernel(in_ref, out_ref):
    out_ref[...] = in_ref[...]


def hold(values):
    return pl.pallas_call(
        hold_kernel,
        out_shape=jax.ShapeDtypeStruct(values.shape, values.dtype),
        compiler_params=pltpu.CompilerParams(vmem_limit_bytes=16 * 1024 * 1024),
    )(values)


def own_kernel(first_step, extended_ref, matrix_ref, previous_ref, *refs):
    out_ref = refs[-1]
    width = 256

    def body(step, carry):
        at = pl.ds(pl.multiple_of(step * width, width), width)
        product = jnp.dot(extended_ref[...], matrix_ref[:, at], preferred_element_type=jnp.float32)
        if not first_step:
            product = 2.0 * product - previous_ref[:, at].astype(jnp.float32)
        out_ref[:, at] = product
        return carry

    lax.fori_loop(0, out_ref.shape[1] // width, body, 0)


def own_part(first_step, extended, matrix, previous, after):
    rows, depth = extended.shape
    columns = matrix.shape[1]
    whole = pl.BlockSpec(memory_space=pltpu.VMEM)
    return pl.pallas_call(
        functools.partial(own_kernel, first_step),
        out_shape=jax.ShapeDtypeStruct((rows, columns), jnp.float32),
        in_specs=[whole] * 3 + [pl.BlockSpec(memory_space=pl.ANY)] * len(after),
        out_specs=whole,
        compiler_params=pltpu.CompilerParams(vmem_limit_bytes=16 * 1024 * 1024),
        cost_estimate=pl.CostEstimate(
            flops=8 * rows * depth * columns,
            bytes_accessed=2 * depth * columns + 4 * rows * columns,
            transcendentals=0,
        ),
    )(extended, matrix, previous, *after)


def exact(left, right, contract):
    return lax.dot_general(
        left,
        right,
        (contract, ((), ())),
        precision=lax.Precision.HIGHEST,
        preferred_element_type=jnp.float32,
    )


def inverse_factor(block):
    size = block.shape[0]
    groups = size // SUBLANES
    row = lax.broadcasted_iota(jnp.int32, (SUBLANES, LANES), 0)
    lane = lax.broadcasted_iota(jnp.int32, (SUBLANES, LANES), 1)
    left = [block[g * SUBLANES : (g + 1) * SUBLANES, :] for g in range(groups)]
    right = [(lane == row + g * SUBLANES).astype(jnp.float32) for g in range(groups)]

    def over_rows(values, index):
        return jnp.broadcast_to(values[index : index + 1, :], (SUBLANES, LANES))

    for k in range(groups):
        later = range(k, groups)
        column = {
            g: [
                jnp.broadcast_to(
                    left[g][:, k * SUBLANES + q : k * SUBLANES + q + 1], (SUBLANES, LANES)
                )
                for q in range(SUBLANES)
            ]
            for g in later
        }
        for q in range(SUBLANES):
            scale = lax.rsqrt(over_rows(column[k][q], q))
            factor = {g: column[g][q] * scale for g in later}
            left_row = over_rows(left[k], q) * scale
            right_row = over_rows(right[k], q) * scale
            below = jnp.where(row > q, factor[k], 0.0)
            left[k] = jnp.where(row == q, left_row, left[k] - below * left_row)
            right[k] = jnp.where(row == q, right_row, right[k] - below * right_row)
            for other in range(q + 1, SUBLANES):
                weight = over_rows(factor[k], other)
                for g in later:
                    column[g][other] = column[g][other] - factor[g] * weight
            for g in range(k + 1, groups):
                left[g] = left[g] - factor[g] * left_row
                right[g] = right[g] - factor[g] * right_row
    return jnp.concatenate(right, axis=0)


def orthonormal_kernel(scale, block_ref, gram_ref, filtered_ref, out_ref, inverse):
    size = gram_ref.shape[0]
    count = size // LANES
    at = [slice(i * LANES, (i + 1) * LANES) for i in range(count)]
    lower = {}
    inverses = {}
    for i in range(count):
        diagonal = gram_ref[at[i], at[i]]
        for j in range(i):
            diagonal = diagonal - exact(lower[i, j], lower[i, j], ((1,), (1,)))
        inverses[i, i] = inverse_factor(diagonal)
        for k in range(i + 1, count):
            entry = gram_ref[at[k], at[i]]
            for j in range(i):
                entry = entry - exact(lower[k, j], lower[i, j], ((1,), (1,)))
            lower[k, i] = exact(entry, inverses[i, i], ((1,), (1,)))
    inverse[...] = jnp.zeros_like(inverse)
    for i in range(count):
        for j in range(i):
            entry = exact(lower[i, j], inverses[j, j], ((1,), (0,)))
            for m in range(j + 1, i):
                entry = entry + exact(lower[i, m], inverses[m, j], ((1,), (0,)))
            inverses[i, j] = -exact(inverses[i, i], entry, ((1,), (0,)))
            inverse[at[i], at[j]] = inverses[i, j] * scale
        inverse[at[i], at[i]] = inverses[i, i] * scale
    rows = out_ref.shape[0]
    mine = inverse[pl.ds(pl.multiple_of(block_ref[0] * rows, rows), rows), :]
    high = mine.astype(jnp.bfloat16)
    low = (mine - high.astype(jnp.float32)).astype(jnp.bfloat16)
    width = 512
    for first in range(0, out_ref.shape[1], width):
        part = filtered_ref[:, first : first + width]
        out_ref[:, first : first + width] = jnp.dot(
            high, part, preferred_element_type=jnp.float32
        ) + jnp.dot(low, part, preferred_element_type=jnp.float32)


def orthonormal(block, gram, filtered, rows, scale):
    size = gram.shape[0]
    return pl.pallas_call(
        functools.partial(orthonormal_kernel, scale),
        out_shape=jax.ShapeDtypeStruct((rows, filtered.shape[1]), jnp.float32),
        in_specs=[
            pl.BlockSpec(memory_space=pltpu.SMEM),
            pl.BlockSpec(memory_space=pltpu.VMEM),
            pl.BlockSpec(memory_space=pltpu.VMEM),
        ],
        out_specs=pl.BlockSpec(memory_space=pltpu.VMEM),
        scratch_shapes=[pltpu.VMEM((size, size), jnp.float32)],
        compiler_params=pltpu.CompilerParams(vmem_limit_bytes=16 * 1024 * 1024),
    )(block, gram, filtered)


def swap_pairs(count, first):
    pairs = []
    for low in range(first, count - 1, 2):
        pairs += [(low, low + 1), (low + 1, low)]
    return pairs


def sum_over(values, axis):
    count = lax.axis_size(axis)
    if count & (count - 1):
        return lax.psum(values.astype(jnp.bfloat16), axis).astype(jnp.float32)
    step = 1
    while step < count:
        sent = values.astype(jnp.bfloat16)
        got = lax.ppermute(sent, axis, [(i, i ^ step) for i in range(count)])
        values = sent.astype(jnp.float32) + got.astype(jnp.float32)
        step *= 2
    return values


def per_device(orbitals, cell_matrices, connectivity, face_lower, face_upper):
    own_count = orbitals.shape[1]
    face = face_lower.shape[0]
    ext_count = own_count + 2 * face
    slabs = lax.axis_size("slab")
    slab = lax.axis_index("slab")
    even = slab % 2 == 0

    has_lower = slab > 0
    has_upper = slab < slabs - 1
    has_a = jnp.where(even, has_upper, has_lower)
    has_b = jnp.where(even, has_lower, has_upper)
    ghost_lower = jnp.arange(face, dtype=jnp.int32)
    ghost_upper = ghost_lower + (face + own_count)
    face_a = jnp.where(even, face_upper, face_lower)
    face_b = jnp.where(even, face_lower, face_upper)
    ghost_a = jnp.where(even, ghost_upper, ghost_lower)
    ghost_b = jnp.where(even, ghost_lower, ghost_upper)

    lower_at = jnp.where(even, own_count + face, own_count)
    upper_at = jnp.where(even, own_count, own_count + face)
    places = jnp.where(
        connectivity < face,
        connectivity + lower_at,
        jnp.where(
            connectivity < face + own_count,
            connectivity - face,
            connectivity - (face + own_count) + upper_at,
        ),
    ).reshape(-1) * PITCH
    columns_b = jnp.concatenate([ghost_b, face_b + face])
    columns_a = jnp.concatenate([ghost_a, face_a + face])
    own_columns = jnp.arange(own_count, dtype=jnp.int32) + face
    nodes = jnp.broadcast_to(connectivity[:, :, None], connectivity.shape + (LANES,))

    face_nodes = jnp.concatenate([face_a, face_b])
    face_table = (
        face_nodes[:, None] == lax.broadcasted_iota(jnp.int32, (2 * face, own_count), 1)
    ).astype(jnp.bfloat16)

    pairs_a = swap_pairs(slabs, 0)
    pairs_b = swap_pairs(slabs, 1)

    def times(left, right):
        return jnp.dot(left, right, preferred_element_type=jnp.float32)

    rounded = orbitals.astype(jnp.bfloat16)
    faces = lax.dot_general(
        rounded, face_table, (((1,), (1,)), ((), ())), preferred_element_type=jnp.float32
    ).astype(jnp.bfloat16)
    ghosts_b = lax.ppermute(faces[:, face:], "slab", pairs_b)
    ghosts_a = lax.ppermute(faces[:, :face], "slab", pairs_a)
    mine = jnp.concatenate([rounded, ghosts_a, ghosts_b], axis=1)
    gathered = lax.all_gather(mine, "orb", axis=0, tiled=True)
    matrix_b, matrix_a, own_matrix = assemble(
        places,
        jnp.concatenate([columns_b, columns_a, own_columns]),
        nodes,
        cell_matrices,
        ext_count,
        mine,
    )

    def following(first_step, extended, previous):
        factor = 1.0 if first_step else 2.0
        part_b = times(extended, matrix_b)
        sent_b = part_b.astype(jnp.bfloat16)
        got_b = lax.ppermute(sent_b, "slab", pairs_b)
        part_a = times(extended, matrix_a)
        sent_a = part_a.astype(jnp.bfloat16)
        got_a = lax.ppermute(sent_a, "slab", pairs_a)
        own = own_part(first_step, extended, own_matrix, previous[0], (sent_a, sent_b))
        incoming = jnp.concatenate([got_a[:, :face], got_b[:, :face]], axis=1)
        own = own + factor * times(incoming, face_table)

        def ghosts_of(there, part, got, before):
            value = factor * (part[:, :face] + got[:, face:].astype(jnp.float32))
            if not first_step:
                value = value - before.astype(jnp.float32)
            return jnp.where(there, value, 0.0)

        at_a = ghosts_of(has_a, part_a, got_a, previous[1])
        at_b = ghosts_of(has_b, part_b, got_b, previous[2])
        return own, at_a, at_b

    def extend(own, at_a, at_b):
        return jnp.concatenate([own, at_a, at_b], axis=1).astype(jnp.bfloat16)

    start = hold(gathered)
    previous = (start, start[:, own_count : own_count + face], start[:, own_count + face :])
    current = following(True, start, previous)
    for degree_step in range(1, DEGREE):
        previous, current = current, following(False, extend(*current), previous)

    filtered = current[0].astype(jnp.bfloat16)
    gram = lax.dot_general(
        filtered, filtered, (((1,), (1,)), ((), ())), preferred_element_type=jnp.float32
    )
    total = sum_over(gram, "slab")
    block = lax.axis_index("orb").astype(jnp.int32).reshape(1)
    return orthonormal(block, total, filtered, orbitals.shape[0], math.sqrt(own_count * slabs))


def solution(mesh):
    in_specs = (P("orb", "slab"), P("slab", None, None), P("slab", None), P("slab"), P("slab"))
    out_specs = P("orb", "slab")
    return jax.shard_map(
        per_device, mesh=mesh, in_specs=in_specs, out_specs=out_specs, check_vma=False
    )
```

```python
import functools
import math

import jax
import jax.numpy as jnp
from jax import lax
from jax.experimental import pallas as pl
from jax.experimental.pallas import tpu as pltpu
from jax.sharding import PartitionSpec as P

DEGREE = 4
LANES = 128
SUBLANES = 8
CHUNK = LANES * SUBLANES
PITCH = SUBLANES + 1


def assemble_kernel(
    places_ref, column_ref, nodes_ref, cell_ref, after_ref, shared_b_ref, shared_a_ref, own_ref,
    total, even_terms, odd_terms,
):
    chunk = pl.program_id(0)
    cell = pl.program_id(1)
    cells = pl.num_programs(1)
    cell_nodes = cell_ref.shape[1]
    ext_count = own_ref.shape[0]
    parts = CHUNK // 256
    part_rows = cell_nodes // parts
    group = 32

    def spread_part(part):
        columns = column_ref[:, part * 256 : (part + 1) * 256]
        picker = jnp.concatenate(
            [
                (nodes_ref[0] == columns[:, half * LANES : (half + 1) * LANES])
                .astype(jnp.float32)
                .astype(jnp.bfloat16)
                for half in range(2)
            ],
            axis=1,
        )
        return jnp.dot(cell_ref[0], picker, preferred_element_type=jnp.float32)

    def keep_part(part, spread, terms):
        for first in range(0, cell_nodes, SUBLANES):
            for half in range(2):
                terms[pl.ds(first * PITCH + 2 * part + half, SUBLANES, stride=PITCH), :] = spread[
                    first : first + SUBLANES, half * LANES : (half + 1) * LANES
                ]

    def add_part(part, of_cell, terms):
        first = part * part_rows
        for start in range(0, part_rows, group):
            places = [places_ref[of_cell * cell_nodes + first + start + k] for k in range(group)]
            sums = [
                total[pl.ds(places[k], SUBLANES), :]
                + terms[pl.ds((first + start + k) * PITCH, SUBLANES), :]
                for k in range(group)
            ]
            for k in range(group):
                total[pl.ds(places[k], SUBLANES), :] = sums[k]

    @pl.when(cell == 0)
    def _():
        zero_rows = total.shape[0] // parts
        for part in range(parts):
            spread = spread_part(part)
            total[part * zero_rows : (part + 1) * zero_rows, :] = jnp.zeros(
                (zero_rows, LANES), jnp.float32
            )
            keep_part(part, spread, even_terms)

    for parity, (before, now) in enumerate(((odd_terms, even_terms), (even_terms, odd_terms))):

        @pl.when((cell > 0) & (cell % 2 == parity))
        def _():
            spread = spread_part(0)
            for part in range(parts):
                following = spread_part(part + 1) if part + 1 < parts else None
                add_part(part, cell - 1, before)
                keep_part(part, spread, now)
                spread = following

        @pl.when((cell == cells - 1) & (cell % 2 == parity))
        def _():
            def body(part, carry):
                add_part(part, cell, now)
                return carry

            lax.fori_loop(0, parts, body, 0)

    def write_out(*out_refs):
        per_out = SUBLANES // len(out_refs)

        def write_rows(step, carry):
            first = pl.multiple_of(step * 16, 16)
            for block in range(SUBLANES):
                upper = total[pl.ds(first * PITCH + block, SUBLANES, stride=PITCH), :]
                lower = total[pl.ds((first + 8) * PITCH + block, SUBLANES, stride=PITCH), :]
                at = block % per_out * LANES
                out_refs[block // per_out][pl.ds(first, 16), at : at + LANES] = jnp.concatenate(
                    [upper, lower], axis=0
                ).astype(jnp.bfloat16)
            return carry

        lax.fori_loop(0, ext_count // 16, write_rows, 0, unroll=8)

    @pl.when((cell == cells - 1) & (chunk == 0))
    def _():
        write_out(shared_b_ref, shared_a_ref)

    @pl.when((cell == cells - 1) & (chunk > 0))
    def _():
        write_out(own_ref)


def assemble(places, columns, nodes, cell_matrices, ext_count, after):
    cells, cell_nodes, _ = cell_matrices.shape
    count = columns.shape[0]
    chunks = count // CHUNK
    half = pl.BlockSpec((ext_count, CHUNK // 2), lambda q, c, places: (0, 0))
    return pl.pallas_call(
        assemble_kernel,
        out_shape=tuple(
            jax.ShapeDtypeStruct((ext_count, width), jnp.bfloat16)
            for width in (CHUNK // 2, CHUNK // 2, count - CHUNK)
        ),
        grid_spec=pltpu.PrefetchScalarGridSpec(
            num_scalar_prefetch=1,
            grid=(chunks, cells),
            in_specs=[
                pl.BlockSpec((1, CHUNK), lambda q, c, places: (0, q)),
                pl.BlockSpec((1, cell_nodes, LANES), lambda q, c, places: (c, 0, 0)),
                pl.BlockSpec((1, cell_nodes, cell_nodes), lambda q, c, places: (c, 0, 0)),
                pl.BlockSpec(memory_space=pl.ANY),
            ],
            out_specs=(
                half,
                half,
                pl.BlockSpec((ext_count, CHUNK), lambda q, c, places: (0, jnp.maximum(q - 1, 0))),
            ),
            scratch_shapes=[
                pltpu.VMEM((ext_count * PITCH, LANES), jnp.float32),
                pltpu.VMEM((cell_nodes * PITCH, LANES), jnp.float32),
                pltpu.VMEM((cell_nodes * PITCH, LANES), jnp.float32),
            ],
        ),
        compiler_params=pltpu.CompilerParams(vmem_limit_bytes=57 * 1024 * 1024),
        cost_estimate=pl.CostEstimate(
            flops=16 * cells * cell_nodes * cell_nodes * count,
            bytes_accessed=chunks * cells * cell_nodes * cell_nodes * 2 + ext_count * count * 2,
            transcendentals=0,
        ),
    )(places, columns[None, :], nodes, cell_matrices, after)


def hold_kernel(in_ref, out_ref):
    out_ref[...] = in_ref[...]


def hold(values):
    return pl.pallas_call(
        hold_kernel,
        out_shape=jax.ShapeDtypeStruct(values.shape, values.dtype),
        compiler_params=pltpu.CompilerParams(vmem_limit_bytes=16 * 1024 * 1024),
    )(values)


def own_kernel(first_step, extended_ref, matrix_ref, previous_ref, *refs):
    product = jnp.dot(extended_ref[...], matrix_ref[...], preferred_element_type=jnp.float32)
    if not first_step:
        product = 2.0 * product - previous_ref[...].astype(jnp.float32)
    refs[-1][...] = product


def own_part(first_step, extended, matrix, previous, after):
    rows, depth = extended.shape
    columns = matrix.shape[1]
    width = 256
    return pl.pallas_call(
        functools.partial(own_kernel, first_step),
        out_shape=jax.ShapeDtypeStruct((rows, columns), jnp.float32),
        grid=(columns // width,),
        in_specs=[
            pl.BlockSpec((rows, depth), lambda t: (0, 0)),
            pl.BlockSpec((depth, width), lambda t: (0, t)),
            pl.BlockSpec((rows, width), lambda t: (0, t)),
        ]
        + [pl.BlockSpec(memory_space=pl.ANY)] * len(after),
        out_specs=pl.BlockSpec((rows, width), lambda t: (0, t)),
        compiler_params=pltpu.CompilerParams(vmem_limit_bytes=44 * 1024 * 1024),
        cost_estimate=pl.CostEstimate(
            flops=8 * rows * depth * columns,
            bytes_accessed=2 * depth * columns + 4 * rows * columns,
            transcendentals=0,
        ),
    )(extended, matrix, previous, *after)


def exact(left, right, contract):
    return lax.dot_general(
        left,
        right,
        (contract, ((), ())),
        precision=lax.Precision.HIGHEST,
        preferred_element_type=jnp.float32,
    )


def inverse_factor(block):
    size = block.shape[0]
    groups = size // SUBLANES
    row = lax.broadcasted_iota(jnp.int32, (SUBLANES, LANES), 0)
    lane = lax.broadcasted_iota(jnp.int32, (SUBLANES, LANES), 1)
    left = [block[g * SUBLANES : (g + 1) * SUBLANES, :] for g in range(groups)]
    right = [(lane == row + g * SUBLANES).astype(jnp.float32) for g in range(groups)]

    def over_rows(values, index):
        return jnp.broadcast_to(values[index : index + 1, :], (SUBLANES, LANES))

    for k in range(groups):
        later = range(k, groups)
        column = {
            g: [
                jnp.broadcast_to(
                    left[g][:, k * SUBLANES + q : k * SUBLANES + q + 1], (SUBLANES, LANES)
                )
                for q in range(SUBLANES)
            ]
            for g in later
        }
        for q in range(SUBLANES):
            scale = lax.rsqrt(over_rows(column[k][q], q))
            factor = {g: column[g][q] * scale for g in later}
            left_row = over_rows(left[k], q) * scale
            right_row = over_rows(right[k], q) * scale
            below = jnp.where(row > q, factor[k], 0.0)
            left[k] = jnp.where(row == q, left_row, left[k] - below * left_row)
            right[k] = jnp.where(row == q, right_row, right[k] - below * right_row)
            for other in range(q + 1, SUBLANES):
                weight = over_rows(factor[k], other)
                for g in later:
                    column[g][other] = column[g][other] - factor[g] * weight
            for g in range(k + 1, groups):
                left[g] = left[g] - factor[g] * left_row
                right[g] = right[g] - factor[g] * right_row
    return jnp.concatenate(right, axis=0)


def orthonormal_kernel(scale, block_ref, gram_ref, filtered_ref, out_ref, inverse):
    size = gram_ref.shape[0]
    count = size // LANES
    at = [slice(i * LANES, (i + 1) * LANES) for i in range(count)]
    lower = {}
    inverses = {}
    for i in range(count):
        diagonal = gram_ref[at[i], at[i]]
        for j in range(i):
            diagonal = diagonal - exact(lower[i, j], lower[i, j], ((1,), (1,)))
        inverses[i, i] = inverse_factor(diagonal)
        for k in range(i + 1, count):
            entry = gram_ref[at[k], at[i]]
            for j in range(i):
                entry = entry - exact(lower[k, j], lower[i, j], ((1,), (1,)))
            lower[k, i] = exact(entry, inverses[i, i], ((1,), (1,)))
    inverse[...] = jnp.zeros_like(inverse)
    for i in range(count):
        for j in range(i):
            entry = exact(lower[i, j], inverses[j, j], ((1,), (0,)))
            for m in range(j + 1, i):
                entry = entry + exact(lower[i, m], inverses[m, j], ((1,), (0,)))
            inverses[i, j] = -exact(inverses[i, i], entry, ((1,), (0,)))
            inverse[at[i], at[j]] = inverses[i, j] * scale
        inverse[at[i], at[i]] = inverses[i, i] * scale
    rows = out_ref.shape[0]
    mine = inverse[pl.ds(pl.multiple_of(block_ref[0] * rows, rows), rows), :]
    high = mine.astype(jnp.bfloat16)
    low = (mine - high.astype(jnp.float32)).astype(jnp.bfloat16)
    width = 512
    for first in range(0, out_ref.shape[1], width):
        part = filtered_ref[:, first : first + width]
        out_ref[:, first : first + width] = jnp.dot(
            high, part, preferred_element_type=jnp.float32
        ) + jnp.dot(low, part, preferred_element_type=jnp.float32)


def orthonormal(block, gram, filtered, rows, scale):
    size = gram.shape[0]
    return pl.pallas_call(
        functools.partial(orthonormal_kernel, scale),
        out_shape=jax.ShapeDtypeStruct((rows, filtered.shape[1]), jnp.float32),
        in_specs=[
            pl.BlockSpec(memory_space=pltpu.SMEM),
            pl.BlockSpec(memory_space=pltpu.VMEM),
            pl.BlockSpec(memory_space=pltpu.VMEM),
        ],
        out_specs=pl.BlockSpec(memory_space=pltpu.VMEM),
        scratch_shapes=[pltpu.VMEM((size, size), jnp.float32)],
        compiler_params=pltpu.CompilerParams(vmem_limit_bytes=16 * 1024 * 1024),
    )(block, gram, filtered)


def swap_pairs(count, first):
    pairs = []
    for low in range(first, count - 1, 2):
        pairs += [(low, low + 1), (low + 1, low)]
    return pairs


def sum_over(values, axis):
    count = lax.axis_size(axis)
    if count & (count - 1):
        return lax.psum(values.astype(jnp.bfloat16), axis).astype(jnp.float32)
    step = 1
    while step < count:
        sent = values.astype(jnp.bfloat16)
        got = lax.ppermute(sent, axis, [(i, i ^ step) for i in range(count)])
        values = sent.astype(jnp.float32) + got.astype(jnp.float32)
        step *= 2
    return values


def per_device(orbitals, cell_matrices, connectivity, face_lower, face_upper):
    own_count = orbitals.shape[1]
    face = face_lower.shape[0]
    ext_count = own_count + 2 * face
    slabs = lax.axis_size("slab")
    slab = lax.axis_index("slab")
    even = slab % 2 == 0

    has_lower = slab > 0
    has_upper = slab < slabs - 1
    has_a = jnp.where(even, has_upper, has_lower)
    has_b = jnp.where(even, has_lower, has_upper)
    ghost_lower = jnp.arange(face, dtype=jnp.int32)
    ghost_upper = ghost_lower + (face + own_count)
    face_a = jnp.where(even, face_upper, face_lower)
    face_b = jnp.where(even, face_lower, face_upper)
    ghost_a = jnp.where(even, ghost_upper, ghost_lower)
    ghost_b = jnp.where(even, ghost_lower, ghost_upper)

    lower_at = jnp.where(even, own_count + face, own_count)
    upper_at = jnp.where(even, own_count, own_count + face)
    places = jnp.where(
        connectivity < face,
        connectivity + lower_at,
        jnp.where(
            connectivity < face + own_count,
            connectivity - face,
            connectivity - (face + own_count) + upper_at,
        ),
    ).reshape(-1) * PITCH
    columns_b = jnp.concatenate([ghost_b, face_b + face])
    columns_a = jnp.concatenate([ghost_a, face_a + face])
    own_columns = jnp.arange(own_count, dtype=jnp.int32) + face
    nodes = jnp.broadcast_to(connectivity[:, :, None], connectivity.shape + (LANES,))

    face_nodes = jnp.concatenate([face_a, face_b])
    face_table = (
        face_nodes[:, None] == lax.broadcasted_iota(jnp.int32, (2 * face, own_count), 1)
    ).astype(jnp.bfloat16)

    pairs_a = swap_pairs(slabs, 0)
    pairs_b = swap_pairs(slabs, 1)

    def times(left, right):
        return jnp.dot(left, right, preferred_element_type=jnp.float32)

    rounded = orbitals.astype(jnp.bfloat16)
    faces = lax.dot_general(
        rounded, face_table, (((1,), (1,)), ((), ())), preferred_element_type=jnp.float32
    ).astype(jnp.bfloat16)
    ghosts_b = lax.ppermute(faces[:, face:], "slab", pairs_b)
    ghosts_a = lax.ppermute(faces[:, :face], "slab", pairs_a)
    mine = jnp.concatenate([rounded, ghosts_a, ghosts_b], axis=1)
    gathered = lax.all_gather(mine, "orb", axis=0, tiled=True)
    matrix_b, matrix_a, own_matrix = assemble(
        places,
        jnp.concatenate([columns_b, columns_a, own_columns]),
        nodes,
        cell_matrices,
        ext_count,
        mine,
    )

    def following(step, extended, previous):
        factor = 1.0 if step == 0 else 2.0
        last = step == DEGREE - 1
        part_b = times(extended, matrix_b[:, :face] if last else matrix_b)
        sent_b = part_b.astype(jnp.bfloat16)
        got_b = lax.ppermute(sent_b, "slab", pairs_b)
        part_a = times(extended, matrix_a[:, :face] if last else matrix_a)
        sent_a = part_a.astype(jnp.bfloat16)
        got_a = lax.ppermute(sent_a, "slab", pairs_a)
        own = own_part(step == 0, extended, own_matrix, previous[0], (sent_a, sent_b))
        incoming = jnp.concatenate([got_a[:, :face], got_b[:, :face]], axis=1)
        own = own + factor * times(incoming, face_table)
        if last:
            return (own,)

        def ghosts_of(there, part, got, before):
            value = factor * (part[:, :face] + got[:, face:].astype(jnp.float32))
            if step > 0:
                value = value - before.astype(jnp.float32)
            return jnp.where(there, value, 0.0)

        at_a = ghosts_of(has_a, part_a, got_a, previous[1])
        at_b = ghosts_of(has_b, part_b, got_b, previous[2])
        return own, at_a, at_b

    def extend(own, at_a, at_b):
        return jnp.concatenate([own, at_a, at_b], axis=1).astype(jnp.bfloat16)

    start = hold(gathered)
    previous = (start, start[:, own_count : own_count + face], start[:, own_count + face :])
    current = following(0, start, previous)
    for degree_step in range(1, DEGREE):
        previous, current = current, following(degree_step, extend(*current), previous)

    filtered = current[0].astype(jnp.bfloat16)
    gram = lax.dot_general(
        filtered, filtered, (((1,), (1,)), ((), ())), preferred_element_type=jnp.float32
    )
    total = sum_over(gram, "slab")
    block = lax.axis_index("orb").astype(jnp.int32).reshape(1)
    return orthonormal(block, total, filtered, orbitals.shape[0], math.sqrt(own_count * slabs))


def solution(mesh):
    in_specs = (P("orb", "slab"), P("slab", None, None), P("slab", None), P("slab"), P("slab"))
    out_specs = P("orb", "slab")
    return jax.shard_map(
        per_device, mesh=mesh, in_specs=in_specs, out_specs=out_specs, check_vma=False
    )
```

```python
import functools
import math

import jax
import jax.numpy as jnp
from jax import lax
from jax.experimental import pallas as pl
from jax.experimental.pallas import tpu as pltpu
from jax.sharding import PartitionSpec as P

DEGREE = 4
LANES = 128
SUBLANES = 8
CHUNK = LANES * SUBLANES
PITCH = SUBLANES + 1
TILE = 256


def assemble_kernel(
    places_ref, column_ref, nodes_ref, cell_ref, after_ref, shared_b_ref, shared_a_ref, own_ref,
    total, even_terms, odd_terms, rounded, sent,
):
    chunk = pl.program_id(0)
    chunks = pl.num_programs(0)
    cell = pl.program_id(1)
    cells = pl.num_programs(1)
    cell_nodes = cell_ref.shape[1]
    ext_count = own_ref.shape[1]
    share = rounded.shape[1] // (places_ref.shape[0] // (2 * cell_nodes))
    parts = CHUNK // TILE
    part_rows = cell_nodes // parts
    group = 32
    table = chunk % 2 * (cells * cell_nodes)

    def spread_part(part):
        columns = column_ref[:, part * TILE : (part + 1) * TILE]
        picker = jnp.concatenate(
            [
                (nodes_ref[0] == columns[:, half * LANES : (half + 1) * LANES])
                .astype(jnp.float32)
                .astype(jnp.bfloat16)
                for half in range(2)
            ],
            axis=1,
        )
        return jnp.dot(cell_ref[0], picker, preferred_element_type=jnp.float32)

    def keep_part(part, spread, terms):
        for first in range(0, cell_nodes, SUBLANES):
            for half in range(2):
                terms[pl.ds(first * PITCH + 2 * part + half, SUBLANES, stride=PITCH), :] = spread[
                    first : first + SUBLANES, half * LANES : (half + 1) * LANES
                ]

    def add_part(part, of_cell, terms):
        first = part * part_rows
        for start in range(0, part_rows, group):
            places = [
                places_ref[table + of_cell * cell_nodes + first + start + k] for k in range(group)
            ]
            sums = [
                total[pl.ds(places[k], SUBLANES), :]
                + terms[pl.ds((first + start + k) * PITCH, SUBLANES), :]
                for k in range(group)
            ]
            for k in range(group):
                total[pl.ds(places[k], SUBLANES), :] = sums[k]

    def round_rows(first, which, zero):
        base = (which * ext_count + first) * PITCH
        for block in range(SUBLANES):
            upper = total[pl.ds(base + block, SUBLANES, stride=PITCH), :]
            lower = total[pl.ds(base + SUBLANES * PITCH + block, SUBLANES, stride=PITCH), :]
            rounded[
                block // 2, pl.ds(first, 16), block % 2 * LANES : (block % 2 + 1) * LANES
            ] = jnp.concatenate([upper, lower], axis=0).astype(jnp.bfloat16)
        if zero:
            total[pl.ds(pl.multiple_of(base, SUBLANES), 16 * PITCH), :] = jnp.zeros(
                (16 * PITCH, LANES), jnp.float32
            )

    def round_part(part):
        pieces = share // 16
        for piece in range(part * pieces // parts, (part + 1) * pieces // parts):
            round_rows(pl.multiple_of(cell * share + piece * 16, 16), 1 - chunk % 2, True)

    def sends(index, of_chunk, to_own):
        rows = pl.ds(pl.multiple_of(index * share, 16), share)
        copies = []
        for part in range(parts):
            if to_own:
                target = own_ref.at[(of_chunk - 1) * parts + part, rows]
            else:
                half = (shared_b_ref, shared_a_ref)[part // 2]
                target = half.at[rows, part % 2 * TILE : (part % 2 + 1) * TILE]
            copies.append(
                pltpu.make_async_copy(rounded.at[part, rows], target, sent.at[index, part])
            )
        return copies

    def wait_share(index):
        for copy in sends(index, 1, True):
            copy.wait()

    @pl.when(chunk > 1)
    def _():
        wait_share(cell)

    @pl.when((cell == 0) & (chunk == 0))
    def _():
        def zero(step, carry):
            total[pl.ds(pl.multiple_of(step * 64, 64), 64), :] = jnp.zeros((64, LANES), jnp.float32)
            return carry

        lax.fori_loop(0, ext_count * PITCH // 64, zero, 0, unroll=4)

    @pl.when(cell == 0)
    def _():
        for part in range(parts):
            spread = spread_part(part)
            round_part(part)
            keep_part(part, spread, even_terms)

    for parity, (before, now) in enumerate(((odd_terms, even_terms), (even_terms, odd_terms))):

        @pl.when((cell > 0) & (cell % 2 == parity))
        def _():
            spread = spread_part(0)
            for part in range(parts):
                following = spread_part(part + 1) if part + 1 < parts else None
                add_part(part, cell - 1, before)
                round_part(part)
                keep_part(part, spread, now)
                spread = following

        @pl.when((cell == cells - 1) & (cell % 2 == parity))
        def _():
            def body(part, carry):
                add_part(part, cell, now)
                return carry

            lax.fori_loop(0, parts, body, 0)

    @pl.when(chunk == 1)
    def _():
        for copy in sends(cell, 0, False):
            copy.start()

    @pl.when(chunk > 1)
    def _():
        for copy in sends(cell, chunk - 1, True):
            copy.start()

    @pl.when((cell == cells - 1) & (chunk == chunks - 1))
    def _():
        def last_share(index, carry):
            wait_share(index)

            def last_rows(piece, inner):
                round_rows(pl.multiple_of(index * share + piece * 16, 16), chunk % 2, False)
                return inner

            lax.fori_loop(0, share // 16, last_rows, 0, unroll=4)
            for copy in sends(index, chunk, True):
                copy.start()
            return carry

        lax.fori_loop(0, cells, last_share, 0)

        def settle(index, carry):
            wait_share(index)
            return carry

        lax.fori_loop(0, cells, settle, 0)


def assemble(places, columns, nodes, cell_matrices, ext_count, after):
    cells, cell_nodes, _ = cell_matrices.shape
    count = columns.shape[0]
    chunks = count // CHUNK
    assert chunks > 1 and ext_count % (16 * cells) == 0
    half = jax.ShapeDtypeStruct((ext_count, CHUNK // 2), jnp.bfloat16)
    return pl.pallas_call(
        assemble_kernel,
        out_shape=(
            half,
            half,
            jax.ShapeDtypeStruct(((count - CHUNK) // TILE, ext_count, TILE), jnp.bfloat16),
        ),
        grid_spec=pltpu.PrefetchScalarGridSpec(
            num_scalar_prefetch=1,
            grid=(chunks, cells),
            in_specs=[
                pl.BlockSpec((1, CHUNK), lambda q, c, places: (0, q)),
                pl.BlockSpec((1, cell_nodes, LANES), lambda q, c, places: (c, 0, 0)),
                pl.BlockSpec((1, cell_nodes, cell_nodes), lambda q, c, places: (c, 0, 0)),
                pl.BlockSpec(memory_space=pl.ANY),
            ],
            out_specs=(pl.BlockSpec(memory_space=pl.ANY),) * 3,
            scratch_shapes=[
                pltpu.VMEM((2 * ext_count * PITCH, LANES), jnp.float32),
                pltpu.VMEM((cell_nodes * PITCH, LANES), jnp.float32),
                pltpu.VMEM((cell_nodes * PITCH, LANES), jnp.float32),
                pltpu.VMEM((CHUNK // TILE, ext_count, TILE), jnp.bfloat16),
                pltpu.SemaphoreType.DMA((cells, CHUNK // TILE)),
            ],
        ),
        compiler_params=pltpu.CompilerParams(vmem_limit_bytes=57 * 1024 * 1024),
        cost_estimate=pl.CostEstimate(
            flops=16 * cells * cell_nodes * cell_nodes * count,
            bytes_accessed=chunks * cells * cell_nodes * cell_nodes * 2 + ext_count * count * 2,
            transcendentals=0,
        ),
    )(
        jnp.concatenate([places, places + ext_count * PITCH]),
        columns[None, :],
        nodes,
        cell_matrices,
        after,
    )


def hold_kernel(in_ref, out_ref):
    out_ref[...] = in_ref[...]


def hold(values):
    return pl.pallas_call(
        hold_kernel,
        out_shape=jax.ShapeDtypeStruct(values.shape, values.dtype),
        compiler_params=pltpu.CompilerParams(vmem_limit_bytes=16 * 1024 * 1024),
    )(values)


def own_kernel(first_step, extended_ref, matrix_ref, previous_ref, *refs):
    product = jnp.dot(extended_ref[...], matrix_ref[0], preferred_element_type=jnp.float32)
    if not first_step:
        product = 2.0 * product - previous_ref[...].astype(jnp.float32)
    refs[-1][...] = product


def own_part(first_step, extended, matrix, previous, after):
    rows, depth = extended.shape
    tiles, _, width = matrix.shape
    columns = tiles * width
    return pl.pallas_call(
        functools.partial(own_kernel, first_step),
        out_shape=jax.ShapeDtypeStruct((rows, columns), jnp.float32),
        grid=(tiles,),
        in_specs=[
            pl.BlockSpec((rows, depth), lambda t: (0, 0)),
            pl.BlockSpec((1, depth, width), lambda t: (t, 0, 0)),
            pl.BlockSpec((rows, width), lambda t: (0, t)),
        ]
        + [pl.BlockSpec(memory_space=pl.ANY)] * len(after),
        out_specs=pl.BlockSpec((rows, width), lambda t: (0, t)),
        compiler_params=pltpu.CompilerParams(vmem_limit_bytes=44 * 1024 * 1024),
        cost_estimate=pl.CostEstimate(
            flops=8 * rows * depth * columns,
            bytes_accessed=2 * depth * columns + 4 * rows * columns,
            transcendentals=0,
        ),
    )(extended, matrix, previous, *after)


def exact(left, right, contract):
    return lax.dot_general(
        left,
        right,
        (contract, ((), ())),
        precision=lax.Precision.HIGHEST,
        preferred_element_type=jnp.float32,
    )


def inverse_factor(block):
    size = block.shape[0]
    groups = size // SUBLANES
    row = lax.broadcasted_iota(jnp.int32, (SUBLANES, LANES), 0)
    lane = lax.broadcasted_iota(jnp.int32, (SUBLANES, LANES), 1)
    left = [block[g * SUBLANES : (g + 1) * SUBLANES, :] for g in range(groups)]
    right = [(lane == row + g * SUBLANES).astype(jnp.float32) for g in range(groups)]

    def over_rows(values, index):
        return jnp.broadcast_to(values[index : index + 1, :], (SUBLANES, LANES))

    for k in range(groups):
        later = range(k, groups)
        column = {
            g: [
                jnp.broadcast_to(
                    left[g][:, k * SUBLANES + q : k * SUBLANES + q + 1], (SUBLANES, LANES)
                )
                for q in range(SUBLANES)
            ]
            for g in later
        }
        for q in range(SUBLANES):
            scale = lax.rsqrt(over_rows(column[k][q], q))
            factor = {g: column[g][q] * scale for g in later}
            left_row = over_rows(left[k], q) * scale
            right_row = over_rows(right[k], q) * scale
            below = jnp.where(row > q, factor[k], 0.0)
            left[k] = jnp.where(row == q, left_row, left[k] - below * left_row)
            right[k] = jnp.where(row == q, right_row, right[k] - below * right_row)
            for other in range(q + 1, SUBLANES):
                weight = over_rows(factor[k], other)
                for g in later:
                    column[g][other] = column[g][other] - factor[g] * weight
            for g in range(k + 1, groups):
                left[g] = left[g] - factor[g] * left_row
                right[g] = right[g] - factor[g] * right_row
    return jnp.concatenate(right, axis=0)


def orthonormal_kernel(scale, block_ref, gram_ref, filtered_ref, out_ref, inverse):
    size = gram_ref.shape[0]
    count = size // LANES
    at = [slice(i * LANES, (i + 1) * LANES) for i in range(count)]
    lower = {}
    inverses = {}
    for i in range(count):
        diagonal = gram_ref[at[i], at[i]]
        for j in range(i):
            diagonal = diagonal - exact(lower[i, j], lower[i, j], ((1,), (1,)))
        inverses[i, i] = inverse_factor(diagonal)
        for k in range(i + 1, count):
            entry = gram_ref[at[k], at[i]]
            for j in range(i):
                entry = entry - exact(lower[k, j], lower[i, j], ((1,), (1,)))
            lower[k, i] = exact(entry, inverses[i, i], ((1,), (1,)))
    inverse[...] = jnp.zeros_like(inverse)
    for i in range(count):
        for j in range(i):
            entry = exact(lower[i, j], inverses[j, j], ((1,), (0,)))
            for m in range(j + 1, i):
                entry = entry + exact(lower[i, m], inverses[m, j], ((1,), (0,)))
            inverses[i, j] = -exact(inverses[i, i], entry, ((1,), (0,)))
            inverse[at[i], at[j]] = inverses[i, j] * scale
        inverse[at[i], at[i]] = inverses[i, i] * scale
    rows = out_ref.shape[0]
    mine = inverse[pl.ds(pl.multiple_of(block_ref[0] * rows, rows), rows), :]
    high = mine.astype(jnp.bfloat16)
    low = (mine - high.astype(jnp.float32)).astype(jnp.bfloat16)
    width = 512
    for first in range(0, out_ref.shape[1], width):
        part = filtered_ref[:, first : first + width]
        out_ref[:, first : first + width] = jnp.dot(
            high, part, preferred_element_type=jnp.float32
        ) + jnp.dot(low, part, preferred_element_type=jnp.float32)


def orthonormal(block, gram, filtered, rows, scale):
    size = gram.shape[0]
    return pl.pallas_call(
        functools.partial(orthonormal_kernel, scale),
        out_shape=jax.ShapeDtypeStruct((rows, filtered.shape[1]), jnp.float32),
        in_specs=[
            pl.BlockSpec(memory_space=pltpu.SMEM),
            pl.BlockSpec(memory_space=pltpu.VMEM),
            pl.BlockSpec(memory_space=pltpu.VMEM),
        ],
        out_specs=pl.BlockSpec(memory_space=pltpu.VMEM),
        scratch_shapes=[pltpu.VMEM((size, size), jnp.float32)],
        compiler_params=pltpu.CompilerParams(vmem_limit_bytes=16 * 1024 * 1024),
    )(block, gram, filtered)


def swap_pairs(count, first):
    pairs = []
    for low in range(first, count - 1, 2):
        pairs += [(low, low + 1), (low + 1, low)]
    return pairs


def sum_over(values, axis):
    count = lax.axis_size(axis)
    if count & (count - 1):
        return lax.psum(values.astype(jnp.bfloat16), axis).astype(jnp.float32)
    step = 1
    while step < count:
        sent = values.astype(jnp.bfloat16)
        got = lax.ppermute(sent, axis, [(i, i ^ step) for i in range(count)])
        values = sent.astype(jnp.float32) + got.astype(jnp.float32)
        step *= 2
    return values


def per_device(orbitals, cell_matrices, connectivity, face_lower, face_upper):
    own_count = orbitals.shape[1]
    face = face_lower.shape[0]
    ext_count = own_count + 2 * face
    slabs = lax.axis_size("slab")
    slab = lax.axis_index("slab")
    even = slab % 2 == 0

    has_lower = slab > 0
    has_upper = slab < slabs - 1
    has_a = jnp.where(even, has_upper, has_lower)
    has_b = jnp.where(even, has_lower, has_upper)
    ghost_lower = jnp.arange(face, dtype=jnp.int32)
    ghost_upper = ghost_lower + (face + own_count)
    face_a = jnp.where(even, face_upper, face_lower)
    face_b = jnp.where(even, face_lower, face_upper)
    ghost_a = jnp.where(even, ghost_upper, ghost_lower)
    ghost_b = jnp.where(even, ghost_lower, ghost_upper)

    lower_at = jnp.where(even, own_count + face, own_count)
    upper_at = jnp.where(even, own_count, own_count + face)
    places = jnp.where(
        connectivity < face,
        connectivity + lower_at,
        jnp.where(
            connectivity < face + own_count,
            connectivity - face,
            connectivity - (face + own_count) + upper_at,
        ),
    ).reshape(-1) * PITCH
    columns_b = jnp.concatenate([ghost_b, face_b + face])
    columns_a = jnp.concatenate([ghost_a, face_a + face])
    own_columns = jnp.arange(own_count, dtype=jnp.int32) + face
    nodes = jnp.broadcast_to(connectivity[:, :, None], connectivity.shape + (LANES,))

    face_nodes = jnp.concatenate([face_a, face_b])
    face_table = (
        face_nodes[:, None] == lax.broadcasted_iota(jnp.int32, (2 * face, own_count), 1)
    ).astype(jnp.bfloat16)

    pairs_a = swap_pairs(slabs, 0)
    pairs_b = swap_pairs(slabs, 1)

    def times(left, right):
        return jnp.dot(left, right, preferred_element_type=jnp.float32)

    rounded = orbitals.astype(jnp.bfloat16)
    faces = lax.dot_general(
        rounded, face_table, (((1,), (1,)), ((), ())), preferred_element_type=jnp.float32
    ).astype(jnp.bfloat16)
    ghosts_b = lax.ppermute(faces[:, face:], "slab", pairs_b)
    ghosts_a = lax.ppermute(faces[:, :face], "slab", pairs_a)
    mine = jnp.concatenate([rounded, ghosts_a, ghosts_b], axis=1)
    gathered = lax.all_gather(mine, "orb", axis=0, tiled=True)
    matrix_b, matrix_a, own_matrix = assemble(
        places,
        jnp.concatenate([columns_b, columns_a, own_columns]),
        nodes,
        cell_matrices,
        ext_count,
        mine,
    )

    def following(step, extended, previous):
        factor = 1.0 if step == 0 else 2.0
        last = step == DEGREE - 1
        part_b = times(extended, matrix_b[:, :face] if last else matrix_b)
        sent_b = part_b.astype(jnp.bfloat16)
        got_b = lax.ppermute(sent_b, "slab", pairs_b)
        part_a = times(extended, matrix_a[:, :face] if last else matrix_a)
        sent_a = part_a.astype(jnp.bfloat16)
        got_a = lax.ppermute(sent_a, "slab", pairs_a)
        own = own_part(step == 0, extended, own_matrix, previous[0], (sent_a, sent_b))
        incoming = jnp.concatenate([got_a[:, :face], got_b[:, :face]], axis=1)
        own = own + factor * times(incoming, face_table)
        if last:
            return (own,)

        def ghosts_of(there, part, got, before):
            value = factor * (part[:, :face] + got[:, face:].astype(jnp.float32))
            if step > 0:
                value = value - before.astype(jnp.float32)
            return jnp.where(there, value, 0.0)

        at_a = ghosts_of(has_a, part_a, got_a, previous[1])
        at_b = ghosts_of(has_b, part_b, got_b, previous[2])
        return own, at_a, at_b

    def extend(own, at_a, at_b):
        return jnp.concatenate([own, at_a, at_b], axis=1).astype(jnp.bfloat16)

    start = hold(gathered)
    previous = (start, start[:, own_count : own_count + face], start[:, own_count + face :])
    current = following(0, start, previous)
    for degree_step in range(1, DEGREE):
        previous, current = current, following(degree_step, extend(*current), previous)

    filtered = current[0].astype(jnp.bfloat16)
    gram = lax.dot_general(
        filtered, filtered, (((1,), (1,)), ((), ())), preferred_element_type=jnp.float32
    )
    total = sum_over(gram, "slab")
    block = lax.axis_index("orb").astype(jnp.int32).reshape(1)
    return orthonormal(block, total, filtered, orbitals.shape[0], math.sqrt(own_count * slabs))


def solution(mesh):
    in_specs = (P("orb", "slab"), P("slab", None, None), P("slab", None), P("slab"), P("slab"))
    out_specs = P("orb", "slab")
    return jax.shard_map(
        per_device, mesh=mesh, in_specs=in_specs, out_specs=out_specs, check_vma=False
    )
```

```python
import functools
import math

import jax
import jax.numpy as jnp
from jax import lax
from jax.experimental import pallas as pl
from jax.experimental.pallas import tpu as pltpu
from jax.sharding import PartitionSpec as P

DEGREE = 4
LANES = 128
SUBLANES = 8
CHUNK = LANES * SUBLANES
TILE = 256


def turn(tiles):
    row = lax.broadcasted_iota(jnp.int32, (SUBLANES, LANES), 0)
    tiles = [pltpu.roll(tile, i, 0) if i else tile for i, tile in enumerate(tiles)]
    step = 1
    while step < SUBLANES:
        far = (row & step) != 0
        tiles = [
            jnp.where(far, tiles[(i + step) % SUBLANES], tiles[i]) for i in range(SUBLANES)
        ]
        step *= 2
    tiles = [tiles[-i % SUBLANES] for i in range(SUBLANES)]
    return [
        pltpu.roll(tile, SUBLANES - i, 0) if i else tile for i, tile in enumerate(tiles)
    ]


def assemble_kernel(
    places_ref, column_ref, nodes_ref, cell_ref, after_ref, shared_b_ref, shared_a_ref, own_ref,
    total, even_terms, odd_terms, rounded, sent,
):
    chunk = pl.program_id(0)
    chunks = pl.num_programs(0)
    cell = pl.program_id(1)
    cells = pl.num_programs(1)
    cell_nodes = cell_ref.shape[1]
    ext_count = own_ref.shape[1]
    share = rounded.shape[1] // (places_ref.shape[0] // (2 * cell_nodes))
    parts = CHUNK // TILE
    part_rows = cell_nodes // parts
    group = 32
    table = chunk % 2 * (cells * cell_nodes)

    def spread_part(part):
        columns = column_ref[:, part * TILE : (part + 1) * TILE]
        picker = jnp.concatenate(
            [
                (nodes_ref[0] == columns[:, half * LANES : (half + 1) * LANES])
                .astype(jnp.float32)
                .astype(jnp.bfloat16)
                for half in range(2)
            ],
            axis=1,
        )
        return jnp.dot(cell_ref[0], picker, preferred_element_type=jnp.float32)

    def keep_part(part, spread, terms):
        for half in range(2):
            terms[2 * part + half] = spread[:, half * LANES : (half + 1) * LANES]

    def add_part(part, of_cell, terms):
        first = part * part_rows if isinstance(part, int) else pl.multiple_of(part * part_rows, part_rows)
        for start in range(0, part_rows, group):
            places = [
                pl.multiple_of(
                    places_ref[table + of_cell * cell_nodes + first + start + k], SUBLANES
                )
                for k in range(group)
            ]
            added = []
            for inner in range(0, group, SUBLANES):
                added += turn(
                    [terms[b, pl.ds(first + start + inner, SUBLANES), :] for b in range(SUBLANES)]
                )
            sums = [total[pl.ds(places[k], SUBLANES), :] + added[k] for k in range(group)]
            for k in range(group):
                total[pl.ds(places[k], SUBLANES), :] = sums[k]

    def round_rows(first, which, zero):
        base = pl.multiple_of((which * ext_count + first) * SUBLANES, 16 * SUBLANES)
        upper, lower = (
            turn(
                [
                    total[pl.ds(base + (start + i) * SUBLANES, SUBLANES), :]
                    for i in range(SUBLANES)
                ]
            )
            for start in (0, SUBLANES)
        )
        for block in range(SUBLANES):
            rounded[
                block // 2, pl.ds(first, 16), block % 2 * LANES : (block % 2 + 1) * LANES
            ] = jnp.concatenate([upper[block], lower[block]], axis=0).astype(jnp.bfloat16)
        if zero:
            total[pl.ds(base, 16 * SUBLANES), :] = jnp.zeros((16 * SUBLANES, LANES), jnp.float32)

    def round_part(part):
        pieces = share // 16
        for piece in range(part * pieces // parts, (part + 1) * pieces // parts):
            round_rows(pl.multiple_of(cell * share + piece * 16, 16), 1 - chunk % 2, True)

    def sends(index, of_chunk, to_own):
        rows = pl.ds(pl.multiple_of(index * share, 16), share)
        copies = []
        for part in range(parts):
            if to_own:
                target = own_ref.at[(of_chunk - 1) * parts + part, rows]
            else:
                half = (shared_b_ref, shared_a_ref)[part // 2]
                target = half.at[rows, part % 2 * TILE : (part % 2 + 1) * TILE]
            copies.append(
                pltpu.make_async_copy(rounded.at[part, rows], target, sent.at[index, part])
            )
        return copies

    def wait_share(index):
        for copy in sends(index, 1, True):
            copy.wait()

    @pl.when(chunk > 1)
    def _():
        wait_share(cell)

    @pl.when((cell == 0) & (chunk == 0))
    def _():
        def zero(step, carry):
            total[pl.ds(pl.multiple_of(step * 64, 64), 64), :] = jnp.zeros((64, LANES), jnp.float32)
            return carry

        lax.fori_loop(0, ext_count * SUBLANES // 64, zero, 0, unroll=4)

    @pl.when(cell == 0)
    def _():
        for part in range(parts):
            spread = spread_part(part)
            round_part(part)
            keep_part(part, spread, even_terms)

    for parity, (before, now) in enumerate(((odd_terms, even_terms), (even_terms, odd_terms))):

        @pl.when((cell > 0) & (cell % 2 == parity))
        def _():
            spread = spread_part(0)
            for part in range(parts):
                following = spread_part(part + 1) if part + 1 < parts else None
                add_part(part, cell - 1, before)
                round_part(part)
                keep_part(part, spread, now)
                spread = following

        @pl.when((cell == cells - 1) & (cell % 2 == parity))
        def _():
            def body(part, carry):
                add_part(part, cell, now)
                return carry

            lax.fori_loop(0, parts, body, 0)

    @pl.when(chunk == 1)
    def _():
        for copy in sends(cell, 0, False):
            copy.start()

    @pl.when(chunk > 1)
    def _():
        for copy in sends(cell, chunk - 1, True):
            copy.start()

    @pl.when((cell == cells - 1) & (chunk == chunks - 1))
    def _():
        def last_share(index, carry):
            wait_share(index)

            def last_rows(piece, inner):
                round_rows(pl.multiple_of(index * share + piece * 16, 16), chunk % 2, False)
                return inner

            lax.fori_loop(0, share // 16, last_rows, 0, unroll=4)
            for copy in sends(index, chunk, True):
                copy.start()
            return carry

        lax.fori_loop(0, cells, last_share, 0)

        def settle(index, carry):
            wait_share(index)
            return carry

        lax.fori_loop(0, cells, settle, 0)


def assemble(places, columns, nodes, cell_matrices, ext_count, after):
    cells, cell_nodes, _ = cell_matrices.shape
    count = columns.shape[0]
    chunks = count // CHUNK
    assert chunks > 1 and ext_count % (16 * cells) == 0
    half = jax.ShapeDtypeStruct((ext_count, CHUNK // 2), jnp.bfloat16)
    return pl.pallas_call(
        assemble_kernel,
        out_shape=(
            half,
            half,
            jax.ShapeDtypeStruct(((count - CHUNK) // TILE, ext_count, TILE), jnp.bfloat16),
        ),
        grid_spec=pltpu.PrefetchScalarGridSpec(
            num_scalar_prefetch=1,
            grid=(chunks, cells),
            in_specs=[
                pl.BlockSpec((1, CHUNK), lambda q, c, places: (0, q)),
                pl.BlockSpec((1, cell_nodes, LANES), lambda q, c, places: (c, 0, 0)),
                pl.BlockSpec((1, cell_nodes, cell_nodes), lambda q, c, places: (c, 0, 0)),
                pl.BlockSpec(memory_space=pl.ANY),
            ],
            out_specs=(pl.BlockSpec(memory_space=pl.ANY),) * 3,
            scratch_shapes=[
                pltpu.VMEM((2 * ext_count * SUBLANES, LANES), jnp.float32),
                pltpu.VMEM((SUBLANES, cell_nodes, LANES), jnp.float32),
                pltpu.VMEM((SUBLANES, cell_nodes, LANES), jnp.float32),
                pltpu.VMEM((CHUNK // TILE, ext_count, TILE), jnp.bfloat16),
                pltpu.SemaphoreType.DMA((cells, CHUNK // TILE)),
            ],
        ),
        compiler_params=pltpu.CompilerParams(vmem_limit_bytes=57 * 1024 * 1024),
        cost_estimate=pl.CostEstimate(
            flops=16 * cells * cell_nodes * cell_nodes * count,
            bytes_accessed=chunks * cells * cell_nodes * cell_nodes * 2 + ext_count * count * 2,
            transcendentals=0,
        ),
    )(
        jnp.concatenate([places, places + ext_count * SUBLANES]),
        columns[None, :],
        nodes,
        cell_matrices,
        after,
    )


def hold_kernel(in_ref, out_ref):
    out_ref[...] = in_ref[...]


def hold(values):
    return pl.pallas_call(
        hold_kernel,
        out_shape=jax.ShapeDtypeStruct(values.shape, values.dtype),
        compiler_params=pltpu.CompilerParams(vmem_limit_bytes=16 * 1024 * 1024),
    )(values)


def own_kernel(first_step, extended_ref, matrix_ref, previous_ref, *refs):
    out_ref = refs[-1]

    def body(tile, carry):
        at = pl.ds(pl.multiple_of(tile * TILE, TILE), TILE)
        product = jnp.dot(extended_ref[...], matrix_ref[tile], preferred_element_type=jnp.float32)
        if not first_step:
            product = 2.0 * product - previous_ref[:, at].astype(jnp.float32)
        out_ref[:, at] = product
        return carry

    lax.fori_loop(0, matrix_ref.shape[0], body, 0)


def own_part(first_step, extended, matrix, previous, after):
    rows, depth = extended.shape
    tiles, _, width = matrix.shape
    columns = tiles * width
    whole = pl.BlockSpec(memory_space=pltpu.VMEM)
    return pl.pallas_call(
        functools.partial(own_kernel, first_step),
        out_shape=jax.ShapeDtypeStruct((rows, columns), jnp.float32),
        in_specs=[whole] * 3 + [pl.BlockSpec(memory_space=pl.ANY)] * len(after),
        out_specs=whole,
        compiler_params=pltpu.CompilerParams(vmem_limit_bytes=16 * 1024 * 1024),
        cost_estimate=pl.CostEstimate(
            flops=8 * rows * depth * columns,
            bytes_accessed=2 * depth * columns + 4 * rows * columns,
            transcendentals=0,
        ),
    )(extended, matrix, previous, *after)


def exact(left, right, contract):
    return lax.dot_general(
        left,
        right,
        (contract, ((), ())),
        precision=lax.Precision.HIGHEST,
        preferred_element_type=jnp.float32,
    )


def inverse_factor(block):
    size = block.shape[0]
    groups = size // SUBLANES
    row = lax.broadcasted_iota(jnp.int32, (SUBLANES, LANES), 0)
    lane = lax.broadcasted_iota(jnp.int32, (SUBLANES, LANES), 1)
    left = [block[g * SUBLANES : (g + 1) * SUBLANES, :] for g in range(groups)]
    right = [(lane == row + g * SUBLANES).astype(jnp.float32) for g in range(groups)]

    def over_rows(values, index):
        return jnp.broadcast_to(values[index : index + 1, :], (SUBLANES, LANES))

    for k in range(groups):
        later = range(k, groups)
        column = {
            g: [
                jnp.broadcast_to(
                    left[g][:, k * SUBLANES + q : k * SUBLANES + q + 1], (SUBLANES, LANES)
                )
                for q in range(SUBLANES)
            ]
            for g in later
        }
        for q in range(SUBLANES):
            scale = lax.rsqrt(over_rows(column[k][q], q))
            factor = {g: column[g][q] * scale for g in later}
            left_row = over_rows(left[k], q) * scale
            right_row = over_rows(right[k], q) * scale
            below = jnp.where(row > q, factor[k], 0.0)
            left[k] = jnp.where(row == q, left_row, left[k] - below * left_row)
            right[k] = jnp.where(row == q, right_row, right[k] - below * right_row)
            for other in range(q + 1, SUBLANES):
                weight = over_rows(factor[k], other)
                for g in later:
                    column[g][other] = column[g][other] - factor[g] * weight
            for g in range(k + 1, groups):
                left[g] = left[g] - factor[g] * left_row
                right[g] = right[g] - factor[g] * right_row
    return jnp.concatenate(right, axis=0)


def orthonormal_kernel(scale, block_ref, gram_ref, filtered_ref, out_ref, inverse):
    size = gram_ref.shape[0]
    count = size // LANES
    at = [slice(i * LANES, (i + 1) * LANES) for i in range(count)]
    lower = {}
    inverses = {}
    for i in range(count):
        diagonal = gram_ref[at[i], at[i]]
        for j in range(i):
            diagonal = diagonal - exact(lower[i, j], lower[i, j], ((1,), (1,)))
        inverses[i, i] = inverse_factor(diagonal)
        for k in range(i + 1, count):
            entry = gram_ref[at[k], at[i]]
            for j in range(i):
                entry = entry - exact(lower[k, j], lower[i, j], ((1,), (1,)))
            lower[k, i] = exact(entry, inverses[i, i], ((1,), (1,)))
    inverse[...] = jnp.zeros_like(inverse)
    for i in range(count):
        for j in range(i):
            entry = exact(lower[i, j], inverses[j, j], ((1,), (0,)))
            for m in range(j + 1, i):
                entry = entry + exact(lower[i, m], inverses[m, j], ((1,), (0,)))
            inverses[i, j] = -exact(inverses[i, i], entry, ((1,), (0,)))
            inverse[at[i], at[j]] = inverses[i, j] * scale
        inverse[at[i], at[i]] = inverses[i, i] * scale
    rows = out_ref.shape[0]
    mine = inverse[pl.ds(pl.multiple_of(block_ref[0] * rows, rows), rows), :]
    high = mine.astype(jnp.bfloat16)
    low = (mine - high.astype(jnp.float32)).astype(jnp.bfloat16)
    width = 512
    for first in range(0, out_ref.shape[1], width):
        part = filtered_ref[:, first : first + width]
        out_ref[:, first : first + width] = jnp.dot(
            high, part, preferred_element_type=jnp.float32
        ) + jnp.dot(low, part, preferred_element_type=jnp.float32)


def orthonormal(block, gram, filtered, rows, scale):
    size = gram.shape[0]
    return pl.pallas_call(
        functools.partial(orthonormal_kernel, scale),
        out_shape=jax.ShapeDtypeStruct((rows, filtered.shape[1]), jnp.float32),
        in_specs=[
            pl.BlockSpec(memory_space=pltpu.SMEM),
            pl.BlockSpec(memory_space=pltpu.VMEM),
            pl.BlockSpec(memory_space=pltpu.VMEM),
        ],
        out_specs=pl.BlockSpec(memory_space=pltpu.VMEM),
        scratch_shapes=[pltpu.VMEM((size, size), jnp.float32)],
        compiler_params=pltpu.CompilerParams(vmem_limit_bytes=16 * 1024 * 1024),
    )(block, gram, filtered)


def swap_pairs(count, first):
    pairs = []
    for low in range(first, count - 1, 2):
        pairs += [(low, low + 1), (low + 1, low)]
    return pairs


def sum_over(values, axis):
    count = lax.axis_size(axis)
    if count & (count - 1):
        return lax.psum(values.astype(jnp.bfloat16), axis).astype(jnp.float32)
    step = 1
    while step < count:
        sent = values.astype(jnp.bfloat16)
        got = lax.ppermute(sent, axis, [(i, i ^ step) for i in range(count)])
        values = sent.astype(jnp.float32) + got.astype(jnp.float32)
        step *= 2
    return values


def per_device(orbitals, cell_matrices, connectivity, face_lower, face_upper):
    own_count = orbitals.shape[1]
    face = face_lower.shape[0]
    ext_count = own_count + 2 * face
    slabs = lax.axis_size("slab")
    slab = lax.axis_index("slab")
    even = slab % 2 == 0

    has_lower = slab > 0
    has_upper = slab < slabs - 1
    has_a = jnp.where(even, has_upper, has_lower)
    has_b = jnp.where(even, has_lower, has_upper)
    ghost_lower = jnp.arange(face, dtype=jnp.int32)
    ghost_upper = ghost_lower + (face + own_count)
    face_a = jnp.where(even, face_upper, face_lower)
    face_b = jnp.where(even, face_lower, face_upper)
    ghost_a = jnp.where(even, ghost_upper, ghost_lower)
    ghost_b = jnp.where(even, ghost_lower, ghost_upper)

    lower_at = jnp.where(even, own_count + face, own_count)
    upper_at = jnp.where(even, own_count, own_count + face)
    places = jnp.where(
        connectivity < face,
        connectivity + lower_at,
        jnp.where(
            connectivity < face + own_count,
            connectivity - face,
            connectivity - (face + own_count) + upper_at,
        ),
    ).reshape(-1) * SUBLANES
    columns_b = jnp.concatenate([ghost_b, face_b + face])
    columns_a = jnp.concatenate([ghost_a, face_a + face])
    own_columns = jnp.arange(own_count, dtype=jnp.int32) + face
    nodes = jnp.broadcast_to(connectivity[:, :, None], connectivity.shape + (LANES,))

    face_nodes = jnp.concatenate([face_a, face_b])
    face_table = (
        face_nodes[:, None] == lax.broadcasted_iota(jnp.int32, (2 * face, own_count), 1)
    ).astype(jnp.bfloat16)

    pairs_a = swap_pairs(slabs, 0)
    pairs_b = swap_pairs(slabs, 1)

    def times(left, right):
        return jnp.dot(left, right, preferred_element_type=jnp.float32)

    rounded = orbitals.astype(jnp.bfloat16)
    faces = lax.dot_general(
        rounded, face_table, (((1,), (1,)), ((), ())), preferred_element_type=jnp.float32
    ).astype(jnp.bfloat16)
    ghosts_b = lax.ppermute(faces[:, face:], "slab", pairs_b)
    ghosts_a = lax.ppermute(faces[:, :face], "slab", pairs_a)
    mine = jnp.concatenate([rounded, ghosts_a, ghosts_b], axis=1)
    gathered = lax.all_gather(mine, "orb", axis=0, tiled=True)
    matrix_b, matrix_a, own_matrix = assemble(
        places,
        jnp.concatenate([columns_b, columns_a, own_columns]),
        nodes,
        cell_matrices,
        ext_count,
        mine,
    )

    def following(step, extended, previous):
        factor = 1.0 if step == 0 else 2.0
        last = step == DEGREE - 1
        part_b = times(extended, matrix_b[:, :face] if last else matrix_b)
        sent_b = part_b.astype(jnp.bfloat16)
        got_b = lax.ppermute(sent_b, "slab", pairs_b)
        part_a = times(extended, matrix_a[:, :face] if last else matrix_a)
        sent_a = part_a.astype(jnp.bfloat16)
        got_a = lax.ppermute(sent_a, "slab", pairs_a)
        own = own_part(step == 0, extended, own_matrix, previous[0], (sent_a, sent_b))
        incoming = jnp.concatenate([got_a[:, :face], got_b[:, :face]], axis=1)
        own = own + factor * times(incoming, face_table)
        if last:
            return (own,)

        def ghosts_of(there, part, got, before):
            value = factor * (part[:, :face] + got[:, face:].astype(jnp.float32))
            if step > 0:
                value = value - before.astype(jnp.float32)
            return jnp.where(there, value, 0.0)

        at_a = ghosts_of(has_a, part_a, got_a, previous[1])
        at_b = ghosts_of(has_b, part_b, got_b, previous[2])
        return own, at_a, at_b

    def extend(own, at_a, at_b):
        return jnp.concatenate([own, at_a, at_b], axis=1).astype(jnp.bfloat16)

    start = hold(gathered)
    previous = (start, start[:, own_count : own_count + face], start[:, own_count + face :])
    current = following(0, start, previous)
    for degree_step in range(1, DEGREE):
        previous, current = current, following(degree_step, extend(*current), previous)

    filtered = current[0].astype(jnp.bfloat16)
    gram = lax.dot_general(
        filtered, filtered, (((1,), (1,)), ((), ())), preferred_element_type=jnp.float32
    )
    total = sum_over(gram, "slab")
    block = lax.axis_index("orb").astype(jnp.int32).reshape(1)
    return orthonormal(block, total, filtered, orbitals.shape[0], math.sqrt(own_count * slabs))


def solution(mesh):
    in_specs = (P("orb", "slab"), P("slab", None, None), P("slab", None), P("slab"), P("slab"))
    out_specs = P("orb", "slab")
    return jax.shard_map(
        per_device, mesh=mesh, in_specs=in_specs, out_specs=out_specs, check_vma=False
    )
```

```python
import functools
import math

import jax
import jax.numpy as jnp
from jax import lax
from jax.experimental import pallas as pl
from jax.experimental.pallas import tpu as pltpu
from jax.sharding import PartitionSpec as P

DEGREE = 4
LANES = 128
SUBLANES = 8
CHUNK = LANES * SUBLANES
PITCH = SUBLANES + 1
TILE = 256


def assemble_kernel(
    places_ref, column_ref, nodes_ref, cell_ref, after_ref, shared_b_ref, shared_a_ref, own_ref,
    total, even_terms, odd_terms, rounded, sent,
):
    chunk = pl.program_id(0)
    chunks = pl.num_programs(0)
    cell = pl.program_id(1)
    cells = pl.num_programs(1)
    cell_nodes = cell_ref.shape[1]
    ext_count = own_ref.shape[1]
    share = rounded.shape[1] // (places_ref.shape[0] // (2 * cell_nodes))
    parts = CHUNK // TILE
    part_rows = cell_nodes // parts
    group = 32
    table = chunk % 2 * (cells * cell_nodes)

    def spread_part(part):
        columns = column_ref[:, part * TILE : (part + 1) * TILE]
        picker = jnp.concatenate(
            [
                (nodes_ref[0] == columns[:, half * LANES : (half + 1) * LANES])
                .astype(jnp.float32)
                .astype(jnp.bfloat16)
                for half in range(2)
            ],
            axis=1,
        )
        return jnp.dot(cell_ref[0], picker, preferred_element_type=jnp.float32)

    def keep_part(part, spread, terms):
        for first in range(0, cell_nodes, SUBLANES):
            for half in range(2):
                terms[pl.ds(first * PITCH + 2 * part + half, SUBLANES, stride=PITCH), :] = spread[
                    first : first + SUBLANES, half * LANES : (half + 1) * LANES
                ]

    def add_part(part, of_cell, terms):
        first = part * part_rows
        for start in range(0, part_rows, group):
            places = [
                places_ref[table + of_cell * cell_nodes + first + start + k] for k in range(group)
            ]
            sums = [
                total[pl.ds(places[k], SUBLANES), :]
                + terms[pl.ds((first + start + k) * PITCH, SUBLANES), :]
                for k in range(group)
            ]
            for k in range(group):
                total[pl.ds(places[k], SUBLANES), :] = sums[k]

    def round_rows(first, which, zero):
        base = (which * ext_count + first) * PITCH
        for block in range(SUBLANES):
            upper = total[pl.ds(base + block, SUBLANES, stride=PITCH), :]
            lower = total[pl.ds(base + SUBLANES * PITCH + block, SUBLANES, stride=PITCH), :]
            rounded[
                block // 2, pl.ds(first, 16), block % 2 * LANES : (block % 2 + 1) * LANES
            ] = jnp.concatenate([upper, lower], axis=0).astype(jnp.bfloat16)
        if zero:
            total[pl.ds(pl.multiple_of(base, SUBLANES), 16 * PITCH), :] = jnp.zeros(
                (16 * PITCH, LANES), jnp.float32
            )

    def round_part(part):
        pieces = share // 16
        for piece in range(part * pieces // parts, (part + 1) * pieces // parts):
            round_rows(pl.multiple_of(cell * share + piece * 16, 16), 1 - chunk % 2, True)

    def sends(index, of_chunk, to_own):
        rows = pl.ds(pl.multiple_of(index * share, 16), share)
        copies = []
        for part in range(parts):
            if to_own:
                target = own_ref.at[(of_chunk - 1) * parts + part, rows]
            else:
                half = (shared_b_ref, shared_a_ref)[part // 2]
                target = half.at[rows, part % 2 * TILE : (part % 2 + 1) * TILE]
            copies.append(
                pltpu.make_async_copy(rounded.at[part, rows], target, sent.at[index, part])
            )
        return copies

    def wait_share(index):
        for copy in sends(index, 1, True):
            copy.wait()

    @pl.when(chunk > 1)
    def _():
        wait_share(cell)

    @pl.when((cell == 0) & (chunk == 0))
    def _():
        def zero(step, carry):
            total[pl.ds(pl.multiple_of(step * 64, 64), 64), :] = jnp.zeros((64, LANES), jnp.float32)
            return carry

        lax.fori_loop(0, ext_count * PITCH // 64, zero, 0, unroll=4)

    @pl.when(cell == 0)
    def _():
        for part in range(parts):
            keep_part(part, spread_part(part), even_terms)
            round_part(part)

    for parity, (before, now) in enumerate(((odd_terms, even_terms), (even_terms, odd_terms))):

        @pl.when((cell > 0) & (cell % 2 == parity))
        def _():
            for part in range(parts):
                keep_part(part, spread_part(part), now)
                add_part(part, cell - 1, before)
                round_part(part)

        @pl.when((cell == cells - 1) & (cell % 2 == parity))
        def _():
            def body(part, carry):
                add_part(part, cell, now)
                return carry

            lax.fori_loop(0, parts, body, 0)

    @pl.when(chunk == 1)
    def _():
        for copy in sends(cell, 0, False):
            copy.start()

    @pl.when(chunk > 1)
    def _():
        for copy in sends(cell, chunk - 1, True):
            copy.start()

    @pl.when((cell == cells - 1) & (chunk == chunks - 1))
    def _():
        def last_share(index, carry):
            wait_share(index)

            def last_rows(piece, inner):
                round_rows(pl.multiple_of(index * share + piece * 16, 16), chunk % 2, False)
                return inner

            lax.fori_loop(0, share // 16, last_rows, 0, unroll=4)
            for copy in sends(index, chunk, True):
                copy.start()
            return carry

        lax.fori_loop(0, cells, last_share, 0)

        def settle(index, carry):
            wait_share(index)
            return carry

        lax.fori_loop(0, cells, settle, 0)


def assemble(places, columns, nodes, cell_matrices, ext_count, after):
    cells, cell_nodes, _ = cell_matrices.shape
    count = columns.shape[0]
    chunks = count // CHUNK
    assert chunks > 1 and ext_count % (16 * cells) == 0
    half = jax.ShapeDtypeStruct((ext_count, CHUNK // 2), jnp.bfloat16)
    return pl.pallas_call(
        assemble_kernel,
        out_shape=(
            half,
            half,
            jax.ShapeDtypeStruct(((count - CHUNK) // TILE, ext_count, TILE), jnp.bfloat16),
        ),
        grid_spec=pltpu.PrefetchScalarGridSpec(
            num_scalar_prefetch=1,
            grid=(chunks, cells),
            in_specs=[
                pl.BlockSpec((1, CHUNK), lambda q, c, places: (0, q)),
                pl.BlockSpec((1, cell_nodes, LANES), lambda q, c, places: (c, 0, 0)),
                pl.BlockSpec((1, cell_nodes, cell_nodes), lambda q, c, places: (c, 0, 0)),
                pl.BlockSpec(memory_space=pl.ANY),
            ],
            out_specs=(pl.BlockSpec(memory_space=pl.ANY),) * 3,
            scratch_shapes=[
                pltpu.VMEM((2 * ext_count * PITCH, LANES), jnp.float32),
                pltpu.VMEM((cell_nodes * PITCH, LANES), jnp.float32),
                pltpu.VMEM((cell_nodes * PITCH, LANES), jnp.float32),
                pltpu.VMEM((CHUNK // TILE, ext_count, TILE), jnp.bfloat16),
                pltpu.SemaphoreType.DMA((cells, CHUNK // TILE)),
            ],
        ),
        compiler_params=pltpu.CompilerParams(vmem_limit_bytes=57 * 1024 * 1024),
        cost_estimate=pl.CostEstimate(
            flops=16 * cells * cell_nodes * cell_nodes * count,
            bytes_accessed=chunks * cells * cell_nodes * cell_nodes * 2 + ext_count * count * 2,
            transcendentals=0,
        ),
    )(
        jnp.concatenate([places, places + ext_count * PITCH]),
        columns[None, :],
        nodes,
        cell_matrices,
        after,
    )


def hold_kernel(in_ref, out_ref):
    out_ref[...] = in_ref[...]


def hold(values):
    return pl.pallas_call(
        hold_kernel,
        out_shape=jax.ShapeDtypeStruct(values.shape, values.dtype),
        compiler_params=pltpu.CompilerParams(vmem_limit_bytes=16 * 1024 * 1024),
    )(values)


def arrived(got_a_ref, got_b_ref, table_ref, at):
    incoming = jnp.concatenate(
        [ref[:, : table_ref.shape[0] // 2] for ref in (got_a_ref, got_b_ref)], axis=1
    )
    return jnp.dot(incoming, table_ref[:, at], preferred_element_type=jnp.float32)


def own_kernel(step, extended_ref, matrix_ref, *refs):
    out_ref = refs[-1]

    def body(tile, carry):
        at = pl.ds(pl.multiple_of(tile * TILE, TILE), TILE)
        product = jnp.dot(extended_ref[...], matrix_ref[tile], preferred_element_type=jnp.float32)
        if step == 1:
            product = 2.0 * product - refs[0][:, at].astype(jnp.float32)
        if step > 1:
            factor = 1.0 if step == 2 else 2.0
            product = 2.0 * product - (refs[0][:, at] + factor * arrived(*refs[1:4], at))
        out_ref[:, at] = product
        return carry

    lax.fori_loop(0, matrix_ref.shape[0], body, 0)


def own_part(step, extended, matrix, before, after):
    rows, depth = extended.shape
    tiles, _, width = matrix.shape
    columns = tiles * width
    whole = pl.BlockSpec(memory_space=pltpu.VMEM)
    operands = (extended, matrix) + before
    return pl.pallas_call(
        functools.partial(own_kernel, step),
        out_shape=jax.ShapeDtypeStruct((rows, columns), jnp.float32),
        in_specs=[whole] * len(operands) + [pl.BlockSpec(memory_space=pl.ANY)] * len(after),
        out_specs=whole,
        compiler_params=pltpu.CompilerParams(vmem_limit_bytes=16 * 1024 * 1024),
        cost_estimate=pl.CostEstimate(
            flops=8 * rows * depth * columns,
            bytes_accessed=2 * depth * columns + 4 * rows * columns,
            transcendentals=0,
        ),
    )(*operands, *after)


def combine_kernel(step, there_ref, own_ref, got_a_ref, got_b_ref, table_ref, *refs):
    factor = 1.0 if step == 0 else 2.0
    columns, face = own_ref.shape[1], table_ref.shape[0] // 2
    ghosts_ref = refs[-1]
    field_ref = refs[-2] if len(refs) > 1 else refs[-1]
    for first in range(0, columns, TILE):
        at = slice(first, first + TILE)
        field_ref[:, at] = (
            own_ref[:, at] + factor * arrived(got_a_ref, got_b_ref, table_ref, at)
        ).astype(jnp.bfloat16)
    if len(refs) == 1:
        return
    for side, got_ref in enumerate((got_a_ref, got_b_ref)):
        at = slice(side * face, (side + 1) * face)
        value = factor * (refs[side][:, :face] + got_ref[:, face:].astype(jnp.float32))
        if step > 0:
            value = value - refs[2][:, at].astype(jnp.float32)
        value = jnp.where(there_ref[side] != 0, value, 0.0)
        ghosts_ref[:, at] = value
        field_ref[:, columns + side * face : columns + (side + 1) * face] = value.astype(jnp.bfloat16)


def combine(step, there, own, got_a, got_b, table, ghost_operands):
    rows, columns = own.shape
    whole = pl.BlockSpec(memory_space=pltpu.VMEM)
    face = table.shape[0] // 2
    if ghost_operands:
        out_shape = (
            jax.ShapeDtypeStruct((rows, columns + 2 * face), jnp.bfloat16),
            jax.ShapeDtypeStruct((rows, 2 * face), jnp.float32),
        )
    else:
        out_shape = (jax.ShapeDtypeStruct((rows, columns), jnp.bfloat16),)
    return pl.pallas_call(
        functools.partial(combine_kernel, step),
        out_shape=out_shape,
        in_specs=[pl.BlockSpec(memory_space=pltpu.SMEM)] + [whole] * (4 + len(ghost_operands)),
        out_specs=(whole,) * len(out_shape),
        compiler_params=pltpu.CompilerParams(vmem_limit_bytes=16 * 1024 * 1024),
    )(there, own, got_a, got_b, table, *ghost_operands)


def exact(left, right, contract):
    return lax.dot_general(
        left,
        right,
        (contract, ((), ())),
        precision=lax.Precision.HIGHEST,
        preferred_element_type=jnp.float32,
    )


def inverse_factor(block):
    size = block.shape[0]
    groups = size // SUBLANES
    row = lax.broadcasted_iota(jnp.int32, (SUBLANES, LANES), 0)
    lane = lax.broadcasted_iota(jnp.int32, (SUBLANES, LANES), 1)
    left = [block[g * SUBLANES : (g + 1) * SUBLANES, :] for g in range(groups)]
    right = [(lane == row + g * SUBLANES).astype(jnp.float32) for g in range(groups)]

    def over_rows(values, index):
        return jnp.broadcast_to(values[index : index + 1, :], (SUBLANES, LANES))

    for k in range(groups):
        later = range(k, groups)
        column = {
            g: [
                jnp.broadcast_to(
                    left[g][:, k * SUBLANES + q : k * SUBLANES + q + 1], (SUBLANES, LANES)
                )
                for q in range(SUBLANES)
            ]
            for g in later
        }
        for q in range(SUBLANES):
            scale = lax.rsqrt(over_rows(column[k][q], q))
            factor = {g: column[g][q] * scale for g in later}
            left_row = over_rows(left[k], q) * scale
            right_row = over_rows(right[k], q) * scale
            below = jnp.where(row > q, factor[k], 0.0)
            left[k] = jnp.where(row == q, left_row, left[k] - below * left_row)
            right[k] = jnp.where(row == q, right_row, right[k] - below * right_row)
            for other in range(q + 1, SUBLANES):
                weight = over_rows(factor[k], other)
                for g in later:
                    column[g][other] = column[g][other] - factor[g] * weight
            for g in range(k + 1, groups):
                left[g] = left[g] - factor[g] * left_row
                right[g] = right[g] - factor[g] * right_row
    return jnp.concatenate(right, axis=0)


def orthonormal_kernel(scale, block_ref, gram_ref, filtered_ref, out_ref, inverse):
    size = gram_ref.shape[0]
    count = size // LANES
    at = [slice(i * LANES, (i + 1) * LANES) for i in range(count)]
    lower = {}
    inverses = {}
    for i in range(count):
        diagonal = gram_ref[at[i], at[i]]
        for j in range(i):
            diagonal = diagonal - exact(lower[i, j], lower[i, j], ((1,), (1,)))
        inverses[i, i] = inverse_factor(diagonal)
        for k in range(i + 1, count):
            entry = gram_ref[at[k], at[i]]
            for j in range(i):
                entry = entry - exact(lower[k, j], lower[i, j], ((1,), (1,)))
            lower[k, i] = exact(entry, inverses[i, i], ((1,), (1,)))
    inverse[...] = jnp.zeros_like(inverse)
    for i in range(count):
        for j in range(i):
            entry = exact(lower[i, j], inverses[j, j], ((1,), (0,)))
            for m in range(j + 1, i):
                entry = entry + exact(lower[i, m], inverses[m, j], ((1,), (0,)))
            inverses[i, j] = -exact(inverses[i, i], entry, ((1,), (0,)))
            inverse[at[i], at[j]] = inverses[i, j] * scale
        inverse[at[i], at[i]] = inverses[i, i] * scale
    rows = out_ref.shape[0]
    mine = inverse[pl.ds(pl.multiple_of(block_ref[0] * rows, rows), rows), :]
    high = mine.astype(jnp.bfloat16)
    low = (mine - high.astype(jnp.float32)).astype(jnp.bfloat16)
    width = 512
    for first in range(0, out_ref.shape[1], width):
        part = filtered_ref[:, first : first + width]
        out_ref[:, first : first + width] = jnp.dot(
            high, part, preferred_element_type=jnp.float32
        ) + jnp.dot(low, part, preferred_element_type=jnp.float32)


def orthonormal(block, gram, filtered, rows, scale):
    size = gram.shape[0]
    return pl.pallas_call(
        functools.partial(orthonormal_kernel, scale),
        out_shape=jax.ShapeDtypeStruct((rows, filtered.shape[1]), jnp.float32),
        in_specs=[
            pl.BlockSpec(memory_space=pltpu.SMEM),
            pl.BlockSpec(memory_space=pltpu.VMEM),
            pl.BlockSpec(memory_space=pltpu.VMEM),
        ],
        out_specs=pl.BlockSpec(memory_space=pltpu.VMEM),
        scratch_shapes=[pltpu.VMEM((size, size), jnp.float32)],
        compiler_params=pltpu.CompilerParams(vmem_limit_bytes=16 * 1024 * 1024),
    )(block, gram, filtered)


def swap_pairs(count, first):
    pairs = []
    for low in range(first, count - 1, 2):
        pairs += [(low, low + 1), (low + 1, low)]
    return pairs


def sum_over(values, axis):
    count = lax.axis_size(axis)
    if count & (count - 1):
        return lax.psum(values.astype(jnp.bfloat16), axis).astype(jnp.float32)
    step = 1
    while step < count:
        sent = values.astype(jnp.bfloat16)
        got = lax.ppermute(sent, axis, [(i, i ^ step) for i in range(count)])
        values = sent.astype(jnp.float32) + got.astype(jnp.float32)
        step *= 2
    return values


def per_device(orbitals, cell_matrices, connectivity, face_lower, face_upper):
    own_count = orbitals.shape[1]
    face = face_lower.shape[0]
    ext_count = own_count + 2 * face
    slabs = lax.axis_size("slab")
    slab = lax.axis_index("slab")
    even = slab % 2 == 0

    has_lower = slab > 0
    has_upper = slab < slabs - 1
    has_a = jnp.where(even, has_upper, has_lower)
    has_b = jnp.where(even, has_lower, has_upper)
    ghost_lower = jnp.arange(face, dtype=jnp.int32)
    ghost_upper = ghost_lower + (face + own_count)
    face_a = jnp.where(even, face_upper, face_lower)
    face_b = jnp.where(even, face_lower, face_upper)
    ghost_a = jnp.where(even, ghost_upper, ghost_lower)
    ghost_b = jnp.where(even, ghost_lower, ghost_upper)

    lower_at = jnp.where(even, own_count + face, own_count)
    upper_at = jnp.where(even, own_count, own_count + face)
    places = jnp.where(
        connectivity < face,
        connectivity + lower_at,
        jnp.where(
            connectivity < face + own_count,
            connectivity - face,
            connectivity - (face + own_count) + upper_at,
        ),
    ).reshape(-1) * PITCH
    columns_b = jnp.concatenate([ghost_b, face_b + face])
    columns_a = jnp.concatenate([ghost_a, face_a + face])
    own_columns = jnp.arange(own_count, dtype=jnp.int32) + face
    nodes = jnp.broadcast_to(connectivity[:, :, None], connectivity.shape + (LANES,))

    face_nodes = jnp.concatenate([face_a, face_b])
    face_table = (
        face_nodes[:, None] == lax.broadcasted_iota(jnp.int32, (2 * face, own_count), 1)
    ).astype(jnp.bfloat16)

    pairs_a = swap_pairs(slabs, 0)
    pairs_b = swap_pairs(slabs, 1)

    def times(left, right):
        return jnp.dot(left, right, preferred_element_type=jnp.float32)

    rounded = orbitals.astype(jnp.bfloat16)
    faces = lax.dot_general(
        rounded, face_table, (((1,), (1,)), ((), ())), preferred_element_type=jnp.float32
    ).astype(jnp.bfloat16)
    ghosts_b = lax.ppermute(faces[:, face:], "slab", pairs_b)
    ghosts_a = lax.ppermute(faces[:, :face], "slab", pairs_a)
    mine = jnp.concatenate([rounded, ghosts_a, ghosts_b], axis=1)
    gathered = lax.all_gather(mine, "orb", axis=0, tiled=True)
    matrix_b, matrix_a, own_matrix = assemble(
        places,
        jnp.concatenate([columns_b, columns_a, own_columns]),
        nodes,
        cell_matrices,
        ext_count,
        mine,
    )

    there = jnp.stack([has_a, has_b]).astype(jnp.int32)
    field = hold(gathered)
    ghosts = [field[:, own_count:]]
    before = ()
    for step in range(DEGREE):
        last = step == DEGREE - 1
        part_b = times(field, matrix_b[:, :face] if last else matrix_b)
        sent_b = part_b.astype(jnp.bfloat16)
        got_b = lax.ppermute(sent_b, "slab", pairs_b)
        part_a = times(field, matrix_a[:, :face] if last else matrix_a)
        sent_a = part_a.astype(jnp.bfloat16)
        got_a = lax.ppermute(sent_a, "slab", pairs_a)
        own = own_part(step, field, own_matrix, before, (sent_a, sent_b))
        if step == 0:
            before = (field,)
        else:
            before = arrivals
        arrivals = (own, got_a, got_b, face_table)
        if last:
            (filtered,) = combine(step, there, own, got_a, got_b, face_table, ())
        else:
            operands = (part_a, part_b) + ((ghosts[-2],) if step else ())
            field, new_ghosts = combine(step, there, own, got_a, got_b, face_table, operands)
            ghosts.append(new_ghosts)

    gram = lax.dot_general(
        filtered, filtered, (((1,), (1,)), ((), ())), preferred_element_type=jnp.float32
    )
    total = sum_over(gram, "slab")
    block = lax.axis_index("orb").astype(jnp.int32).reshape(1)
    return orthonormal(block, total, filtered, orbitals.shape[0], math.sqrt(own_count * slabs))


def solution(mesh):
    in_specs = (P("orb", "slab"), P("slab", None, None), P("slab", None), P("slab"), P("slab"))
    out_specs = P("orb", "slab")
    return jax.shard_map(
        per_device, mesh=mesh, in_specs=in_specs, out_specs=out_specs, check_vma=False
    )
```

```python
import functools
import math

import jax
import jax.numpy as jnp
from jax import lax
from jax.experimental import pallas as pl
from jax.experimental.pallas import tpu as pltpu
from jax.sharding import PartitionSpec as P

DEGREE = 4
LANES = 128
SUBLANES = 8
CHUNK = LANES * SUBLANES
PITCH = SUBLANES + 1
TILE = 256


def turn(tiles):
    row = lax.broadcasted_iota(jnp.int32, (SUBLANES, LANES), 0)
    tiles = [pltpu.roll(tile, i, 0) if i else tile for i, tile in enumerate(tiles)]
    step = 1
    while step < SUBLANES:
        far = (row & step) != 0
        tiles = [
            jnp.where(far, tiles[(i + step) % SUBLANES], tiles[i]) for i in range(SUBLANES)
        ]
        step *= 2
    tiles = [tiles[-i % SUBLANES] for i in range(SUBLANES)]
    return [
        pltpu.roll(tile, SUBLANES - i, 0) if i else tile for i, tile in enumerate(tiles)
    ]


def assemble_kernel(
    places_ref, column_ref, nodes_ref, cell_ref, after_ref, shared_b_ref, shared_a_ref, own_ref,
    total, even_terms, odd_terms, rounded, sent,
):
    chunk = pl.program_id(0)
    chunks = pl.num_programs(0)
    cell = pl.program_id(1)
    cells = pl.num_programs(1)
    cell_nodes = cell_ref.shape[1]
    ext_count = own_ref.shape[1]
    share = rounded.shape[1] // (places_ref.shape[0] // (2 * cell_nodes))
    parts = CHUNK // TILE
    part_rows = cell_nodes // parts
    group = 32
    table = chunk % 2 * (cells * cell_nodes)

    def spread_part(part):
        columns = column_ref[:, part * TILE : (part + 1) * TILE]
        picker = jnp.concatenate(
            [
                (nodes_ref[0] == columns[:, half * LANES : (half + 1) * LANES])
                .astype(jnp.float32)
                .astype(jnp.bfloat16)
                for half in range(2)
            ],
            axis=1,
        )
        return jnp.dot(cell_ref[0], picker, preferred_element_type=jnp.float32)

    def keep_part(part, spread, terms):
        for first in range(0, cell_nodes, SUBLANES):
            for half in range(2):
                terms[pl.ds(first * PITCH + 2 * part + half, SUBLANES, stride=PITCH), :] = spread[
                    first : first + SUBLANES, half * LANES : (half + 1) * LANES
                ]

    def add_part(part, of_cell, terms):
        first = part * part_rows
        for start in range(0, part_rows, group):
            places = [
                pl.multiple_of(
                    places_ref[table + of_cell * cell_nodes + first + start + k], SUBLANES
                )
                for k in range(group)
            ]
            sums = [
                total[pl.ds(places[k], SUBLANES), :]
                + terms[pl.ds((first + start + k) * PITCH, SUBLANES), :]
                for k in range(group)
            ]
            for k in range(group):
                total[pl.ds(places[k], SUBLANES), :] = sums[k]

    def round_rows(first, which, zero):
        base = pl.multiple_of((which * ext_count + first) * SUBLANES, 16 * SUBLANES)
        upper, lower = (
            turn(
                [
                    total[pl.ds(base + (start + i) * SUBLANES, SUBLANES), :]
                    for i in range(SUBLANES)
                ]
            )
            for start in (0, SUBLANES)
        )
        for block in range(SUBLANES):
            rounded[
                block // 2, pl.ds(first, 16), block % 2 * LANES : (block % 2 + 1) * LANES
            ] = jnp.concatenate([upper[block], lower[block]], axis=0).astype(jnp.bfloat16)
        if zero:
            total[pl.ds(base, 16 * SUBLANES), :] = jnp.zeros((16 * SUBLANES, LANES), jnp.float32)

    def round_part(part):
        pieces = share // 16
        for piece in range(part * pieces // parts, (part + 1) * pieces // parts):
            round_rows(pl.multiple_of(cell * share + piece * 16, 16), 1 - chunk % 2, True)

    def sends(index, of_chunk, to_own):
        rows = pl.ds(pl.multiple_of(index * share, 16), share)
        copies = []
        for part in range(parts):
            if to_own:
                target = own_ref.at[(of_chunk - 1) * parts + part, rows]
            else:
                half = (shared_b_ref, shared_a_ref)[part // 2]
                target = half.at[rows, part % 2 * TILE : (part % 2 + 1) * TILE]
            copies.append(
                pltpu.make_async_copy(rounded.at[part, rows], target, sent.at[index, part])
            )
        return copies

    def wait_share(index):
        for copy in sends(index, 1, True):
            copy.wait()

    @pl.when(chunk > 1)
    def _():
        wait_share(cell)

    @pl.when((cell == 0) & (chunk == 0))
    def _():
        def zero(step, carry):
            total[pl.ds(pl.multiple_of(step * 64, 64), 64), :] = jnp.zeros((64, LANES), jnp.float32)
            return carry

        lax.fori_loop(0, ext_count * SUBLANES // 64, zero, 0, unroll=4)

    @pl.when(cell == 0)
    def _():
        for part in range(parts):
            keep_part(part, spread_part(part), even_terms)
            round_part(part)

    for parity, (before, now) in enumerate(((odd_terms, even_terms), (even_terms, odd_terms))):

        @pl.when((cell > 0) & (cell % 2 == parity))
        def _():
            for part in range(parts):
                keep_part(part, spread_part(part), now)
                add_part(part, cell - 1, before)
                round_part(part)

        @pl.when((cell == cells - 1) & (cell % 2 == parity))
        def _():
            def body(part, carry):
                add_part(part, cell, now)
                return carry

            lax.fori_loop(0, parts, body, 0)

    @pl.when(chunk == 1)
    def _():
        for copy in sends(cell, 0, False):
            copy.start()

    @pl.when(chunk > 1)
    def _():
        for copy in sends(cell, chunk - 1, True):
            copy.start()

    @pl.when((cell == cells - 1) & (chunk == chunks - 1))
    def _():
        def last_share(index, carry):
            wait_share(index)

            def last_rows(piece, inner):
                round_rows(pl.multiple_of(index * share + piece * 16, 16), chunk % 2, False)
                return inner

            lax.fori_loop(0, share // 16, last_rows, 0, unroll=4)
            for copy in sends(index, chunk, True):
                copy.start()
            return carry

        lax.fori_loop(0, cells, last_share, 0)

        def settle(index, carry):
            wait_share(index)
            return carry

        lax.fori_loop(0, cells, settle, 0)


def assemble(places, columns, nodes, cell_matrices, ext_count, after):
    cells, cell_nodes, _ = cell_matrices.shape
    count = columns.shape[0]
    chunks = count // CHUNK
    assert chunks > 1 and ext_count % (16 * cells) == 0
    half = jax.ShapeDtypeStruct((ext_count, CHUNK // 2), jnp.bfloat16)
    return pl.pallas_call(
        assemble_kernel,
        out_shape=(
            half,
            half,
            jax.ShapeDtypeStruct(((count - CHUNK) // TILE, ext_count, TILE), jnp.bfloat16),
        ),
        grid_spec=pltpu.PrefetchScalarGridSpec(
            num_scalar_prefetch=1,
            grid=(chunks, cells),
            in_specs=[
                pl.BlockSpec((1, CHUNK), lambda q, c, places: (0, q)),
                pl.BlockSpec((1, cell_nodes, LANES), lambda q, c, places: (c, 0, 0)),
                pl.BlockSpec((1, cell_nodes, cell_nodes), lambda q, c, places: (c, 0, 0)),
                pl.BlockSpec(memory_space=pl.ANY),
            ],
            out_specs=(pl.BlockSpec(memory_space=pl.ANY),) * 3,
            scratch_shapes=[
                pltpu.VMEM((2 * ext_count * SUBLANES, LANES), jnp.float32),
                pltpu.VMEM((cell_nodes * PITCH, LANES), jnp.float32),
                pltpu.VMEM((cell_nodes * PITCH, LANES), jnp.float32),
                pltpu.VMEM((CHUNK // TILE, ext_count, TILE), jnp.bfloat16),
                pltpu.SemaphoreType.DMA((cells, CHUNK // TILE)),
            ],
        ),
        compiler_params=pltpu.CompilerParams(vmem_limit_bytes=38 * 1024 * 1024),
        cost_estimate=pl.CostEstimate(
            flops=16 * cells * cell_nodes * cell_nodes * count,
            bytes_accessed=chunks * cells * cell_nodes * cell_nodes * 2 + ext_count * count * 2,
            transcendentals=0,
        ),
    )(
        jnp.concatenate([places, places + ext_count * SUBLANES]),
        columns[None, :],
        nodes,
        cell_matrices,
        after,
    )


def hold_kernel(in_ref, out_ref):
    out_ref[...] = in_ref[...]


def hold(values):
    return pl.pallas_call(
        hold_kernel,
        out_shape=jax.ShapeDtypeStruct(values.shape, values.dtype),
        compiler_params=pltpu.CompilerParams(vmem_limit_bytes=16 * 1024 * 1024),
    )(values)


def arrived(got_a_ref, got_b_ref, table_ref, at):
    incoming = jnp.concatenate(
        [ref[:, : table_ref.shape[0] // 2] for ref in (got_a_ref, got_b_ref)], axis=1
    )
    return jnp.dot(incoming, table_ref[:, at], preferred_element_type=jnp.float32)


def own_kernel(step, extended_ref, matrix_ref, *refs):
    out_ref = refs[-1]

    def body(tile, carry):
        at = pl.ds(pl.multiple_of(tile * TILE, TILE), TILE)
        product = jnp.dot(extended_ref[...], matrix_ref[tile], preferred_element_type=jnp.float32)
        if step == 1:
            product = 2.0 * product - refs[0][:, at].astype(jnp.float32)
        if step > 1:
            factor = 1.0 if step == 2 else 2.0
            product = 2.0 * product - (refs[0][:, at] + factor * arrived(*refs[1:4], at))
        out_ref[:, at] = product
        return carry

    lax.fori_loop(0, matrix_ref.shape[0], body, 0, unroll=4)


def own_part(step, extended, matrix, before, after):
    rows, depth = extended.shape
    tiles, _, width = matrix.shape
    columns = tiles * width
    whole = pl.BlockSpec(memory_space=pltpu.VMEM)
    operands = (extended, matrix) + before
    return pl.pallas_call(
        functools.partial(own_kernel, step),
        out_shape=jax.ShapeDtypeStruct((rows, columns), jnp.float32),
        in_specs=[whole] * len(operands) + [pl.BlockSpec(memory_space=pl.ANY)] * len(after),
        out_specs=whole,
        compiler_params=pltpu.CompilerParams(vmem_limit_bytes=16 * 1024 * 1024),
        cost_estimate=pl.CostEstimate(
            flops=8 * rows * depth * columns,
            bytes_accessed=2 * depth * columns + 4 * rows * columns,
            transcendentals=0,
        ),
    )(*operands, *after)


def combine_kernel(step, there_ref, own_ref, got_a_ref, got_b_ref, table_ref, *refs):
    factor = 1.0 if step == 0 else 2.0
    columns, face = own_ref.shape[1], table_ref.shape[0] // 2
    ghosts_ref = refs[-1]
    field_ref = refs[-2] if len(refs) > 1 else refs[-1]
    for first in range(0, columns, TILE):
        at = slice(first, first + TILE)
        field_ref[:, at] = (
            own_ref[:, at] + factor * arrived(got_a_ref, got_b_ref, table_ref, at)
        ).astype(jnp.bfloat16)
    if len(refs) == 1:
        return
    for side, got_ref in enumerate((got_a_ref, got_b_ref)):
        at = slice(side * face, (side + 1) * face)
        value = factor * (refs[side][:, :face] + got_ref[:, face:].astype(jnp.float32))
        if step > 0:
            value = value - refs[2][:, at].astype(jnp.float32)
        value = jnp.where(there_ref[side] != 0, value, 0.0)
        ghosts_ref[:, at] = value
        field_ref[:, columns + side * face : columns + (side + 1) * face] = value.astype(jnp.bfloat16)


def combine(step, there, own, got_a, got_b, table, ghost_operands):
    rows, columns = own.shape
    whole = pl.BlockSpec(memory_space=pltpu.VMEM)
    face = table.shape[0] // 2
    if ghost_operands:
        out_shape = (
            jax.ShapeDtypeStruct((rows, columns + 2 * face), jnp.bfloat16),
            jax.ShapeDtypeStruct((rows, 2 * face), jnp.float32),
        )
    else:
        out_shape = (jax.ShapeDtypeStruct((rows, columns), jnp.bfloat16),)
    return pl.pallas_call(
        functools.partial(combine_kernel, step),
        out_shape=out_shape,
        in_specs=[pl.BlockSpec(memory_space=pltpu.SMEM)] + [whole] * (4 + len(ghost_operands)),
        out_specs=(whole,) * len(out_shape),
        compiler_params=pltpu.CompilerParams(vmem_limit_bytes=16 * 1024 * 1024),
    )(there, own, got_a, got_b, table, *ghost_operands)


def exact(left, right, contract):
    return lax.dot_general(
        left,
        right,
        (contract, ((), ())),
        precision=lax.Precision.HIGHEST,
        preferred_element_type=jnp.float32,
    )


def inverse_factor(block):
    size = block.shape[0]
    groups = size // SUBLANES
    row = lax.broadcasted_iota(jnp.int32, (SUBLANES, LANES), 0)
    lane = lax.broadcasted_iota(jnp.int32, (SUBLANES, LANES), 1)
    left = [block[g * SUBLANES : (g + 1) * SUBLANES, :] for g in range(groups)]
    right = [(lane == row + g * SUBLANES).astype(jnp.float32) for g in range(groups)]

    def over_rows(values, index):
        return jnp.broadcast_to(values[index : index + 1, :], (SUBLANES, LANES))

    for k in range(groups):
        later = range(k, groups)
        column = {
            g: [
                jnp.broadcast_to(
                    left[g][:, k * SUBLANES + q : k * SUBLANES + q + 1], (SUBLANES, LANES)
                )
                for q in range(SUBLANES)
            ]
            for g in later
        }
        for q in range(SUBLANES):
            scale = lax.rsqrt(over_rows(column[k][q], q))
            factor = {g: column[g][q] * scale for g in later}
            left_row = over_rows(left[k], q) * scale
            right_row = over_rows(right[k], q) * scale
            below = jnp.where(row > q, factor[k], 0.0)
            left[k] = jnp.where(row == q, left_row, left[k] - below * left_row)
            right[k] = jnp.where(row == q, right_row, right[k] - below * right_row)
            for other in range(q + 1, SUBLANES):
                weight = over_rows(factor[k], other)
                for g in later:
                    column[g][other] = column[g][other] - factor[g] * weight
            for g in range(k + 1, groups):
                left[g] = left[g] - factor[g] * left_row
                right[g] = right[g] - factor[g] * right_row
    return jnp.concatenate(right, axis=0)


def orthonormal_kernel(scale, block_ref, gram_ref, filtered_ref, out_ref, inverse):
    size = gram_ref.shape[0]
    count = size // LANES
    at = [slice(i * LANES, (i + 1) * LANES) for i in range(count)]
    lower = {}
    inverses = {}
    for i in range(count):
        diagonal = gram_ref[at[i], at[i]]
        for j in range(i):
            diagonal = diagonal - exact(lower[i, j], lower[i, j], ((1,), (1,)))
        inverses[i, i] = inverse_factor(diagonal)
        for k in range(i + 1, count):
            entry = gram_ref[at[k], at[i]]
            for j in range(i):
                entry = entry - exact(lower[k, j], lower[i, j], ((1,), (1,)))
            lower[k, i] = exact(entry, inverses[i, i], ((1,), (1,)))
    inverse[...] = jnp.zeros_like(inverse)
    for i in range(count):
        for j in range(i):
            entry = exact(lower[i, j], inverses[j, j], ((1,), (0,)))
            for m in range(j + 1, i):
                entry = entry + exact(lower[i, m], inverses[m, j], ((1,), (0,)))
            inverses[i, j] = -exact(inverses[i, i], entry, ((1,), (0,)))
            inverse[at[i], at[j]] = inverses[i, j] * scale
        inverse[at[i], at[i]] = inverses[i, i] * scale
    rows = out_ref.shape[0]
    mine = inverse[pl.ds(pl.multiple_of(block_ref[0] * rows, rows), rows), :]
    high = mine.astype(jnp.bfloat16)
    low = (mine - high.astype(jnp.float32)).astype(jnp.bfloat16)
    width = 512
    for first in range(0, out_ref.shape[1], width):
        part = filtered_ref[:, first : first + width]
        out_ref[:, first : first + width] = jnp.dot(
            high, part, preferred_element_type=jnp.float32
        ) + jnp.dot(low, part, preferred_element_type=jnp.float32)


def orthonormal(block, gram, filtered, rows, scale):
    size = gram.shape[0]
    return pl.pallas_call(
        functools.partial(orthonormal_kernel, scale),
        out_shape=jax.ShapeDtypeStruct((rows, filtered.shape[1]), jnp.float32),
        in_specs=[
            pl.BlockSpec(memory_space=pltpu.SMEM),
            pl.BlockSpec(memory_space=pltpu.VMEM),
            pl.BlockSpec(memory_space=pltpu.VMEM),
        ],
        out_specs=pl.BlockSpec(memory_space=pltpu.VMEM),
        scratch_shapes=[pltpu.VMEM((size, size), jnp.float32)],
        compiler_params=pltpu.CompilerParams(vmem_limit_bytes=16 * 1024 * 1024),
    )(block, gram, filtered)


def swap_pairs(count, first):
    pairs = []
    for low in range(first, count - 1, 2):
        pairs += [(low, low + 1), (low + 1, low)]
    return pairs


def sum_over(values, axis):
    count = lax.axis_size(axis)
    if count & (count - 1):
        return lax.psum(values.astype(jnp.bfloat16), axis).astype(jnp.float32)
    step = 1
    while step < count:
        sent = values.astype(jnp.bfloat16)
        got = lax.ppermute(sent, axis, [(i, i ^ step) for i in range(count)])
        values = sent.astype(jnp.float32) + got.astype(jnp.float32)
        step *= 2
    return values


def per_device(orbitals, cell_matrices, connectivity, face_lower, face_upper):
    own_count = orbitals.shape[1]
    face = face_lower.shape[0]
    ext_count = own_count + 2 * face
    slabs = lax.axis_size("slab")
    slab = lax.axis_index("slab")
    even = slab % 2 == 0

    has_lower = slab > 0
    has_upper = slab < slabs - 1
    has_a = jnp.where(even, has_upper, has_lower)
    has_b = jnp.where(even, has_lower, has_upper)
    ghost_lower = jnp.arange(face, dtype=jnp.int32)
    ghost_upper = ghost_lower + (face + own_count)
    face_a = jnp.where(even, face_upper, face_lower)
    face_b = jnp.where(even, face_lower, face_upper)
    ghost_a = jnp.where(even, ghost_upper, ghost_lower)
    ghost_b = jnp.where(even, ghost_lower, ghost_upper)

    lower_at = jnp.where(even, own_count + face, own_count)
    upper_at = jnp.where(even, own_count, own_count + face)
    places = jnp.where(
        connectivity < face,
        connectivity + lower_at,
        jnp.where(
            connectivity < face + own_count,
            connectivity - face,
            connectivity - (face + own_count) + upper_at,
        ),
    ).reshape(-1) * SUBLANES
    columns_b = jnp.concatenate([ghost_b, face_b + face])
    columns_a = jnp.concatenate([ghost_a, face_a + face])
    own_columns = jnp.arange(own_count, dtype=jnp.int32) + face
    nodes = jnp.broadcast_to(connectivity[:, :, None], connectivity.shape + (LANES,))

    face_nodes = jnp.concatenate([face_a, face_b])
    face_table = (
        face_nodes[:, None] == lax.broadcasted_iota(jnp.int32, (2 * face, own_count), 1)
    ).astype(jnp.bfloat16)

    pairs_a = swap_pairs(slabs, 0)
    pairs_b = swap_pairs(slabs, 1)

    def times(left, right):
        return jnp.dot(left, right, preferred_element_type=jnp.float32)

    rounded = orbitals.astype(jnp.bfloat16)
    faces = lax.dot_general(
        rounded, face_table, (((1,), (1,)), ((), ())), preferred_element_type=jnp.float32
    ).astype(jnp.bfloat16)
    ghosts_b = lax.ppermute(faces[:, face:], "slab", pairs_b)
    ghosts_a = lax.ppermute(faces[:, :face], "slab", pairs_a)
    mine = jnp.concatenate([rounded, ghosts_a, ghosts_b], axis=1)
    gathered = lax.all_gather(mine, "orb", axis=0, tiled=True)
    matrix_b, matrix_a, own_matrix = assemble(
        places,
        jnp.concatenate([columns_b, columns_a, own_columns]),
        nodes,
        cell_matrices,
        ext_count,
        mine,
    )

    there = jnp.stack([has_a, has_b]).astype(jnp.int32)
    field = hold(gathered)
    ghosts = [field[:, own_count:]]
    before = ()
    for step in range(DEGREE):
        last = step == DEGREE - 1
        part_b = times(field, matrix_b[:, :face] if last else matrix_b)
        sent_b = part_b.astype(jnp.bfloat16)
        got_b = lax.ppermute(sent_b, "slab", pairs_b)
        part_a = times(field, matrix_a[:, :face] if last else matrix_a)
        sent_a = part_a.astype(jnp.bfloat16)
        got_a = lax.ppermute(sent_a, "slab", pairs_a)
        own = own_part(step, field, own_matrix, before, (sent_a, sent_b))
        if step == 0:
            before = (field,)
        else:
            before = arrivals
        arrivals = (own, got_a, got_b, face_table)
        if last:
            (filtered,) = combine(step, there, own, got_a, got_b, face_table, ())
        else:
            operands = (part_a, part_b) + ((ghosts[-2],) if step else ())
            field, new_ghosts = combine(step, there, own, got_a, got_b, face_table, operands)
            ghosts.append(new_ghosts)

    gram = lax.dot_general(
        filtered, filtered, (((1,), (1,)), ((), ())), preferred_element_type=jnp.float32
    )
    total = sum_over(gram, "slab")
    block = lax.axis_index("orb").astype(jnp.int32).reshape(1)
    return orthonormal(block, total, filtered, orbitals.shape[0], math.sqrt(own_count * slabs))


def solution(mesh):
    in_specs = (P("orb", "slab"), P("slab", None, None), P("slab", None), P("slab"), P("slab"))
    out_specs = P("orb", "slab")
    return jax.shard_map(
        per_device, mesh=mesh, in_specs=in_specs, out_specs=out_specs, check_vma=False
    )
```

```python
import functools
import math

import jax
import jax.numpy as jnp
from jax import lax
from jax.experimental import pallas as pl
from jax.experimental.pallas import tpu as pltpu
from jax.sharding import PartitionSpec as P

DEGREE = 4
LANES = 128
SUBLANES = 8
CHUNK = LANES * SUBLANES
PITCH = SUBLANES + 1
TILE = 256


def turn(tiles):
    row = lax.broadcasted_iota(jnp.int32, (SUBLANES, LANES), 0)
    tiles = [pltpu.roll(tile, i, 0) if i else tile for i, tile in enumerate(tiles)]
    step = 1
    while step < SUBLANES:
        far = (row & step) != 0
        tiles = [
            jnp.where(far, tiles[(i + step) % SUBLANES], tiles[i]) for i in range(SUBLANES)
        ]
        step *= 2
    tiles = [tiles[-i % SUBLANES] for i in range(SUBLANES)]
    return [
        pltpu.roll(tile, SUBLANES - i, 0) if i else tile for i, tile in enumerate(tiles)
    ]


def assemble_kernel(
    places_ref, column_ref, nodes_ref, cell_ref, after_ref, shared_b_ref, shared_a_ref, own_ref,
    total, even_terms, odd_terms, rounded, sent,
):
    chunk = pl.program_id(0)
    chunks = pl.num_programs(0)
    cell = pl.program_id(1)
    cells = pl.num_programs(1)
    cell_nodes = cell_ref.shape[1]
    ext_count = own_ref.shape[1]
    share = rounded.shape[1] // (places_ref.shape[0] // (2 * cell_nodes))
    parts = CHUNK // TILE
    part_rows = cell_nodes // parts
    group = 32
    table = chunk % 2 * (cells * cell_nodes)

    def spread_part(part):
        columns = column_ref[:, part * TILE : (part + 1) * TILE]
        picker = jnp.concatenate(
            [
                (nodes_ref[0] == columns[:, half * LANES : (half + 1) * LANES])
                .astype(jnp.float32)
                .astype(jnp.bfloat16)
                for half in range(2)
            ],
            axis=1,
        )
        return jnp.dot(cell_ref[0], picker, preferred_element_type=jnp.float32)

    def keep_part(part, spread, terms):
        for first in range(0, cell_nodes, SUBLANES):
            for half in range(2):
                terms[pl.ds(first * PITCH + 2 * part + half, SUBLANES, stride=PITCH), :] = spread[
                    first : first + SUBLANES, half * LANES : (half + 1) * LANES
                ]

    def add_part(part, of_cell, terms):
        first = part * part_rows
        for start in range(0, part_rows, group):
            places = [
                pl.multiple_of(
                    places_ref[table + of_cell * cell_nodes + first + start + k], SUBLANES
                )
                for k in range(group)
            ]
            sums = [
                total[pl.ds(places[k], SUBLANES), :]
                + terms[pl.ds((first + start + k) * PITCH, SUBLANES), :]
                for k in range(group)
            ]
            for k in range(group):
                total[pl.ds(places[k], SUBLANES), :] = sums[k]

    def round_rows(first, which, zero):
        base = pl.multiple_of((which * ext_count + first) * SUBLANES, 16 * SUBLANES)
        upper, lower = (
            turn(
                [
                    total[pl.ds(base + (start + i) * SUBLANES, SUBLANES), :]
                    for i in range(SUBLANES)
                ]
            )
            for start in (0, SUBLANES)
        )
        for block in range(SUBLANES):
            rounded[
                block // 2, pl.ds(first, 16), block % 2 * LANES : (block % 2 + 1) * LANES
            ] = jnp.concatenate([upper[block], lower[block]], axis=0).astype(jnp.bfloat16)
        if zero:
            total[pl.ds(base, 16 * SUBLANES), :] = jnp.zeros((16 * SUBLANES, LANES), jnp.float32)

    def round_part(part):
        pieces = share // 16
        for piece in range(part * pieces // parts, (part + 1) * pieces // parts):
            round_rows(pl.multiple_of(cell * share + piece * 16, 16), 1 - chunk % 2, True)

    def sends(index, of_chunk, to_own):
        rows = pl.ds(pl.multiple_of(index * share, 16), share)
        copies = []
        for part in range(parts):
            if to_own:
                target = own_ref.at[(of_chunk - 1) * parts + part, rows]
            else:
                half = (shared_b_ref, shared_a_ref)[part // 2]
                target = half.at[rows, part % 2 * TILE : (part % 2 + 1) * TILE]
            copies.append(
                pltpu.make_async_copy(rounded.at[part, rows], target, sent.at[index, part])
            )
        return copies

    def wait_share(index):
        for copy in sends(index, 1, True):
            copy.wait()

    @pl.when(chunk > 1)
    def _():
        wait_share(cell)

    @pl.when((cell == 0) & (chunk == 0))
    def _():
        def zero(step, carry):
            total[pl.ds(pl.multiple_of(step * 64, 64), 64), :] = jnp.zeros((64, LANES), jnp.float32)
            return carry

        lax.fori_loop(0, ext_count * SUBLANES // 64, zero, 0, unroll=4)

    @pl.when(cell == 0)
    def _():
        for part in range(parts):
            keep_part(part, spread_part(part), even_terms)
            round_part(part)

    for parity, (before, now) in enumerate(((odd_terms, even_terms), (even_terms, odd_terms))):

        @pl.when((cell > 0) & (cell % 2 == parity))
        def _():
            for part in range(parts):
                keep_part(part, spread_part(part), now)
                add_part(part, cell - 1, before)
                round_part(part)

        @pl.when((cell == cells - 1) & (cell % 2 == parity))
        def _():
            def body(part, carry):
                add_part(part, cell, now)
                return carry

            lax.fori_loop(0, parts, body, 0)

    @pl.when(chunk == 1)
    def _():
        for copy in sends(cell, 0, False):
            copy.start()

    @pl.when(chunk > 1)
    def _():
        for copy in sends(cell, chunk - 1, True):
            copy.start()

    @pl.when((cell == cells - 1) & (chunk == chunks - 1))
    def _():
        def last_share(index, carry):
            wait_share(index)

            def last_rows(piece, inner):
                round_rows(pl.multiple_of(index * share + piece * 16, 16), chunk % 2, False)
                return inner

            lax.fori_loop(0, share // 16, last_rows, 0, unroll=4)
            for copy in sends(index, chunk, True):
                copy.start()
            return carry

        lax.fori_loop(0, cells, last_share, 0)

        def settle(index, carry):
            wait_share(index)
            return carry

        lax.fori_loop(0, cells, settle, 0)


def assemble(places, columns, nodes, cell_matrices, ext_count, after):
    cells, cell_nodes, _ = cell_matrices.shape
    count = columns.shape[0]
    chunks = count // CHUNK
    assert chunks > 1 and ext_count % (16 * cells) == 0
    half = jax.ShapeDtypeStruct((ext_count, CHUNK // 2), jnp.bfloat16)
    return pl.pallas_call(
        assemble_kernel,
        out_shape=(
            half,
            half,
            jax.ShapeDtypeStruct(((count - CHUNK) // TILE, ext_count, TILE), jnp.bfloat16),
        ),
        grid_spec=pltpu.PrefetchScalarGridSpec(
            num_scalar_prefetch=1,
            grid=(chunks, cells),
            in_specs=[
                pl.BlockSpec((1, CHUNK), lambda q, c, places: (0, q)),
                pl.BlockSpec((1, cell_nodes, LANES), lambda q, c, places: (c, 0, 0)),
                pl.BlockSpec((1, cell_nodes, cell_nodes), lambda q, c, places: (c, 0, 0)),
                pl.BlockSpec(memory_space=pl.ANY),
            ],
            out_specs=(pl.BlockSpec(memory_space=pl.ANY),) * 3,
            scratch_shapes=[
                pltpu.VMEM((2 * ext_count * SUBLANES, LANES), jnp.float32),
                pltpu.VMEM((cell_nodes * PITCH, LANES), jnp.float32),
                pltpu.VMEM((cell_nodes * PITCH, LANES), jnp.float32),
                pltpu.VMEM((CHUNK // TILE, ext_count, TILE), jnp.bfloat16),
                pltpu.SemaphoreType.DMA((cells, CHUNK // TILE)),
            ],
        ),
        compiler_params=pltpu.CompilerParams(vmem_limit_bytes=57 * 1024 * 1024),
        cost_estimate=pl.CostEstimate(
            flops=16 * cells * cell_nodes * cell_nodes * count,
            bytes_accessed=chunks * cells * cell_nodes * cell_nodes * 2 + ext_count * count * 2,
            transcendentals=0,
        ),
    )(
        jnp.concatenate([places, places + ext_count * SUBLANES]),
        columns[None, :],
        nodes,
        cell_matrices,
        after,
    )


def hold_kernel(*refs):
    count = len(refs) // 2
    done = refs[-1]
    copies = [pltpu.make_async_copy(refs[i], refs[count + i], done.at[i]) for i in range(count)]
    for copy in copies:
        copy.start()
    for copy in copies:
        copy.wait()


def hold(*arrays):
    return pl.pallas_call(
        hold_kernel,
        out_shape=tuple(jax.ShapeDtypeStruct(x.shape, x.dtype) for x in arrays),
        in_specs=[pl.BlockSpec(memory_space=pl.ANY)] * len(arrays),
        out_specs=(pl.BlockSpec(memory_space=pltpu.VMEM),) * len(arrays),
        scratch_shapes=[pltpu.SemaphoreType.DMA((len(arrays),))],
        compiler_params=pltpu.CompilerParams(vmem_limit_bytes=16 * 1024 * 1024),
    )(*arrays)


def arrived(got_a_ref, got_b_ref, table_ref, at):
    incoming = jnp.concatenate(
        [ref[:, : table_ref.shape[0] // 2] for ref in (got_a_ref, got_b_ref)], axis=1
    )
    return jnp.dot(incoming, table_ref[:, at], preferred_element_type=jnp.float32)


def own_kernel(step, extended_ref, matrix_ref, *refs):
    out_ref = refs[-1]

    def body(tile, carry):
        at = pl.ds(pl.multiple_of(tile * TILE, TILE), TILE)
        product = jnp.dot(extended_ref[...], matrix_ref[tile], preferred_element_type=jnp.float32)
        if step == 1:
            product = 2.0 * product - refs[0][:, at].astype(jnp.float32)
        if step > 1:
            factor = 1.0 if step == 2 else 2.0
            product = 2.0 * product - (refs[0][:, at] + factor * arrived(*refs[1:4], at))
        out_ref[:, at] = product
        return carry

    lax.fori_loop(0, matrix_ref.shape[0], body, 0, unroll=4)


def own_part(step, extended, matrix, before, after):
    rows, depth = extended.shape
    tiles, _, width = matrix.shape
    columns = tiles * width
    whole = pl.BlockSpec(memory_space=pltpu.VMEM)
    operands = (extended, matrix) + before
    return pl.pallas_call(
        functools.partial(own_kernel, step),
        out_shape=jax.ShapeDtypeStruct((rows, columns), jnp.float32),
        in_specs=[whole] * len(operands) + [pl.BlockSpec(memory_space=pl.ANY)] * len(after),
        out_specs=whole,
        compiler_params=pltpu.CompilerParams(vmem_limit_bytes=16 * 1024 * 1024),
        cost_estimate=pl.CostEstimate(
            flops=8 * rows * depth * columns,
            bytes_accessed=2 * depth * columns + 4 * rows * columns,
            transcendentals=0,
        ),
    )(*operands, *after)


def combine_kernel(step, there_ref, own_ref, got_a_ref, got_b_ref, table_ref, *refs):
    factor = 1.0 if step == 0 else 2.0
    columns, face = own_ref.shape[1], table_ref.shape[0] // 2
    ghosts_ref = refs[-1]
    field_ref = refs[-2] if len(refs) > 1 else refs[-1]
    for first in range(0, columns, TILE):
        at = slice(first, first + TILE)
        field_ref[:, at] = (
            own_ref[:, at] + factor * arrived(got_a_ref, got_b_ref, table_ref, at)
        ).astype(jnp.bfloat16)
    if len(refs) == 1:
        return
    for side, got_ref in enumerate((got_a_ref, got_b_ref)):
        at = slice(side * face, (side + 1) * face)
        value = factor * (refs[side][:, :face] + got_ref[:, face:].astype(jnp.float32))
        if step > 0:
            value = value - refs[2][:, at].astype(jnp.float32)
        value = jnp.where(there_ref[side] != 0, value, 0.0)
        ghosts_ref[:, at] = value
        field_ref[:, columns + side * face : columns + (side + 1) * face] = value.astype(jnp.bfloat16)


def combine(step, there, own, got_a, got_b, table, ghost_operands):
    rows, columns = own.shape
    whole = pl.BlockSpec(memory_space=pltpu.VMEM)
    face = table.shape[0] // 2
    if ghost_operands:
        out_shape = (
            jax.ShapeDtypeStruct((rows, columns + 2 * face), jnp.bfloat16),
            jax.ShapeDtypeStruct((rows, 2 * face), jnp.float32),
        )
    else:
        out_shape = (jax.ShapeDtypeStruct((rows, columns), jnp.bfloat16),)
    return pl.pallas_call(
        functools.partial(combine_kernel, step),
        out_shape=out_shape,
        in_specs=[pl.BlockSpec(memory_space=pltpu.SMEM)] + [whole] * (4 + len(ghost_operands)),
        out_specs=(whole,) * len(out_shape),
        compiler_params=pltpu.CompilerParams(vmem_limit_bytes=16 * 1024 * 1024),
    )(there, own, got_a, got_b, table, *ghost_operands)


def exact(left, right, contract):
    return lax.dot_general(
        left,
        right,
        (contract, ((), ())),
        precision=lax.Precision.HIGHEST,
        preferred_element_type=jnp.float32,
    )


def inverse_factor(block):
    size = block.shape[0]
    groups = size // SUBLANES
    row = lax.broadcasted_iota(jnp.int32, (SUBLANES, LANES), 0)
    lane = lax.broadcasted_iota(jnp.int32, (SUBLANES, LANES), 1)
    left = [block[g * SUBLANES : (g + 1) * SUBLANES, :] for g in range(groups)]
    right = [(lane == row + g * SUBLANES).astype(jnp.float32) for g in range(groups)]

    def over_rows(values, index):
        return jnp.broadcast_to(values[index : index + 1, :], (SUBLANES, LANES))

    for k in range(groups):
        later = range(k, groups)
        column = {
            g: [
                jnp.broadcast_to(
                    left[g][:, k * SUBLANES + q : k * SUBLANES + q + 1], (SUBLANES, LANES)
                )
                for q in range(SUBLANES)
            ]
            for g in later
        }
        pivots = {
            (i, j): over_rows(column[k][j], i) for i in range(SUBLANES) for j in range(i + 1)
        }
        for q in range(SUBLANES):
            scale = lax.rsqrt(pivots[q, q])
            weights = {i: pivots[i, q] * scale for i in range(q + 1, SUBLANES)}
            for i in range(q + 1, SUBLANES):
                for j in range(q + 1, i + 1):
                    pivots[i, j] = pivots[i, j] - weights[i] * weights[j]
            factor = {g: column[g][q] * scale for g in later}
            left_row = over_rows(left[k], q) * scale
            right_row = over_rows(right[k], q) * scale
            below = jnp.where(row > q, factor[k], 0.0)
            left[k] = jnp.where(row == q, left_row, left[k] - below * left_row)
            right[k] = jnp.where(row == q, right_row, right[k] - below * right_row)
            for other in range(q + 1, SUBLANES):
                for g in later:
                    column[g][other] = column[g][other] - factor[g] * weights[other]
            for g in range(k + 1, groups):
                left[g] = left[g] - factor[g] * left_row
                right[g] = right[g] - factor[g] * right_row
    return jnp.concatenate(right, axis=0)


def orthonormal_kernel(scale, block_ref, gram_ref, filtered_ref, out_ref, inverse):
    size = gram_ref.shape[0]
    count = size // LANES
    at = [slice(i * LANES, (i + 1) * LANES) for i in range(count)]
    lower = {}
    inverses = {}
    for i in range(count):
        diagonal = gram_ref[at[i], at[i]]
        for j in range(i):
            diagonal = diagonal - exact(lower[i, j], lower[i, j], ((1,), (1,)))
        inverses[i, i] = inverse_factor(diagonal)
        for k in range(i + 1, count):
            entry = gram_ref[at[k], at[i]]
            for j in range(i):
                entry = entry - exact(lower[k, j], lower[i, j], ((1,), (1,)))
            lower[k, i] = exact(entry, inverses[i, i], ((1,), (1,)))
    inverse[...] = jnp.zeros_like(inverse)
    for i in range(count):
        for j in range(i):
            entry = exact(lower[i, j], inverses[j, j], ((1,), (0,)))
            for m in range(j + 1, i):
                entry = entry + exact(lower[i, m], inverses[m, j], ((1,), (0,)))
            inverses[i, j] = -exact(inverses[i, i], entry, ((1,), (0,)))
            inverse[at[i], at[j]] = inverses[i, j] * scale
        inverse[at[i], at[i]] = inverses[i, i] * scale
    rows = out_ref.shape[0]
    mine = inverse[pl.ds(pl.multiple_of(block_ref[0] * rows, rows), rows), :]
    high = mine.astype(jnp.bfloat16)
    low = (mine - high.astype(jnp.float32)).astype(jnp.bfloat16)
    width = 512
    for first in range(0, out_ref.shape[1], width):
        part = filtered_ref[:, first : first + width]
        out_ref[:, first : first + width] = jnp.dot(
            high, part, preferred_element_type=jnp.float32
        ) + jnp.dot(low, part, preferred_element_type=jnp.float32)


def orthonormal(block, gram, filtered, rows, scale):
    size = gram.shape[0]
    return pl.pallas_call(
        functools.partial(orthonormal_kernel, scale),
        out_shape=jax.ShapeDtypeStruct((rows, filtered.shape[1]), jnp.float32),
        in_specs=[
            pl.BlockSpec(memory_space=pltpu.SMEM),
            pl.BlockSpec(memory_space=pltpu.VMEM),
            pl.BlockSpec(memory_space=pltpu.VMEM),
        ],
        out_specs=pl.BlockSpec(memory_space=pltpu.VMEM),
        scratch_shapes=[pltpu.VMEM((size, size), jnp.float32)],
        compiler_params=pltpu.CompilerParams(vmem_limit_bytes=16 * 1024 * 1024),
    )(block, gram, filtered)


def swap_pairs(count, first):
    pairs = []
    for low in range(first, count - 1, 2):
        pairs += [(low, low + 1), (low + 1, low)]
    return pairs


def sum_over(values, axis):
    count = lax.axis_size(axis)
    if count & (count - 1):
        return lax.psum(values.astype(jnp.bfloat16), axis).astype(jnp.float32)
    step = 1
    while step < count:
        sent = values.astype(jnp.bfloat16)
        got = lax.ppermute(sent, axis, [(i, i ^ step) for i in range(count)])
        values = sent.astype(jnp.float32) + got.astype(jnp.float32)
        step *= 2
    return values


def per_device(orbitals, cell_matrices, connectivity, face_lower, face_upper):
    own_count = orbitals.shape[1]
    face = face_lower.shape[0]
    ext_count = own_count + 2 * face
    slabs = lax.axis_size("slab")
    slab = lax.axis_index("slab")
    even = slab % 2 == 0

    has_lower = slab > 0
    has_upper = slab < slabs - 1
    has_a = jnp.where(even, has_upper, has_lower)
    has_b = jnp.where(even, has_lower, has_upper)
    ghost_lower = jnp.arange(face, dtype=jnp.int32)
    ghost_upper = ghost_lower + (face + own_count)
    face_a = jnp.where(even, face_upper, face_lower)
    face_b = jnp.where(even, face_lower, face_upper)
    ghost_a = jnp.where(even, ghost_upper, ghost_lower)
    ghost_b = jnp.where(even, ghost_lower, ghost_upper)

    lower_at = jnp.where(even, own_count + face, own_count)
    upper_at = jnp.where(even, own_count, own_count + face)
    places = jnp.where(
        connectivity < face,
        connectivity + lower_at,
        jnp.where(
            connectivity < face + own_count,
            connectivity - face,
            connectivity - (face + own_count) + upper_at,
        ),
    ).reshape(-1) * SUBLANES
    columns_b = jnp.concatenate([ghost_b, face_b + face])
    columns_a = jnp.concatenate([ghost_a, face_a + face])
    own_columns = jnp.arange(own_count, dtype=jnp.int32) + face
    nodes = jnp.broadcast_to(connectivity[:, :, None], connectivity.shape + (LANES,))

    face_nodes = jnp.concatenate([face_a, face_b])
    face_table = (
        face_nodes[:, None] == lax.broadcasted_iota(jnp.int32, (2 * face, own_count), 1)
    ).astype(jnp.bfloat16)

    pairs_a = swap_pairs(slabs, 0)
    pairs_b = swap_pairs(slabs, 1)

    def times(left, right):
        return jnp.dot(left, right, preferred_element_type=jnp.float32)

    rounded = orbitals.astype(jnp.bfloat16)
    faces = lax.dot_general(
        rounded, face_table, (((1,), (1,)), ((), ())), preferred_element_type=jnp.float32
    ).astype(jnp.bfloat16)
    ghosts_b = lax.ppermute(faces[:, face:], "slab", pairs_b)
    ghosts_a = lax.ppermute(faces[:, :face], "slab", pairs_a)
    mine = jnp.concatenate([rounded, ghosts_a, ghosts_b], axis=1)
    gathered = lax.all_gather(mine, "orb", axis=0, tiled=True)
    matrix_b, matrix_a, own_matrix = assemble(
        places,
        jnp.concatenate([columns_b, columns_a, own_columns]),
        nodes,
        cell_matrices,
        ext_count,
        mine,
    )

    there = jnp.stack([has_a, has_b]).astype(jnp.int32)
    field, matrix_b, matrix_a = hold(gathered, matrix_b, matrix_a)
    ghosts = [field[:, own_count:]]
    before = ()
    for step in range(DEGREE):
        last = step == DEGREE - 1
        part_b = times(field, matrix_b[:, :face] if last else matrix_b)
        sent_b = part_b.astype(jnp.bfloat16)
        got_b = lax.ppermute(sent_b, "slab", pairs_b)
        part_a = times(field, matrix_a[:, :face] if last else matrix_a)
        sent_a = part_a.astype(jnp.bfloat16)
        got_a = lax.ppermute(sent_a, "slab", pairs_a)
        own = own_part(step, field, own_matrix, before, (sent_a, sent_b))
        if step == 0:
            before = (field,)
        else:
            before = arrivals
        arrivals = (own, got_a, got_b, face_table)
        if last:
            (filtered,) = combine(step, there, own, got_a, got_b, face_table, ())
        else:
            operands = (part_a, part_b) + ((ghosts[-2],) if step else ())
            field, new_ghosts = combine(step, there, own, got_a, got_b, face_table, operands)
            ghosts.append(new_ghosts)

    gram = lax.dot_general(
        filtered, filtered, (((1,), (1,)), ((), ())), preferred_element_type=jnp.float32
    )
    total = sum_over(gram, "slab")
    block = lax.axis_index("orb").astype(jnp.int32).reshape(1)
    return orthonormal(block, total, filtered, orbitals.shape[0], math.sqrt(own_count * slabs))


def solution(mesh):
    in_specs = (P("orb", "slab"), P("slab", None, None), P("slab", None), P("slab"), P("slab"))
    out_specs = P("orb", "slab")
    return jax.shard_map(
        per_device, mesh=mesh, in_specs=in_specs, out_specs=out_specs, check_vma=False
    )
```

```python
import functools
import math

import jax
import jax.numpy as jnp
from jax import lax
from jax.experimental import pallas as pl
from jax.experimental.pallas import tpu as pltpu
from jax.sharding import PartitionSpec as P

DEGREE = 4
LANES = 128
SUBLANES = 8
CHUNK = LANES * SUBLANES
PITCH = SUBLANES + 1
TILE = 256


def assemble_kernel(
    places_ref, column_ref, nodes_ref, cell_ref, after_ref, shared_b_ref, shared_a_ref, own_ref,
    total, even_terms, odd_terms, rounded, sent,
):
    chunk = pl.program_id(0)
    chunks = pl.num_programs(0)
    cell = pl.program_id(1)
    cells = pl.num_programs(1)
    cell_nodes = cell_ref.shape[1]
    ext_count = own_ref.shape[1]
    share = rounded.shape[1] // (places_ref.shape[0] // (2 * cell_nodes))
    parts = CHUNK // TILE
    part_rows = cell_nodes // parts
    group = 32
    table = chunk % 2 * (cells * cell_nodes)

    def spread_part(part):
        columns = column_ref[:, part * TILE : (part + 1) * TILE]
        picker = jnp.concatenate(
            [
                (nodes_ref[0] == columns[:, half * LANES : (half + 1) * LANES])
                .astype(jnp.float32)
                .astype(jnp.bfloat16)
                for half in range(2)
            ],
            axis=1,
        )
        return jnp.dot(cell_ref[0], picker, preferred_element_type=jnp.float32)

    def keep_part(part, spread, terms):
        for first in range(0, cell_nodes, SUBLANES):
            for half in range(2):
                terms[pl.ds(first * PITCH + 2 * part + half, SUBLANES, stride=PITCH), :] = spread[
                    first : first + SUBLANES, half * LANES : (half + 1) * LANES
                ]

    def add_part(part, of_cell, terms):
        first = part * part_rows
        for start in range(0, part_rows, group):
            places = [
                places_ref[table + of_cell * cell_nodes + first + start + k] for k in range(group)
            ]
            sums = [
                total[pl.ds(places[k], SUBLANES), :]
                + terms[pl.ds((first + start + k) * PITCH, SUBLANES), :]
                for k in range(group)
            ]
            for k in range(group):
                total[pl.ds(places[k], SUBLANES), :] = sums[k]

    def round_rows(first, which, zero):
        base = (which * ext_count + first) * PITCH
        for block in range(SUBLANES):
            upper = total[pl.ds(base + block, SUBLANES, stride=PITCH), :]
            lower = total[pl.ds(base + SUBLANES * PITCH + block, SUBLANES, stride=PITCH), :]
            rounded[
                block // 2, pl.ds(first, 16), block % 2 * LANES : (block % 2 + 1) * LANES
            ] = jnp.concatenate([upper, lower], axis=0).astype(jnp.bfloat16)
        if zero:
            total[pl.ds(pl.multiple_of(base, SUBLANES), 16 * PITCH), :] = jnp.zeros(
                (16 * PITCH, LANES), jnp.float32
            )

    def round_part(part):
        pieces = share // 16
        for piece in range(part * pieces // parts, (part + 1) * pieces // parts):
            round_rows(pl.multiple_of(cell * share + piece * 16, 16), 1 - chunk % 2, True)

    def sends(index, of_chunk, to_own):
        rows = pl.ds(pl.multiple_of(index * share, 16), share)
        copies = []
        for part in range(parts):
            if to_own:
                target = own_ref.at[(of_chunk - 1) * parts + part, rows]
            else:
                half = (shared_b_ref, shared_a_ref)[part // 2]
                target = half.at[rows, part % 2 * TILE : (part % 2 + 1) * TILE]
            copies.append(
                pltpu.make_async_copy(rounded.at[part, rows], target, sent.at[index, part])
            )
        return copies

    def wait_share(index):
        for copy in sends(index, 1, True):
            copy.wait()

    @pl.when(chunk > 1)
    def _():
        wait_share(cell)

    @pl.when((cell == 0) & (chunk == 0))
    def _():
        def zero(step, carry):
            total[pl.ds(pl.multiple_of(step * 64, 64), 64), :] = jnp.zeros((64, LANES), jnp.float32)
            return carry

        lax.fori_loop(0, ext_count * PITCH // 64, zero, 0, unroll=4)

    @pl.when(cell == 0)
    def _():
        for part in range(parts):
            keep_part(part, spread_part(part), even_terms)
            round_part(part)

    for parity, (before, now) in enumerate(((odd_terms, even_terms), (even_terms, odd_terms))):

        @pl.when((cell > 0) & (cell % 2 == parity))
        def _():
            for part in range(parts):
                keep_part(part, spread_part(part), now)
                add_part(part, cell - 1, before)
                round_part(part)

        @pl.when((cell == cells - 1) & (cell % 2 == parity))
        def _():
            def body(part, carry):
                add_part(part, cell, now)
                return carry

            lax.fori_loop(0, parts, body, 0)

    @pl.when(chunk == 1)
    def _():
        for copy in sends(cell, 0, False):
            copy.start()

    @pl.when(chunk > 1)
    def _():
        for copy in sends(cell, chunk - 1, True):
            copy.start()

    @pl.when((cell == cells - 1) & (chunk == chunks - 1))
    def _():
        def last_share(index, carry):
            wait_share(index)

            def last_rows(piece, inner):
                round_rows(pl.multiple_of(index * share + piece * 16, 16), chunk % 2, False)
                return inner

            lax.fori_loop(0, share // 16, last_rows, 0, unroll=4)
            for copy in sends(index, chunk, True):
                copy.start()
            return carry

        lax.fori_loop(0, cells, last_share, 0)

        def settle(index, carry):
            wait_share(index)
            return carry

        lax.fori_loop(0, cells, settle, 0)


def assemble(places, columns, nodes, cell_matrices, ext_count, after):
    cells, cell_nodes, _ = cell_matrices.shape
    count = columns.shape[0]
    chunks = count // CHUNK
    assert chunks > 1 and ext_count % (16 * cells) == 0
    half = jax.ShapeDtypeStruct((ext_count, CHUNK // 2), jnp.bfloat16)
    return pl.pallas_call(
        assemble_kernel,
        out_shape=(
            half,
            half,
            jax.ShapeDtypeStruct(((count - CHUNK) // TILE, ext_count, TILE), jnp.bfloat16),
        ),
        grid_spec=pltpu.PrefetchScalarGridSpec(
            num_scalar_prefetch=1,
            grid=(chunks, cells),
            in_specs=[
                pl.BlockSpec((1, CHUNK), lambda q, c, places: (0, q)),
                pl.BlockSpec((1, cell_nodes, LANES), lambda q, c, places: (c, 0, 0)),
                pl.BlockSpec((1, cell_nodes, cell_nodes), lambda q, c, places: (c, 0, 0)),
                pl.BlockSpec(memory_space=pl.ANY),
            ],
            out_specs=(pl.BlockSpec(memory_space=pl.ANY),) * 3,
            scratch_shapes=[
                pltpu.VMEM((2 * ext_count * PITCH, LANES), jnp.float32),
                pltpu.VMEM((cell_nodes * PITCH, LANES), jnp.float32),
                pltpu.VMEM((cell_nodes * PITCH, LANES), jnp.float32),
                pltpu.VMEM((CHUNK // TILE, ext_count, TILE), jnp.bfloat16),
                pltpu.SemaphoreType.DMA((cells, CHUNK // TILE)),
            ],
        ),
        compiler_params=pltpu.CompilerParams(vmem_limit_bytes=57 * 1024 * 1024),
        cost_estimate=pl.CostEstimate(
            flops=16 * cells * cell_nodes * cell_nodes * count,
            bytes_accessed=chunks * cells * cell_nodes * cell_nodes * 2 + ext_count * count * 2,
            transcendentals=0,
        ),
    )(
        jnp.concatenate([places, places + ext_count * PITCH]),
        columns[None, :],
        nodes,
        cell_matrices,
        after,
    )


def hold_kernel(*refs):
    count = len(refs) // 2
    done = refs[-1]
    copies = [pltpu.make_async_copy(refs[i], refs[count + i], done.at[i]) for i in range(count)]
    for copy in copies:
        copy.start()
    for copy in copies:
        copy.wait()


def hold(*arrays):
    return pl.pallas_call(
        hold_kernel,
        out_shape=tuple(jax.ShapeDtypeStruct(x.shape, x.dtype) for x in arrays),
        in_specs=[pl.BlockSpec(memory_space=pl.ANY)] * len(arrays),
        out_specs=(pl.BlockSpec(memory_space=pltpu.VMEM),) * len(arrays),
        scratch_shapes=[pltpu.SemaphoreType.DMA((len(arrays),))],
        compiler_params=pltpu.CompilerParams(vmem_limit_bytes=16 * 1024 * 1024),
    )(*arrays)


def arrived(got_a_ref, got_b_ref, table_ref, at):
    incoming = jnp.concatenate(
        [ref[:, : table_ref.shape[0] // 2] for ref in (got_a_ref, got_b_ref)], axis=1
    )
    return jnp.dot(incoming, table_ref[:, at], preferred_element_type=jnp.float32)


def own_kernel(step, extended_ref, matrix_ref, *refs):
    out_ref = refs[-1]

    def body(tile, carry):
        at = pl.ds(pl.multiple_of(tile * TILE, TILE), TILE)
        product = jnp.dot(extended_ref[...], matrix_ref[tile], preferred_element_type=jnp.float32)
        if step == 1:
            product = 2.0 * product - refs[0][:, at].astype(jnp.float32)
        if step > 1:
            factor = 1.0 if step == 2 else 2.0
            product = 2.0 * product - (refs[0][:, at] + factor * arrived(*refs[1:4], at))
        out_ref[:, at] = product
        return carry

    lax.fori_loop(0, matrix_ref.shape[0], body, 0, unroll=4)


def own_part(step, extended, matrix, before, after):
    rows, depth = extended.shape
    tiles, _, width = matrix.shape
    columns = tiles * width
    whole = pl.BlockSpec(memory_space=pltpu.VMEM)
    operands = (extended, matrix) + before
    return pl.pallas_call(
        functools.partial(own_kernel, step),
        out_shape=jax.ShapeDtypeStruct((rows, columns), jnp.float32),
        in_specs=[whole] * len(operands) + [pl.BlockSpec(memory_space=pl.ANY)] * len(after),
        out_specs=whole,
        compiler_params=pltpu.CompilerParams(vmem_limit_bytes=16 * 1024 * 1024),
        cost_estimate=pl.CostEstimate(
            flops=8 * rows * depth * columns,
            bytes_accessed=2 * depth * columns + 4 * rows * columns,
            transcendentals=0,
        ),
    )(*operands, *after)


def combine_kernel(step, there_ref, own_ref, got_a_ref, got_b_ref, table_ref, *refs):
    factor = 1.0 if step == 0 else 2.0
    columns, face = own_ref.shape[1], table_ref.shape[0] // 2
    ghosts_ref = refs[-1]
    field_ref = refs[-2] if len(refs) > 1 else refs[-1]
    for first in range(0, columns, TILE):
        at = slice(first, first + TILE)
        field_ref[:, at] = (
            own_ref[:, at] + factor * arrived(got_a_ref, got_b_ref, table_ref, at)
        ).astype(jnp.bfloat16)
    if len(refs) == 1:
        return
    for side, got_ref in enumerate((got_a_ref, got_b_ref)):
        at = slice(side * face, (side + 1) * face)
        value = factor * (refs[side][:, :face] + got_ref[:, face:].astype(jnp.float32))
        if step > 0:
            value = value - refs[2][:, at].astype(jnp.float32)
        value = jnp.where(there_ref[side] != 0, value, 0.0)
        ghosts_ref[:, at] = value
        field_ref[:, columns + side * face : columns + (side + 1) * face] = value.astype(jnp.bfloat16)


def combine(step, there, own, got_a, got_b, table, ghost_operands):
    rows, columns = own.shape
    whole = pl.BlockSpec(memory_space=pltpu.VMEM)
    face = table.shape[0] // 2
    if ghost_operands:
        out_shape = (
            jax.ShapeDtypeStruct((rows, columns + 2 * face), jnp.bfloat16),
            jax.ShapeDtypeStruct((rows, 2 * face), jnp.float32),
        )
    else:
        out_shape = (jax.ShapeDtypeStruct((rows, columns), jnp.bfloat16),)
    return pl.pallas_call(
        functools.partial(combine_kernel, step),
        out_shape=out_shape,
        in_specs=[pl.BlockSpec(memory_space=pltpu.SMEM)] + [whole] * (4 + len(ghost_operands)),
        out_specs=(whole,) * len(out_shape),
        compiler_params=pltpu.CompilerParams(vmem_limit_bytes=16 * 1024 * 1024),
    )(there, own, got_a, got_b, table, *ghost_operands)


def exact(left, right, contract):
    return lax.dot_general(
        left,
        right,
        (contract, ((), ())),
        precision=lax.Precision.HIGHEST,
        preferred_element_type=jnp.float32,
    )


def inverse_factor(block):
    size = block.shape[0]
    groups = size // SUBLANES
    row = lax.broadcasted_iota(jnp.int32, (SUBLANES, LANES), 0)
    lane = lax.broadcasted_iota(jnp.int32, (SUBLANES, LANES), 1)
    left = [block[g * SUBLANES : (g + 1) * SUBLANES, :] for g in range(groups)]
    right = [(lane == row + g * SUBLANES).astype(jnp.float32) for g in range(groups)]

    def over_rows(values, index):
        return jnp.broadcast_to(values[index : index + 1, :], (SUBLANES, LANES))

    for k in range(groups):
        later = range(k, groups)
        column = {
            g: [
                jnp.broadcast_to(
                    left[g][:, k * SUBLANES + q : k * SUBLANES + q + 1], (SUBLANES, LANES)
                )
                for q in range(SUBLANES)
            ]
            for g in later
        }
        for q in range(SUBLANES):
            scale = lax.rsqrt(over_rows(column[k][q], q))
            factor = {g: column[g][q] * scale for g in later}
            left_row = over_rows(left[k], q) * scale
            right_row = over_rows(right[k], q) * scale
            below = jnp.where(row > q, factor[k], 0.0)
            left[k] = jnp.where(row == q, left_row, left[k] - below * left_row)
            right[k] = jnp.where(row == q, right_row, right[k] - below * right_row)
            for other in range(q + 1, SUBLANES):
                weight = over_rows(factor[k], other)
                for g in later:
                    column[g][other] = column[g][other] - factor[g] * weight
            for g in range(k + 1, groups):
                left[g] = left[g] - factor[g] * left_row
                right[g] = right[g] - factor[g] * right_row
    return jnp.concatenate(right, axis=0)


def orthonormal_kernel(scale, block_ref, gram_ref, filtered_ref, out_ref, inverse):
    size = gram_ref.shape[0]
    count = size // LANES
    at = [slice(i * LANES, (i + 1) * LANES) for i in range(count)]
    lower = {}
    inverses = {}
    for i in range(count):
        diagonal = gram_ref[at[i], at[i]]
        for j in range(i):
            diagonal = diagonal - exact(lower[i, j], lower[i, j], ((1,), (1,)))
        inverses[i, i] = inverse_factor(diagonal)
        for k in range(i + 1, count):
            entry = gram_ref[at[k], at[i]]
            for j in range(i):
                entry = entry - exact(lower[k, j], lower[i, j], ((1,), (1,)))
            lower[k, i] = exact(entry, inverses[i, i], ((1,), (1,)))
    inverse[...] = jnp.zeros_like(inverse)
    for i in range(count):
        for j in range(i):
            entry = exact(lower[i, j], inverses[j, j], ((1,), (0,)))
            for m in range(j + 1, i):
                entry = entry + exact(lower[i, m], inverses[m, j], ((1,), (0,)))
            inverses[i, j] = -exact(inverses[i, i], entry, ((1,), (0,)))
            inverse[at[i], at[j]] = inverses[i, j] * scale
        inverse[at[i], at[i]] = inverses[i, i] * scale
    rows = out_ref.shape[0]
    mine = inverse[pl.ds(pl.multiple_of(block_ref[0] * rows, rows), rows), :]
    high = mine.astype(jnp.bfloat16)
    low = (mine - high.astype(jnp.float32)).astype(jnp.bfloat16)
    width = 512
    for first in range(0, out_ref.shape[1], width):
        part = filtered_ref[:, first : first + width]
        out_ref[:, first : first + width] = jnp.dot(
            high, part, preferred_element_type=jnp.float32
        ) + jnp.dot(low, part, preferred_element_type=jnp.float32)


def orthonormal(block, gram, filtered, rows, scale):
    size = gram.shape[0]
    return pl.pallas_call(
        functools.partial(orthonormal_kernel, scale),
        out_shape=jax.ShapeDtypeStruct((rows, filtered.shape[1]), jnp.float32),
        in_specs=[
            pl.BlockSpec(memory_space=pltpu.SMEM),
            pl.BlockSpec(memory_space=pltpu.VMEM),
            pl.BlockSpec(memory_space=pltpu.VMEM),
        ],
        out_specs=pl.BlockSpec(memory_space=pltpu.VMEM),
        scratch_shapes=[pltpu.VMEM((size, size), jnp.float32)],
        compiler_params=pltpu.CompilerParams(vmem_limit_bytes=16 * 1024 * 1024),
    )(block, gram, filtered)


def swap_pairs(count, first):
    pairs = []
    for low in range(first, count - 1, 2):
        pairs += [(low, low + 1), (low + 1, low)]
    return pairs


def sum_over(values, axis):
    count = lax.axis_size(axis)
    if count & (count - 1):
        return lax.psum(values.astype(jnp.bfloat16), axis).astype(jnp.float32)
    step = 1
    while step < count:
        sent = values.astype(jnp.bfloat16)
        got = lax.ppermute(sent, axis, [(i, i ^ step) for i in range(count)])
        values = sent.astype(jnp.float32) + got.astype(jnp.float32)
        step *= 2
    return values


def per_device(orbitals, cell_matrices, connectivity, face_lower, face_upper):
    own_count = orbitals.shape[1]
    face = face_lower.shape[0]
    ext_count = own_count + 2 * face
    slabs = lax.axis_size("slab")
    slab = lax.axis_index("slab")
    even = slab % 2 == 0

    has_lower = slab > 0
    has_upper = slab < slabs - 1
    has_a = jnp.where(even, has_upper, has_lower)
    has_b = jnp.where(even, has_lower, has_upper)
    ghost_lower = jnp.arange(face, dtype=jnp.int32)
    ghost_upper = ghost_lower + (face + own_count)
    face_a = jnp.where(even, face_upper, face_lower)
    face_b = jnp.where(even, face_lower, face_upper)
    ghost_a = jnp.where(even, ghost_upper, ghost_lower)
    ghost_b = jnp.where(even, ghost_lower, ghost_upper)

    lower_at = jnp.where(even, own_count + face, own_count)
    upper_at = jnp.where(even, own_count, own_count + face)
    places = jnp.where(
        connectivity < face,
        connectivity + lower_at,
        jnp.where(
            connectivity < face + own_count,
            connectivity - face,
            connectivity - (face + own_count) + upper_at,
        ),
    ).reshape(-1) * PITCH
    columns_b = jnp.concatenate([ghost_b, face_b + face])
    columns_a = jnp.concatenate([ghost_a, face_a + face])
    own_columns = jnp.arange(own_count, dtype=jnp.int32) + face
    nodes = jnp.broadcast_to(connectivity[:, :, None], connectivity.shape + (LANES,))

    face_nodes = jnp.concatenate([face_a, face_b])
    face_table = (
        face_nodes[:, None] == lax.broadcasted_iota(jnp.int32, (2 * face, own_count), 1)
    ).astype(jnp.bfloat16)

    pairs_a = swap_pairs(slabs, 0)
    pairs_b = swap_pairs(slabs, 1)

    def times(left, right):
        return jnp.dot(left, right, preferred_element_type=jnp.float32)

    rounded = orbitals.astype(jnp.bfloat16)
    faces = lax.dot_general(
        rounded, face_table, (((1,), (1,)), ((), ())), preferred_element_type=jnp.float32
    ).astype(jnp.bfloat16)
    ghosts_b = lax.ppermute(faces[:, face:], "slab", pairs_b)
    ghosts_a = lax.ppermute(faces[:, :face], "slab", pairs_a)
    mine = jnp.concatenate([rounded, ghosts_a, ghosts_b], axis=1)
    gathered = lax.all_gather(mine, "orb", axis=0, tiled=True)
    matrix_b, matrix_a, own_matrix = assemble(
        places,
        jnp.concatenate([columns_b, columns_a, own_columns]),
        nodes,
        cell_matrices,
        ext_count,
        mine,
    )

    there = jnp.stack([has_a, has_b]).astype(jnp.int32)
    field, matrix_b, matrix_a = hold(gathered, matrix_b, matrix_a)
    ghosts = [field[:, own_count:]]
    before = ()
    for step in range(DEGREE):
        last = step == DEGREE - 1
        part_b = times(field, matrix_b[:, :face] if last else matrix_b)
        sent_b = part_b.astype(jnp.bfloat16)
        got_b = lax.ppermute(sent_b, "slab", pairs_b)
        part_a = times(field, matrix_a[:, :face] if last else matrix_a)
        sent_a = part_a.astype(jnp.bfloat16)
        got_a = lax.ppermute(sent_a, "slab", pairs_a)
        own = own_part(step, field, own_matrix, before, (sent_a, sent_b))
        if step == 0:
            before = (field,)
        else:
            before = arrivals
        arrivals = (own, got_a, got_b, face_table)
        if last:
            (filtered,) = combine(step, there, own, got_a, got_b, face_table, ())
        else:
            operands = (part_a, part_b) + ((ghosts[-2],) if step else ())
            field, new_ghosts = combine(step, there, own, got_a, got_b, face_table, operands)
            ghosts.append(new_ghosts)

    gram = lax.dot_general(
        filtered, filtered, (((1,), (1,)), ((), ())), preferred_element_type=jnp.float32
    )
    total = sum_over(gram, "slab")
    block = lax.axis_index("orb").astype(jnp.int32).reshape(1)
    return orthonormal(block, total, filtered, orbitals.shape[0], math.sqrt(own_count * slabs))


def solution(mesh):
    in_specs = (P("orb", "slab"), P("slab", None, None), P("slab", None), P("slab"), P("slab"))
    out_specs = P("orb", "slab")
    return jax.shard_map(
        per_device, mesh=mesh, in_specs=in_specs, out_specs=out_specs, check_vma=False
    )
```

```python
import functools
import math

import jax
import jax.numpy as jnp
from jax import lax
from jax.experimental import pallas as pl
from jax.experimental.pallas import tpu as pltpu
from jax.sharding import PartitionSpec as P

DEGREE = 4
LANES = 128
SUBLANES = 8
CHUNK = LANES * SUBLANES
PITCH = SUBLANES + 1
TILE = 256


def assemble_kernel(
    places_ref, column_ref, nodes_ref, cell_ref, after_ref, shared_b_ref, shared_a_ref, own_ref,
    total, even_terms, odd_terms, rounded, sent,
):
    chunk = pl.program_id(0)
    chunks = pl.num_programs(0)
    cell = pl.program_id(1)
    cells = pl.num_programs(1)
    cell_nodes = cell_ref.shape[1]
    ext_count = own_ref.shape[1]
    share = rounded.shape[1] // (places_ref.shape[0] // (2 * cell_nodes))
    parts = CHUNK // TILE
    part_rows = cell_nodes // parts
    group = 32
    table = chunk % 2 * (cells * cell_nodes)

    def spread_part(part):
        columns = column_ref[:, part * TILE : (part + 1) * TILE]
        picker = jnp.concatenate(
            [
                (nodes_ref[0] == columns[:, half * LANES : (half + 1) * LANES])
                .astype(jnp.float32)
                .astype(jnp.bfloat16)
                for half in range(2)
            ],
            axis=1,
        )
        return jnp.dot(cell_ref[0], picker, preferred_element_type=jnp.float32)

    def keep_part(part, spread, terms):
        for first in range(0, cell_nodes, SUBLANES):
            for half in range(2):
                terms[pl.ds(first * PITCH + 2 * part + half, SUBLANES, stride=PITCH), :] = spread[
                    first : first + SUBLANES, half * LANES : (half + 1) * LANES
                ]

    def add_part(part, of_cell, terms):
        first = part * part_rows
        for start in range(0, part_rows, group):
            places = [
                places_ref[table + of_cell * cell_nodes + first + start + k] for k in range(group)
            ]
            sums = [
                total[pl.ds(places[k], SUBLANES), :]
                + terms[pl.ds((first + start + k) * PITCH, SUBLANES), :]
                for k in range(group)
            ]
            for k in range(group):
                total[pl.ds(places[k], SUBLANES), :] = sums[k]

    def round_rows(first, which, zero):
        base = (which * ext_count + first) * PITCH
        for block in range(SUBLANES):
            upper = total[pl.ds(base + block, SUBLANES, stride=PITCH), :]
            lower = total[pl.ds(base + SUBLANES * PITCH + block, SUBLANES, stride=PITCH), :]
            rounded[
                block // 2, pl.ds(first, 16), block % 2 * LANES : (block % 2 + 1) * LANES
            ] = jnp.concatenate([upper, lower], axis=0).astype(jnp.bfloat16)
        if zero:
            total[pl.ds(pl.multiple_of(base, SUBLANES), 16 * PITCH), :] = jnp.zeros(
                (16 * PITCH, LANES), jnp.float32
            )

    def round_part(part):
        pieces = share // 16
        for piece in range(part * pieces // parts, (part + 1) * pieces // parts):
            round_rows(pl.multiple_of(cell * share + piece * 16, 16), 1 - chunk % 2, True)

    def sends(index, of_chunk, to_own):
        rows = pl.ds(pl.multiple_of(index * share, 16), share)
        copies = []
        for part in range(parts):
            if to_own:
                target = own_ref.at[(of_chunk - 1) * parts + part, rows]
            else:
                half = (shared_b_ref, shared_a_ref)[part // 2]
                target = half.at[rows, part % 2 * TILE : (part % 2 + 1) * TILE]
            copies.append(
                pltpu.make_async_copy(rounded.at[part, rows], target, sent.at[index, part])
            )
        return copies

    def wait_share(index):
        for copy in sends(index, 1, True):
            copy.wait()

    @pl.when(chunk > 1)
    def _():
        wait_share(cell)

    @pl.when((cell == 0) & (chunk == 0))
    def _():
        def zero(step, carry):
            total[pl.ds(pl.multiple_of(step * 64, 64), 64), :] = jnp.zeros((64, LANES), jnp.float32)
            return carry

        lax.fori_loop(0, ext_count * PITCH // 64, zero, 0, unroll=4)

    @pl.when(cell == 0)
    def _():
        for part in range(parts):
            keep_part(part, spread_part(part), even_terms)
            round_part(part)

    for parity, (before, now) in enumerate(((odd_terms, even_terms), (even_terms, odd_terms))):

        @pl.when((cell > 0) & (cell % 2 == parity))
        def _():
            for part in range(parts):
                keep_part(part, spread_part(part), now)
                add_part(part, cell - 1, before)
                round_part(part)

        @pl.when((cell == cells - 1) & (cell % 2 == parity))
        def _():
            def body(part, carry):
                add_part(part, cell, now)
                return carry

            lax.fori_loop(0, parts, body, 0)

    @pl.when(chunk == 1)
    def _():
        for copy in sends(cell, 0, False):
            copy.start()

    @pl.when(chunk > 1)
    def _():
        for copy in sends(cell, chunk - 1, True):
            copy.start()

    @pl.when((cell == cells - 1) & (chunk == chunks - 1))
    def _():
        def last_share(index, carry):
            wait_share(index)

            def last_rows(piece, inner):
                round_rows(pl.multiple_of(index * share + piece * 16, 16), chunk % 2, False)
                return inner

            lax.fori_loop(0, share // 16, last_rows, 0, unroll=4)
            for copy in sends(index, chunk, True):
                copy.start()
            return carry

        lax.fori_loop(0, cells, last_share, 0)

        def settle(index, carry):
            wait_share(index)
            return carry

        lax.fori_loop(0, cells, settle, 0)


def assemble(places, columns, nodes, cell_matrices, ext_count, after):
    cells, cell_nodes, _ = cell_matrices.shape
    count = columns.shape[0]
    chunks = count // CHUNK
    assert chunks > 1 and ext_count % (16 * cells) == 0
    half = jax.ShapeDtypeStruct((ext_count, CHUNK // 2), jnp.bfloat16)
    return pl.pallas_call(
        assemble_kernel,
        out_shape=(
            half,
            half,
            jax.ShapeDtypeStruct(((count - CHUNK) // TILE, ext_count, TILE), jnp.bfloat16),
        ),
        grid_spec=pltpu.PrefetchScalarGridSpec(
            num_scalar_prefetch=1,
            grid=(chunks, cells),
            in_specs=[
                pl.BlockSpec((1, CHUNK), lambda q, c, places: (0, q)),
                pl.BlockSpec((1, cell_nodes, LANES), lambda q, c, places: (c, 0, 0)),
                pl.BlockSpec((1, cell_nodes, cell_nodes), lambda q, c, places: (c, 0, 0)),
                pl.BlockSpec(memory_space=pl.ANY),
            ],
            out_specs=(pl.BlockSpec(memory_space=pl.ANY),) * 3,
            scratch_shapes=[
                pltpu.VMEM(((2 * ext_count + SUBLANES) * PITCH, LANES), jnp.float32),
                pltpu.VMEM(((cell_nodes + SUBLANES) * PITCH, LANES), jnp.float32),
                pltpu.VMEM(((cell_nodes + SUBLANES) * PITCH, LANES), jnp.float32),
                pltpu.VMEM((CHUNK // TILE, ext_count, TILE), jnp.bfloat16),
                pltpu.SemaphoreType.DMA((cells, CHUNK // TILE)),
            ],
        ),
        compiler_params=pltpu.CompilerParams(vmem_limit_bytes=57 * 1024 * 1024),
        cost_estimate=pl.CostEstimate(
            flops=16 * cells * cell_nodes * cell_nodes * count,
            bytes_accessed=chunks * cells * cell_nodes * cell_nodes * 2 + ext_count * count * 2,
            transcendentals=0,
        ),
    )(
        jnp.concatenate([places, places + ext_count * PITCH]),
        columns[None, :],
        nodes,
        cell_matrices,
        after,
    )


def hold_kernel(*refs):
    count = len(refs) // 2
    done = refs[-1]
    copies = [pltpu.make_async_copy(refs[i], refs[count + i], done.at[i]) for i in range(count)]
    for copy in copies:
        copy.start()
    for copy in copies:
        copy.wait()


def hold(*arrays):
    return pl.pallas_call(
        hold_kernel,
        out_shape=tuple(jax.ShapeDtypeStruct(x.shape, x.dtype) for x in arrays),
        in_specs=[pl.BlockSpec(memory_space=pl.ANY)] * len(arrays),
        out_specs=(pl.BlockSpec(memory_space=pltpu.VMEM),) * len(arrays),
        scratch_shapes=[pltpu.SemaphoreType.DMA((len(arrays),))],
        compiler_params=pltpu.CompilerParams(vmem_limit_bytes=16 * 1024 * 1024),
    )(*arrays)


def arrived(got_a_ref, got_b_ref, table_ref, at):
    incoming = jnp.concatenate(
        [ref[:, : table_ref.shape[0] // 2] for ref in (got_a_ref, got_b_ref)], axis=1
    )
    return jnp.dot(incoming, table_ref[:, at], preferred_element_type=jnp.float32)


def own_kernel(step, extended_ref, matrix_ref, *refs):
    out_ref = refs[-1]

    def body(tile, carry):
        at = pl.ds(pl.multiple_of(tile * TILE, TILE), TILE)
        product = jnp.dot(extended_ref[...], matrix_ref[tile], preferred_element_type=jnp.float32)
        if step == 1:
            product = 2.0 * product - refs[0][:, at].astype(jnp.float32)
        if step > 1:
            factor = 1.0 if step == 2 else 2.0
            product = 2.0 * product - (refs[0][:, at] + factor * arrived(*refs[1:4], at))
        out_ref[:, at] = product
        return carry

    lax.fori_loop(0, matrix_ref.shape[0], body, 0, unroll=8)


def own_part(step, extended, matrix, before, after):
    rows, depth = extended.shape
    tiles, _, width = matrix.shape
    columns = tiles * width
    whole = pl.BlockSpec(memory_space=pltpu.VMEM)
    operands = (extended, matrix) + before
    return pl.pallas_call(
        functools.partial(own_kernel, step),
        out_shape=jax.ShapeDtypeStruct((rows, columns), jnp.float32),
        in_specs=[whole] * len(operands) + [pl.BlockSpec(memory_space=pl.ANY)] * len(after),
        out_specs=whole,
        compiler_params=pltpu.CompilerParams(vmem_limit_bytes=16 * 1024 * 1024),
        cost_estimate=pl.CostEstimate(
            flops=8 * rows * depth * columns,
            bytes_accessed=2 * depth * columns + 4 * rows * columns,
            transcendentals=0,
        ),
    )(*operands, *after)


def combine_kernel(step, there_ref, own_ref, got_a_ref, got_b_ref, table_ref, *refs):
    factor = 1.0 if step == 0 else 2.0
    columns, face = own_ref.shape[1], table_ref.shape[0] // 2
    ghosts_ref = refs[-1]
    field_ref = refs[-2] if len(refs) > 1 else refs[-1]
    for first in range(0, columns, TILE):
        at = slice(first, first + TILE)
        field_ref[:, at] = (
            own_ref[:, at] + factor * arrived(got_a_ref, got_b_ref, table_ref, at)
        ).astype(jnp.bfloat16)
    if len(refs) == 1:
        return
    for side, got_ref in enumerate((got_a_ref, got_b_ref)):
        at = slice(side * face, (side + 1) * face)
        value = factor * (refs[side][:, :face] + got_ref[:, face:].astype(jnp.float32))
        if step > 0:
            value = value - refs[2][:, at].astype(jnp.float32)
        value = jnp.where(there_ref[side] != 0, value, 0.0)
        ghosts_ref[:, at] = value
        field_ref[:, columns + side * face : columns + (side + 1) * face] = value.astype(jnp.bfloat16)


def combine(step, there, own, got_a, got_b, table, ghost_operands):
    rows, columns = own.shape
    whole = pl.BlockSpec(memory_space=pltpu.VMEM)
    face = table.shape[0] // 2
    if ghost_operands:
        out_shape = (
            jax.ShapeDtypeStruct((rows, columns + 2 * face), jnp.bfloat16),
            jax.ShapeDtypeStruct((rows, 2 * face), jnp.float32),
        )
    else:
        out_shape = (jax.ShapeDtypeStruct((rows, columns), jnp.bfloat16),)
    return pl.pallas_call(
        functools.partial(combine_kernel, step),
        out_shape=out_shape,
        in_specs=[pl.BlockSpec(memory_space=pltpu.SMEM)] + [whole] * (4 + len(ghost_operands)),
        out_specs=(whole,) * len(out_shape),
        compiler_params=pltpu.CompilerParams(vmem_limit_bytes=16 * 1024 * 1024),
    )(there, own, got_a, got_b, table, *ghost_operands)


def exact(left, right, contract):
    return lax.dot_general(
        left,
        right,
        (contract, ((), ())),
        precision=lax.Precision.HIGHEST,
        preferred_element_type=jnp.float32,
    )


def inverse_factor(block):
    size = block.shape[0]
    groups = size // SUBLANES
    row = lax.broadcasted_iota(jnp.int32, (SUBLANES, LANES), 0)
    lane = lax.broadcasted_iota(jnp.int32, (SUBLANES, LANES), 1)
    left = [block[g * SUBLANES : (g + 1) * SUBLANES, :] for g in range(groups)]
    right = [(lane == row + g * SUBLANES).astype(jnp.float32) for g in range(groups)]

    def over_rows(values, index):
        return jnp.broadcast_to(values[index : index + 1, :], (SUBLANES, LANES))

    for k in range(groups):
        later = range(k, groups)
        column = {
            g: [
                jnp.broadcast_to(
                    left[g][:, k * SUBLANES + q : k * SUBLANES + q + 1], (SUBLANES, LANES)
                )
                for q in range(SUBLANES)
            ]
            for g in later
        }
        for q in range(SUBLANES):
            scale = lax.rsqrt(over_rows(column[k][q], q))
            factor = {g: column[g][q] * scale for g in later}
            left_row = over_rows(left[k], q) * scale
            right_row = over_rows(right[k], q) * scale
            below = jnp.where(row > q, factor[k], 0.0)
            left[k] = jnp.where(row == q, left_row, left[k] - below * left_row)
            right[k] = jnp.where(row == q, right_row, right[k] - below * right_row)
            for other in range(q + 1, SUBLANES):
                weight = over_rows(factor[k], other)
                for g in later:
                    column[g][other] = column[g][other] - factor[g] * weight
            for g in range(k + 1, groups):
                left[g] = left[g] - factor[g] * left_row
                right[g] = right[g] - factor[g] * right_row
    return jnp.concatenate(right, axis=0)


def orthonormal_kernel(scale, block_ref, gram_ref, filtered_ref, out_ref, inverse):
    size = gram_ref.shape[0]
    count = size // LANES
    at = [slice(i * LANES, (i + 1) * LANES) for i in range(count)]
    lower = {}
    inverses = {}
    for i in range(count):
        diagonal = gram_ref[at[i], at[i]]
        for j in range(i):
            diagonal = diagonal - exact(lower[i, j], lower[i, j], ((1,), (1,)))
        inverses[i, i] = inverse_factor(diagonal)
        for k in range(i + 1, count):
            entry = gram_ref[at[k], at[i]]
            for j in range(i):
                entry = entry - exact(lower[k, j], lower[i, j], ((1,), (1,)))
            lower[k, i] = exact(entry, inverses[i, i], ((1,), (1,)))
    inverse[...] = jnp.zeros_like(inverse)
    for i in range(count):
        for j in range(i):
            entry = exact(lower[i, j], inverses[j, j], ((1,), (0,)))
            for m in range(j + 1, i):
                entry = entry + exact(lower[i, m], inverses[m, j], ((1,), (0,)))
            inverses[i, j] = -exact(inverses[i, i], entry, ((1,), (0,)))
            inverse[at[i], at[j]] = inverses[i, j] * scale
        inverse[at[i], at[i]] = inverses[i, i] * scale
    rows = out_ref.shape[0]
    mine = inverse[pl.ds(pl.multiple_of(block_ref[0] * rows, rows), rows), :]
    high = mine.astype(jnp.bfloat16)
    low = (mine - high.astype(jnp.float32)).astype(jnp.bfloat16)
    width = 512
    for first in range(0, out_ref.shape[1], width):
        part = filtered_ref[:, first : first + width]
        out_ref[:, first : first + width] = jnp.dot(
            high, part, preferred_element_type=jnp.float32
        ) + jnp.dot(low, part, preferred_element_type=jnp.float32)


def orthonormal(block, gram, filtered, rows, scale):
    size = gram.shape[0]
    return pl.pallas_call(
        functools.partial(orthonormal_kernel, scale),
        out_shape=jax.ShapeDtypeStruct((rows, filtered.shape[1]), jnp.float32),
        in_specs=[
            pl.BlockSpec(memory_space=pltpu.SMEM),
            pl.BlockSpec(memory_space=pltpu.VMEM),
            pl.BlockSpec(memory_space=pltpu.VMEM),
        ],
        out_specs=pl.BlockSpec(memory_space=pltpu.VMEM),
        scratch_shapes=[pltpu.VMEM((size, size), jnp.float32)],
        compiler_params=pltpu.CompilerParams(vmem_limit_bytes=16 * 1024 * 1024),
    )(block, gram, filtered)


def swap_pairs(count, first):
    pairs = []
    for low in range(first, count - 1, 2):
        pairs += [(low, low + 1), (low + 1, low)]
    return pairs


def sum_over(values, axis):
    count = lax.axis_size(axis)
    if count & (count - 1):
        return lax.psum(values.astype(jnp.bfloat16), axis).astype(jnp.float32)
    step = 1
    while step < count:
        sent = values.astype(jnp.bfloat16)
        got = lax.ppermute(sent, axis, [(i, i ^ step) for i in range(count)])
        values = sent.astype(jnp.float32) + got.astype(jnp.float32)
        step *= 2
    return values


def per_device(orbitals, cell_matrices, connectivity, face_lower, face_upper):
    own_count = orbitals.shape[1]
    face = face_lower.shape[0]
    ext_count = own_count + 2 * face
    slabs = lax.axis_size("slab")
    slab = lax.axis_index("slab")
    even = slab % 2 == 0

    has_lower = slab > 0
    has_upper = slab < slabs - 1
    has_a = jnp.where(even, has_upper, has_lower)
    has_b = jnp.where(even, has_lower, has_upper)
    ghost_lower = jnp.arange(face, dtype=jnp.int32)
    ghost_upper = ghost_lower + (face + own_count)
    face_a = jnp.where(even, face_upper, face_lower)
    face_b = jnp.where(even, face_lower, face_upper)
    ghost_a = jnp.where(even, ghost_upper, ghost_lower)
    ghost_b = jnp.where(even, ghost_lower, ghost_upper)

    lower_at = jnp.where(even, own_count + face, own_count)
    upper_at = jnp.where(even, own_count, own_count + face)
    places = jnp.where(
        connectivity < face,
        connectivity + lower_at,
        jnp.where(
            connectivity < face + own_count,
            connectivity - face,
            connectivity - (face + own_count) + upper_at,
        ),
    ).reshape(-1) * PITCH
    columns_b = jnp.concatenate([ghost_b, face_b + face])
    columns_a = jnp.concatenate([ghost_a, face_a + face])
    own_columns = jnp.arange(own_count, dtype=jnp.int32) + face
    nodes = jnp.broadcast_to(connectivity[:, :, None], connectivity.shape + (LANES,))

    face_nodes = jnp.concatenate([face_a, face_b])
    face_table = (
        face_nodes[:, None] == lax.broadcasted_iota(jnp.int32, (2 * face, own_count), 1)
    ).astype(jnp.bfloat16)

    pairs_a = swap_pairs(slabs, 0)
    pairs_b = swap_pairs(slabs, 1)

    def times(left, right):
        return jnp.dot(left, right, preferred_element_type=jnp.float32)

    rounded = orbitals.astype(jnp.bfloat16)
    faces = lax.dot_general(
        rounded, face_table, (((1,), (1,)), ((), ())), preferred_element_type=jnp.float32
    ).astype(jnp.bfloat16)
    ghosts_b = lax.ppermute(faces[:, face:], "slab", pairs_b)
    ghosts_a = lax.ppermute(faces[:, :face], "slab", pairs_a)
    mine = jnp.concatenate([rounded, ghosts_a, ghosts_b], axis=1)
    gathered = lax.all_gather(mine, "orb", axis=0, tiled=True)
    matrix_b, matrix_a, own_matrix = assemble(
        places,
        jnp.concatenate([columns_b, columns_a, own_columns]),
        nodes,
        cell_matrices,
        ext_count,
        mine,
    )

    there = jnp.stack([has_a, has_b]).astype(jnp.int32)
    field, matrix_b, matrix_a = hold(gathered, matrix_b, matrix_a)
    ghosts = [field[:, own_count:]]
    before = ()
    for step in range(DEGREE):
        last = step == DEGREE - 1
        part_b = times(field, matrix_b[:, :face] if last else matrix_b)
        sent_b = part_b.astype(jnp.bfloat16)
        got_b = lax.ppermute(sent_b, "slab", pairs_b)
        part_a = times(field, matrix_a[:, :face] if last else matrix_a)
        sent_a = part_a.astype(jnp.bfloat16)
        got_a = lax.ppermute(sent_a, "slab", pairs_a)
        own = own_part(step, field, own_matrix, before, (sent_a, sent_b))
        if step == 0:
            before = (field,)
        else:
            before = arrivals
        arrivals = (own, got_a, got_b, face_table)
        if last:
            (filtered,) = combine(step, there, own, got_a, got_b, face_table, ())
        else:
            operands = (part_a, part_b) + ((ghosts[-2],) if step else ())
            field, new_ghosts = combine(step, there, own, got_a, got_b, face_table, operands)
            ghosts.append(new_ghosts)

    gram = lax.dot_general(
        filtered, filtered, (((1,), (1,)), ((), ())), preferred_element_type=jnp.float32
    )
    total = sum_over(gram, "slab")
    block = lax.axis_index("orb").astype(jnp.int32).reshape(1)
    return orthonormal(block, total, filtered, orbitals.shape[0], math.sqrt(own_count * slabs))


def solution(mesh):
    in_specs = (P("orb", "slab"), P("slab", None, None), P("slab", None), P("slab"), P("slab"))
    out_specs = P("orb", "slab")
    return jax.shard_map(
        per_device, mesh=mesh, in_specs=in_specs, out_specs=out_specs, check_vma=False
    )
```
